32 devices in a mesh: ctx: 4 (over z), head: 8 (over y, x, core).
Axes of the slice: x: 2, y: 2, z: 4, core: 2. Of those that a mesh axis runs over, the one named last changes fastest.
Arguments:
- queries: bfloat16 [4096, 4096], P(('ctx', 'head')), may hold values from -12 to 12
- keys_in: bfloat16 [4096, 4096], P(('ctx', 'head')), may hold values from -5 to 5
- values_in: bfloat16 [4096, 4096], P(('ctx', 'head')), may hold values from -6 to 6
- out_grad: bfloat16 [4096, 4096], P(('ctx', 'head')), may hold values from -6 to 6
- rand_owner: int32 [32, 3], replicated, may hold values from 0 to 3, all different within a row; in each aligned block of 8 rows (0 to 7, 8 to 15, ...) at most 8 rows name the same one
- rand_local: int32 [32, 3], replicated, may hold values from 0 to 7
Outputs:
- grad_queries: bfloat16 [4096, 4096], P(('ctx', 'head'))
- grad_keys: bfloat16 [4096, 4096], P(('ctx', 'head'))
- grad_values: bfloat16 [4096, 4096], P(('ctx', 'head'))
The draws below stay inside these ranges and needn't reach their ends.
Inputs may be any that keep to these rules, and one draw needn't show every extreme that they name: `rand_owner`: each row names 3 different ranges. Among the 8 rows of one aligned block of rows, at most 8 name the same range.
All inputs are finite; a program needn't handle non-finite values.
Results may differ from the reference program's by a relative error of at most 0.035.
Values may be sent and summed in bfloat16 or wider, within the bound.
A program may use at most 192 MiB of HBM per device.

```python
import math
import jax
import jax.numpy as jnp
import numpy as np
from jax import lax

NUM_HEADS = 32
HEAD_DIM = 128
BLOCK_LEN = 128
GLOBALS = 2
RANDOMS = 3
SEQ_LEN = 4096
NUM_BLOCKS = 32
RANGE_BLOCKS = 8
CAPACITY = 8
N_CTX = 4


def draw_queries(key, part):
    drawn = jax.random.truncated_normal(jax.random.fold_in(key, 1), -4.0, 4.0, (SEQ_LEN, NUM_HEADS * HEAD_DIM), jnp.float32)
    row_scale = jnp.where(jnp.arange(SEQ_LEN) < GLOBALS * BLOCK_LEN, 3.0, 1.0).astype(jnp.float32)
    drawn = drawn * row_scale[:, None]
    return drawn.astype(jnp.bfloat16)


def draw_keys_in(key, part):
    drawn = jax.random.truncated_normal(jax.random.fold_in(key, 2), -4.0, 4.0, (SEQ_LEN, NUM_HEADS * HEAD_DIM), jnp.float32)
    return drawn.astype(jnp.bfloat16)


def plant(values, stream_key, smallest, high):
    longest = values.shape.index(max(values.shape))
    spots = []
    for shift in (0, 1):
        where = [jax.random.randint(jax.random.fold_in(stream_key, axis), (), 0, length) for axis, length in enumerate(values.shape)]
        where[longest] = (where[longest] + shift) % values.shape[longest]
        spots.append(tuple(where))
    return values.at[spots[0]].set(smallest).at[spots[1]].set(high)


def block_scale(stream_key, extent, split, least, top_value):
    gain, own = 1.0, jax.random.fold_in(stream_key, 6)
    for axis_at, shards_of in split:
        draws = jnp.exp(jax.random.uniform(jax.random.fold_in(own, axis_at), (shards_of,), jnp.float32, least / len(split), top_value / len(split)))
        gain = gain * jnp.repeat(draws, extent[axis_at] // shards_of).reshape([-1 if axis == axis_at else 1 for axis in range(len(extent))])
    return gain


def shared_out(rng, own, number, rows, amount, top, bound, lean):
    order = jax.random.permutation(rng, amount)
    heavy_load, ordinary = portions_of(amount, rows * top, bound, lean, True), portions_of(amount, rows * top, bound, lean, False)
    places = jnp.arange(amount)

    def named(lengths, turn):
        used = int((lengths > 0).sum())
        fixed = max(1, used // 4)
        moved = fixed + (places - fixed + turn * (used - fixed)) % max(1, amount - fixed)
        return jnp.zeros((amount,), jnp.int32).at[order[jnp.where(places < fixed, places, moved)]].set(jnp.asarray(lengths, jnp.int32))

    lengths = jnp.where(number % 4 == 0, named(heavy_load, number // 4), named(ordinary, number - number // 4 - 1))
    mixed = jax.random.permutation(jax.random.fold_in(own, 3), amount)
    source_of, sink = mixed[0:amount // 2 * 2:2], mixed[1:amount // 2 * 2:2]
    slack = jnp.minimum(lengths[source_of] - 1, bound - lengths[sink]) // 2
    slack = jnp.where((source_of == order[0]) | (sink == order[0]) | (lengths[sink] == 0), 0, jnp.maximum(slack, 0))
    moved = jax.random.randint(jax.random.fold_in(own, 4), (amount // 2,), 0, 1 << 20) % (slack + 1)
    lengths = lengths.at[source_of].add(-moved).at[sink].add(moved)
    members = jnp.searchsorted(jnp.cumsum(lengths), jnp.arange(rows * top), side="right").astype(jnp.int32)
    table = members.reshape(top, rows).T
    table = table[jax.random.permutation(jax.random.fold_in(own, 1), rows)]
    turn = jax.random.randint(jax.random.fold_in(own, 2), (rows, 1), 0, top)
    return jnp.take_along_axis(table, (jnp.arange(top)[None, :] + turn) % top, axis=1)


def portions_of(number_of, total, most, skew, full):
    weights = [(1 << 20) // math.isqrt(grade ** skew) + 1 for grade in range(1, number_of + 1)]
    largest = most if full else min(most, max(-(-total // number_of), total * weights[0] // sum(weights)))
    least = 1 if total - largest >= number_of - 1 else 0
    given, spare = [largest] + [least] * (number_of - 1), total - largest - least * (number_of - 1)
    while spare > 0:
        candidates = [i for i in range(1, number_of) if given[i] < largest] or [i for i in range(1, number_of) if given[i] < most]
        mass, budget = sum([weights[i] for i in candidates]), spare
        for i in candidates:
            addition = min(most - given[i], max(1, budget * weights[i] // mass), spare)
            given[i] = given[i] + addition
            spare = spare - addition
    return np.array(given)


def centred(rng, extent, spread, bound, shards=(), kind=jnp.bfloat16):
    values = jax.random.normal(rng, extent, jnp.float32) * spread
    if len(shards) > 0:
        values = block_scale(rng, extent, shards, -0.22, 0.18) * values
    return jnp.clip(values, min=-bound, max=bound).astype(kind)


def setup_inputs(seed: int = 0) -> dict:
    key_list = jax.random.split(jax.random.key(seed), 7)
    queries = draw_queries(jax.random.fold_in(key_list[6], 71), 0)
    keys_in = draw_keys_in(jax.random.fold_in(key_list[6], 71), 0)
    values_in = centred(key_list[2], (SEQ_LEN, NUM_HEADS * HEAD_DIM), 1.0, 6.0, ((0, 32),))
    out_grad = centred(key_list[3], (SEQ_LEN, NUM_HEADS * HEAD_DIM), 1.0, 6.0, ((0, 32),))
    rand_owner_keys = jax.random.split(jax.random.fold_in(key_list[4], 1), NUM_BLOCKS // RANGE_BLOCKS)
    rand_owner_turns = jax.random.permutation(jax.random.fold_in(key_list[4], 3), NUM_BLOCKS // RANGE_BLOCKS)
    rand_owner = jax.vmap(lambda own, number: shared_out(jax.random.fold_in(key_list[4], 2), own, number, RANGE_BLOCKS, N_CTX, RANDOMS, CAPACITY, 2))(rand_owner_keys, rand_owner_turns).reshape((NUM_BLOCKS, RANDOMS))
    rand_local = plant(jax.random.randint(key_list[5], (NUM_BLOCKS, RANDOMS), 0, RANGE_BLOCKS), jax.random.fold_in(key_list[5], 1), 0, RANGE_BLOCKS - 1).astype(jnp.int32)
    return {"queries": queries, "keys_in": keys_in, "values_in": values_in, "out_grad": out_grad, "rand_owner": rand_owner, "rand_local": rand_local}


NEG_BIG = -1e+30

def entry_blocks(rand_owner, rand_local, range_blocks, glob_count, total_blocks):
    block_ids = jnp.arange(total_blocks, dtype=jnp.int32)
    fixed_cols = [block_ids - 1, block_ids, block_ids + 1]
    fixed_cols = fixed_cols + [jnp.full((total_blocks,), glob_id, jnp.int32) for glob_id in range(glob_count)]
    listed = jnp.concatenate([jnp.stack(fixed_cols, axis=1), rand_owner * range_blocks + rand_local], axis=1)
    inside = (listed >= 0) & (listed < total_blocks)
    entry_count = listed.shape[1]
    equal_pair = (listed[:, :, None] == listed[:, None, :]) & inside[:, None, :]
    earlier = jnp.tril(jnp.ones((entry_count, entry_count), jnp.int32), -1) > 0
    repeated = jnp.any(equal_pair & earlier[None, :, :], axis=2)
    usable = inside & jnp.logical_not(repeated) & (block_ids >= glob_count)[:, None]
    return (jnp.clip(listed, 0, total_blocks - 1), usable)

def reference(queries, keys_in, values_in, out_grad, rand_owner, rand_local):
    score_scale = 1.0 / math.sqrt(HEAD_DIM)
    highest = lax.Precision.HIGHEST
    listed, usable = entry_blocks(rand_owner, rand_local, RANGE_BLOCKS, GLOBALS, NUM_BLOCKS)
    entry_count = listed.shape[1]
    block_shape = (NUM_BLOCKS, BLOCK_LEN, NUM_HEADS, HEAD_DIM)
    q_blocks = queries.reshape(block_shape)
    k_blocks = keys_in.reshape(block_shape)
    v_blocks = values_in.reshape(block_shape)
    g_blocks = out_grad.reshape(block_shape)
    tile_shape = (entry_count * BLOCK_LEN, NUM_HEADS, HEAD_DIM)

    def block_grads(block_id):
        q_tile = q_blocks[block_id].astype(jnp.float32)
        g_tile = g_blocks[block_id].astype(jnp.float32)
        key_ids = listed[block_id]
        k_tile = k_blocks[key_ids].astype(jnp.float32).reshape(tile_shape)
        v_tile = v_blocks[key_ids].astype(jnp.float32).reshape(tile_shape)
        key_mask = jnp.repeat(usable[block_id], BLOCK_LEN)[None, None, :]
        scores = jnp.einsum('qhd,khd->hqk', q_tile, k_tile, precision=highest) * score_scale
        scores = jnp.where(key_mask, scores, NEG_BIG)
        row_top = lax.optimization_barrier(jnp.max(scores, axis=2, keepdims=True))
        row_total = lax.optimization_barrier(jnp.sum(jnp.where(key_mask, jnp.exp(scores - row_top), 0.0), axis=2, keepdims=True))
        log_norm = row_top + jnp.log(jnp.where(row_total > 0, row_total, 1.0))
        prob_vals = jnp.where(key_mask, jnp.exp(scores - log_norm), 0.0)
        probs_bf = prob_vals.astype(jnp.bfloat16).astype(jnp.float32)
        attended = jnp.einsum('hqk,khd->qhd', probs_bf, v_tile, precision=highest)
        row_delta = lax.optimization_barrier(jnp.sum(g_tile * attended, axis=2))
        dprobs = jnp.einsum('qhd,khd->hqk', g_tile, v_tile, precision=highest)
        dscores = prob_vals * (dprobs - jnp.transpose(row_delta)[:, :, None])
        ds_bf = dscores.astype(jnp.bfloat16).astype(jnp.float32)
        dq_tile = (jnp.einsum('hqk,khd->qhd', ds_bf, k_tile, precision=highest) * score_scale).astype(jnp.bfloat16)
        dk_tile = jnp.einsum('hqk,qhd->khd', ds_bf, q_tile, precision=highest) * score_scale
        dv_tile = jnp.einsum('hqk,qhd->khd', probs_bf, g_tile, precision=highest)
        entry_shape = (entry_count, BLOCK_LEN, NUM_HEADS, HEAD_DIM)
        return (dq_tile, dk_tile.reshape(entry_shape), dv_tile.reshape(entry_shape))
    zero_acc = jnp.zeros(block_shape, jnp.float32)

    def range_step(totals, range_id):

        def block_step(acc_pair, offset):
            block_id = range_id * RANGE_BLOCKS + offset
            dq_tile, dk_tile, dv_tile = block_grads(block_id)
            key_ids = listed[block_id]
            return ((acc_pair[0].at[key_ids].add(dk_tile), acc_pair[1].at[key_ids].add(dv_tile)), dq_tile)
        acc_pair, dq_tiles = lax.scan(block_step, (zero_acc, zero_acc), jnp.arange(RANGE_BLOCKS, dtype=jnp.int32))
        rounded_k = lax.optimization_barrier(acc_pair[0].astype(jnp.bfloat16)).astype(jnp.float32)
        rounded_v = lax.optimization_barrier(acc_pair[1].astype(jnp.bfloat16)).astype(jnp.float32)
        return ((totals[0] + rounded_k, totals[1] + rounded_v), dq_tiles)
    totals, dq_ranges = lax.scan(range_step, (zero_acc, zero_acc), jnp.arange(N_CTX, dtype=jnp.int32))
    glob_rows = GLOBALS * BLOCK_LEN

    def head_grads(head_id):
        col_start = head_id * HEAD_DIM
        q_head = lax.dynamic_slice_in_dim(queries[:glob_rows], col_start, HEAD_DIM, 1)
        g_head = lax.dynamic_slice_in_dim(out_grad[:glob_rows], col_start, HEAD_DIM, 1)
        k_head = lax.dynamic_slice_in_dim(keys_in, col_start, HEAD_DIM, 1)
        v_head = lax.dynamic_slice_in_dim(values_in, col_start, HEAD_DIM, 1)
        scores = jnp.dot(q_head, k_head.T, preferred_element_type=jnp.float32) * score_scale
        row_top = lax.optimization_barrier(jnp.max(scores, axis=1, keepdims=True))
        log_norm = row_top + jnp.log(lax.optimization_barrier(jnp.sum(jnp.exp(scores - row_top), axis=1, keepdims=True)))
        prob_vals = jnp.exp(scores - log_norm)
        probs_bf = prob_vals.astype(jnp.bfloat16)
        attended = jnp.dot(probs_bf, v_head, preferred_element_type=jnp.float32)
        row_delta = lax.optimization_barrier(jnp.sum(g_head.astype(jnp.float32) * attended, axis=1, keepdims=True))
        dprobs = jnp.dot(g_head, v_head.T, preferred_element_type=jnp.float32)
        ds_bf = (prob_vals * (dprobs - row_delta)).astype(jnp.bfloat16)
        dq_head = jnp.dot(ds_bf, k_head, preferred_element_type=jnp.float32) * score_scale
        dk_head = jnp.dot(ds_bf.T, q_head, preferred_element_type=jnp.float32) * score_scale
        dv_head = jnp.dot(probs_bf.T, g_head, preferred_element_type=jnp.float32)
        return (dq_head, dk_head, dv_head)
    dq_glob, dk_glob, dv_glob = lax.map(head_grads, jnp.arange(NUM_HEADS, dtype=jnp.int32))
    feat_width = NUM_HEADS * HEAD_DIM

    def heads_last(tensor):
        return jnp.transpose(tensor, (1, 0, 2)).reshape(tensor.shape[1], feat_width)
    grad_keys = (totals[0].reshape(SEQ_LEN, feat_width) + heads_last(dk_glob)).astype(jnp.bfloat16)
    grad_values = (totals[1].reshape(SEQ_LEN, feat_width) + heads_last(dv_glob)).astype(jnp.bfloat16)
    dq_regular = dq_ranges.reshape(SEQ_LEN, feat_width)
    grad_queries = jnp.concatenate([heads_last(dq_glob).astype(jnp.bfloat16), dq_regular[glob_rows:]], axis=0)
    return (grad_queries, grad_keys, grad_values)
```

```python
import functools
import math

import jax
import jax.numpy as jnp
from jax import lax
from jax.experimental import pallas as pl
from jax.experimental.pallas import tpu as pltpu
from jax.sharding import PartitionSpec as P

MESH = pl.DeviceIdType.MESH

HEAD_DIM = 128
BLOCK_LEN = 128
GLOBALS = 2


NEG_BIG = -1e30


def broadcast(block, axis, holder):
    block = jnp.where(lax.axis_index(axis) == holder, block, jnp.zeros_like(block))
    return lax.psum(block, axis)


def entry_blocks(rand_owner, rand_local, range_blocks, glob_count, total_blocks):
    block_ids = jnp.arange(total_blocks, dtype=jnp.int32)
    fixed_cols = [block_ids - 1, block_ids, block_ids + 1]
    fixed_cols = fixed_cols + [
        jnp.full((total_blocks,), glob_id, jnp.int32) for glob_id in range(glob_count)
    ]
    listed = jnp.concatenate(
        [jnp.stack(fixed_cols, axis=1), rand_owner * range_blocks + rand_local], axis=1
    )
    inside = (listed >= 0) & (listed < total_blocks)
    entry_count = listed.shape[1]
    equal_pair = (listed[:, :, None] == listed[:, None, :]) & inside[:, None, :]
    earlier = jnp.tril(jnp.ones((entry_count, entry_count), jnp.int32), -1) > 0
    repeated = jnp.any(equal_pair & earlier[None, :, :], axis=2)
    usable = inside & jnp.logical_not(repeated) & (block_ids >= glob_count)[:, None]
    return (jnp.clip(listed, 0, total_blocks - 1), usable)


def head_major(rows_arr, block_len, head_dim):
    row_count, feat_width = rows_arr.shape
    shaped = rows_arr.reshape(row_count // block_len, block_len, feat_width // head_dim, head_dim)
    return jnp.transpose(shaped, (0, 2, 1, 3))


def token_major(blocks_arr):
    block_count, heads, block_len, head_dim = blocks_arr.shape
    return jnp.transpose(blocks_arr, (0, 2, 1, 3)).reshape(
        block_count * block_len, heads * head_dim
    )


def regular_part(q_blocks, g_blocks, key_pool, pool_index, usable, score_scale):
    range_blocks, local_heads, block_len, head_dim = q_blocks.shape
    entry_count = pool_index.shape[1]
    group_size = math.gcd(range_blocks, max(1, 512 // block_len))
    group_count = range_blocks // group_size

    def split_groups(tensor):
        return tensor.reshape((group_count, group_size) + tensor.shape[1:])

    def group_step(grad_acc, inputs):
        q_tile, g_tile, index_group, usable_group = inputs
        kv_tile = jnp.stack(
            [
                lax.dynamic_index_in_dim(key_pool, index_group[row, col], 0, keepdims=False)
                for row in range(group_size)
                for col in range(entry_count)
            ]
        ).reshape(index_group.shape + key_pool.shape[1:])
        k_tile = kv_tile[:, :, 0]
        v_tile = kv_tile[:, :, 1]
        key_mask = usable_group[:, None, None, :, None]
        scores = (
            jnp.einsum("ghqd,gehkd->ghqek", q_tile, k_tile, preferred_element_type=jnp.float32)
            * score_scale
        )
        scores = jnp.where(key_mask, scores, NEG_BIG)
        row_top = jnp.max(scores, axis=(3, 4), keepdims=True)
        row_total = jnp.sum(
            jnp.where(key_mask, jnp.exp(scores - row_top), 0.0), axis=(3, 4), keepdims=True
        )
        log_norm = row_top + jnp.log(jnp.where(row_total > 0, row_total, 1.0))
        prob_vals = jnp.where(key_mask, jnp.exp(scores - log_norm), 0.0)
        probs_bf = prob_vals.astype(jnp.bfloat16)
        attended = jnp.einsum(
            "ghqek,gehkd->ghqd", probs_bf, v_tile, preferred_element_type=jnp.float32
        )
        row_delta = jnp.sum(g_tile.astype(jnp.float32) * attended, axis=3)
        dprobs = jnp.einsum("ghqd,gehkd->ghqek", g_tile, v_tile, preferred_element_type=jnp.float32)
        dscores = prob_vals * (dprobs - row_delta[:, :, :, None, None])
        ds_bf = dscores.astype(jnp.bfloat16)
        dq_tile = (
            jnp.einsum("ghqek,gehkd->ghqd", ds_bf, k_tile, preferred_element_type=jnp.float32)
            * score_scale
        ).astype(jnp.bfloat16)
        dk_tile = (
            jnp.einsum("ghqek,ghqd->gehkd", ds_bf, q_tile, preferred_element_type=jnp.float32)
            * score_scale
        )
        dv_tile = jnp.einsum(
            "ghqek,ghqd->gehkd", probs_bf, g_tile, preferred_element_type=jnp.float32
        )
        grads = jnp.stack([dk_tile, dv_tile], axis=2)
        grads = grads.reshape((group_size * entry_count,) + grads.shape[2:])
        grad_acc = grad_acc.at[index_group.reshape(-1)].add(grads)
        return (grad_acc, dq_tile)

    zero_acc = jnp.zeros(key_pool.shape, jnp.float32)
    inputs = (
        split_groups(q_blocks),
        split_groups(g_blocks),
        split_groups(pool_index),
        split_groups(usable),
    )
    grad_acc, dq_groups = lax.scan(group_step, zero_acc, inputs)
    return (grad_acc, dq_groups.reshape(q_blocks.shape))


def global_scores(q_glob, k_slice, score_scale):
    return (
        jnp.einsum("hqd,nhbd->hqnb", q_glob, k_slice, preferred_element_type=jnp.float32)
        * score_scale
    )


def global_grads(scores, log_norm, row_delta, g_glob, v_slice):
    prob_vals = jnp.exp(scores - log_norm[:, :, None, None])
    probs_bf = prob_vals.astype(jnp.bfloat16)
    dprobs = jnp.einsum("hqd,nhbd->hqnb", g_glob, v_slice, preferred_element_type=jnp.float32)
    ds_bf = (prob_vals * (dprobs - row_delta[:, :, None, None])).astype(jnp.bfloat16)
    return (probs_bf, ds_bf)


def split_heads(queries, keys_in, values_in, out_grad, rand_owner, rand_local):
    q_local, k_local, v_local, g_local = (
        lax.all_to_all(queries, "head", split_axis=1, concat_axis=0, tiled=True),
        lax.all_to_all(keys_in, "head", split_axis=1, concat_axis=0, tiled=True),
        lax.all_to_all(values_in, "head", split_axis=1, concat_axis=0, tiled=True),
        lax.all_to_all(out_grad, "head", split_axis=1, concat_axis=0, tiled=True),
    )
    n_ctx = lax.axis_size("ctx")
    ctx_id = lax.axis_index("ctx")
    local_rows, feat_width = q_local.shape
    range_blocks = local_rows // BLOCK_LEN
    local_heads = feat_width // HEAD_DIM
    total_blocks = range_blocks * n_ctx
    glob_rows = GLOBALS * BLOCK_LEN
    score_scale = 1.0 / math.sqrt(HEAD_DIM)
    q_blocks = head_major(q_local, BLOCK_LEN, HEAD_DIM)
    g_blocks = head_major(g_local, BLOCK_LEN, HEAD_DIM)
    kv_local = jnp.stack(
        [head_major(k_local, BLOCK_LEN, HEAD_DIM), head_major(v_local, BLOCK_LEN, HEAD_DIM)], axis=1
    )
    pool_tail = (2, local_heads, BLOCK_LEN, HEAD_DIM)
    listed, usable = entry_blocks(rand_owner, rand_local, range_blocks, GLOBALS, total_blocks)
    my_listed = lax.dynamic_slice_in_dim(listed, ctx_id * range_blocks, range_blocks, 0)
    my_usable = lax.dynamic_slice_in_dim(usable, ctx_id * range_blocks, range_blocks, 0)
    key_pool = lax.all_gather(kv_local, "ctx", axis=0, tiled=True)
    grad_acc, dq_regular = regular_part(
        q_blocks, g_blocks, key_pool, my_listed, my_usable, score_scale
    )
    summed = lax.psum_scatter(
        grad_acc.astype(jnp.bfloat16), "ctx", scatter_dimension=0, tiled=True
    ).astype(jnp.float32)
    q_shared, g_shared = (
        broadcast(q_blocks[:GLOBALS], "ctx", 0),
        broadcast(g_blocks[:GLOBALS], "ctx", 0),
    )
    q_glob = jnp.transpose(q_shared, (1, 0, 2, 3)).reshape(local_heads, glob_rows, HEAD_DIM)
    g_glob = jnp.transpose(g_shared, (1, 0, 2, 3)).reshape(local_heads, glob_rows, HEAD_DIM)
    k_own = kv_local[:, 0]
    v_own = kv_local[:, 1]
    slice_parts = key_pool.reshape((n_ctx, range_blocks) + pool_tail)

    def stats_step(stats_carry, slice_part):
        row_top, row_total = stats_carry
        scores = global_scores(q_glob, slice_part[:, 0], score_scale)
        new_top = jnp.maximum(row_top, jnp.max(scores, axis=(2, 3)))
        row_total = row_total * jnp.exp(row_top - new_top) + jnp.sum(
            jnp.exp(scores - new_top[:, :, None, None]), axis=(2, 3)
        )
        return ((new_top, row_total), None)

    start_stats = (
        jnp.full((local_heads, glob_rows), NEG_BIG, jnp.float32),
        jnp.zeros((local_heads, glob_rows), jnp.float32),
    )
    (row_top, row_total), _ = lax.scan(stats_step, start_stats, slice_parts)
    log_norm = row_top + jnp.log(row_total)

    def out_step(attended, slice_part):
        scores = global_scores(q_glob, slice_part[:, 0], score_scale)
        probs_bf = jnp.exp(scores - log_norm[:, :, None, None]).astype(jnp.bfloat16)
        return (
            attended
            + jnp.einsum(
                "hqnb,nhbd->hqd", probs_bf, slice_part[:, 1], preferred_element_type=jnp.float32
            ),
            None,
        )

    attended, _ = lax.scan(
        out_step, jnp.zeros((local_heads, glob_rows, HEAD_DIM), jnp.float32), slice_parts
    )
    row_delta = jnp.sum(g_glob.astype(jnp.float32) * attended, axis=2)

    def dq_step(dq_acc, slice_part):
        k_slice = slice_part[:, 0]
        scores = global_scores(q_glob, k_slice, score_scale)
        probs_bf, ds_bf = global_grads(scores, log_norm, row_delta, g_glob, slice_part[:, 1])
        return (
            dq_acc
            + jnp.einsum("hqnb,nhbd->hqd", ds_bf, k_slice, preferred_element_type=jnp.float32)
            * score_scale,
            None,
        )

    dq_glob, _ = lax.scan(
        dq_step, jnp.zeros((local_heads, glob_rows, HEAD_DIM), jnp.float32), slice_parts
    )
    own_scores = global_scores(q_glob, k_own, score_scale)
    probs_bf, ds_bf = global_grads(own_scores, log_norm, row_delta, g_glob, v_own)
    dk_glob = (
        jnp.einsum("hqnb,hqd->nhbd", ds_bf, q_glob, preferred_element_type=jnp.float32)
        * score_scale
    )
    dv_glob = jnp.einsum("hqnb,hqd->nhbd", probs_bf, g_glob, preferred_element_type=jnp.float32)
    glob_extra = jnp.stack([dk_glob, dv_glob], axis=1)
    final_kv = (summed + glob_extra).astype(jnp.bfloat16)
    dq_rows = token_major(dq_regular)
    glob_dq_rows = (
        jnp.transpose(dq_glob, (1, 0, 2)).reshape(glob_rows, feat_width).astype(jnp.bfloat16)
    )
    head_rows = jnp.where(ctx_id == 0, glob_dq_rows, dq_rows[:glob_rows])
    dq_final = jnp.concatenate([head_rows, dq_rows[glob_rows:]], axis=0)
    dk_final = token_major(final_kv[:, 0])
    dv_final = token_major(final_kv[:, 1])
    return (
        lax.all_to_all(dq_final, "head", split_axis=0, concat_axis=1, tiled=True),
        lax.all_to_all(dk_final, "head", split_axis=0, concat_axis=1, tiled=True),
        lax.all_to_all(dv_final, "head", split_axis=0, concat_axis=1, tiled=True),
    )


def dot_nn(left, right):
    return lax.dot_general(left, right, (((1,), (0,)), ((), ())), preferred_element_type=jnp.float32)


def dot_nt(left, right):
    return lax.dot_general(left, right, (((1,), (1,)), ((), ())), preferred_element_type=jnp.float32)


def name_edges(range_blocks, owner_ref, local_ref, named_ref, bias_ref):
    randoms, blocks = owner_ref.shape

    def name_step(block_id, carry):
        earlier = []
        for nth in range(randoms):
            named = owner_ref[nth, block_id] * range_blocks + local_ref[nth, block_id]
            fresh = (named >= GLOBALS) & ((named < block_id - 1) | (named > block_id + 1))
            for before in earlier:
                fresh = fresh & (named != before)
            earlier.append(named)
            edge = block_id * randoms + nth
            named_ref[edge] = named
            bias_ref[edge] = jnp.where(fresh, 0.0, -NEG_BIG).astype(jnp.float32)
        return carry

    lax.fori_loop(0, blocks, name_step, 0)


def link_edges(range_blocks, owner, local, width):
    randoms, blocks = owner.shape
    named = owner * range_blocks + local
    row_id = lax.broadcasted_iota(jnp.int32, (blocks, blocks), 0)
    column_id = lax.broadcasted_iota(jnp.int32, (blocks, blocks), 1)
    across = [jnp.broadcast_to(named[nth : nth + 1], (blocks, blocks)) for nth in range(randoms)]

    def latest(wanted, before):
        found = jnp.full((blocks, blocks), -1, jnp.int32)
        for nth in range(randoms):
            hit = (across[nth] == wanted) & (column_id >= GLOBALS) & (column_id < before)
            found = jnp.maximum(found, jnp.where(hit, column_id * randoms + nth, -1))
        return jnp.max(found, axis=1, keepdims=True)

    columns = []
    for nth in range(randoms):
        down = jnp.sum(jnp.where(row_id == column_id, across[nth], 0), axis=1, keepdims=True)
        columns.append(latest(down, row_id))
    columns.append(latest(row_id, blocks))
    slot = lax.broadcasted_iota(jnp.int32, (blocks, width), 1)
    table = jnp.full((blocks, width), -1, jnp.int32)
    for nth, column in enumerate(columns):
        table = jnp.where(slot == nth, column, table)
    return table


def head_kernel(ctx_size, heads_axis, owner_ref, local_ref, owner_rows, local_rows, k_in, v_in, q_in, g_in,
                dq_out, dk_out, dv_out, named_ref, bias_ref, links_ref, table_ref, kv_ref, qg_ref, grads_ref, acc_ref, edge_ref, kt_ref, pair_ref, s_ref, dp_ref,
                send_sem, recv_sem, own_sem, table_sem):
    blocks, randoms = kv_ref.shape[0], edge_ref.shape[0] // kv_ref.shape[0]
    devices = ctx_size * heads_axis
    score_scale = 1.0 / math.sqrt(HEAD_DIM)
    exp_scale = score_scale * math.log2(math.e)
    glob_rows = GLOBALS * BLOCK_LEN
    group = 4
    chunk = group * BLOCK_LEN
    chunks = blocks // group
    bf16 = jnp.bfloat16
    ctx_id, head_id = lax.axis_index("ctx"), lax.axis_index("head")
    me = ctx_id * heads_axis + head_id
    ins = (k_in, v_in, q_in, g_in)
    landing = (kv_ref, kv_ref, qg_ref, qg_ref)
    outs = (dq_out, dk_out, dv_out)

    def head_columns(block_id):
        return pl.ds(pl.multiple_of(block_id * HEAD_DIM, HEAD_DIM), HEAD_DIM)

    inner = (ctx_id > 0) & (ctx_id < ctx_size - 1)
    near = (1, 0)
    far = (jnp.where(inner, 3, 2), jnp.where(inner, 2, 3))

    def peer_at(ctx_off, head_off):
        return ctx_id ^ ctx_off, head_id ^ head_off, ctx_off * heads_axis + head_off

    def ends(which, peer):
        if which < 4:
            half = (which % 2) * HEAD_DIM
            return (
                ins[which].at[:, head_columns(peer)],
                landing[which].at[me, :, half : half + HEAD_DIM],
            )
        return (
            grads_ref.at[which - 4, peer],
            outs[which - 4].at[:, head_columns(me)],
        )

    def remote(which, peer_ctx, peer_head, offset):
        src, dst = ends(which, peer_ctx * heads_axis + peer_head)
        return pltpu.make_async_remote_copy(
            src_ref=src,
            dst_ref=dst,
            send_sem=send_sem.at[which, offset],
            recv_sem=recv_sem.at[which, offset],
            device_id=(peer_ctx, peer_head),
            device_id_type=MESH,
        )

    def own(which):
        src, dst = ends(which, me)
        return pltpu.make_async_copy(src, dst, own_sem.at[which])

    def over_peers(ctx_offs, action, first=0, until=heads_axis):
        def one(head_off, carry):
            for ctx_off in ctx_offs:
                if isinstance(ctx_off, int) and ctx_off == 0:

                    @pl.when(head_off > 0)
                    def _():
                        action(*peer_at(ctx_off, head_off))

                else:
                    action(*peer_at(ctx_off, head_off))
            return carry

        lax.fori_loop(first, until, one, 0)

    def start_all(ctx_offs, *names):
        def action(*peer):
            for which in names:
                remote(which, *peer).start()

        over_peers(ctx_offs, action)

    barrier = pltpu.get_barrier_semaphore()

    def greet(peer_ctx, peer_head, offset):
        pl.semaphore_signal(barrier, inc=1, device_id=(peer_ctx, peer_head), device_id_type=MESH)

    over_peers(far + near, greet)
    pl.semaphore_wait(barrier, devices - 1)
    start_all(far + near, 0)
    start_all(far + near, 1)

    for which in range(4):
        own(which).start()
    table_ref[...] = link_edges(
        blocks // ctx_size, owner_rows[...], local_rows[...], table_ref.shape[1]
    )
    table_copy = pltpu.make_async_copy(table_ref, links_ref, table_sem)
    table_copy.start()
    name_edges(blocks // ctx_size, owner_ref, local_ref, named_ref, bias_ref)
    pair_ref[...] = jnp.zeros_like(pair_ref)
    acc_ref[...] = jnp.zeros_like(acc_ref)
    edge_ref[: GLOBALS * randoms] = jnp.zeros(
        (GLOBALS * randoms, BLOCK_LEN, 2 * HEAD_DIM), jnp.float32
    )
    for which in range(4):
        own(which).wait()
    table_copy.wait()

    early = 4

    def keys_arrived(*peer):
        remote(0, *peer).wait_recv()
        remote(1, *peer).wait_recv()

    over_peers(far, keys_arrived, 0, early)

    start_all(far + near, 2, 3)
    over_peers(far, keys_arrived, early, heads_axis)
    over_peers(near, keys_arrived)

    def turn_step(block_id, carry):
        kt_ref[block_id] = kv_ref[block_id, :, :HEAD_DIM].T
        return carry

    lax.fori_loop(0, blocks, turn_step, 0, unroll=4)

    def attend(block_id):
        pair_ref[:BLOCK_LEN, :HEAD_DIM] = qg_ref[block_id, :, :HEAD_DIM]
        pair_ref[BLOCK_LEN:, HEAD_DIM:] = qg_ref[block_id, :, HEAD_DIM:]
        pair = pair_ref[...]
        ids = [block_id - 1, block_id, jnp.minimum(block_id + 1, blocks - 1)]
        bias = [
            jnp.where(block_id - 1 >= GLOBALS, 0.0, -NEG_BIG).astype(jnp.float32),
            0.0,
            jnp.where(block_id + 1 < blocks, 0.0, -NEG_BIG).astype(jnp.float32),
        ]
        ids += list(range(GLOBALS))
        bias += [0.0] * GLOBALS
        fixed = len(ids)
        for nth in range(randoms):
            ids.append(named_ref[block_id * randoms + nth])
            bias.append(bias_ref[block_id * randoms + nth])
        both = [dot_nt(kv_ref[key_id], pair) for key_id in ids]
        row_top = None
        for part, off in zip(both, bias):
            part_top = jnp.max(part[:, :BLOCK_LEN], axis=0, keepdims=True) - off
            row_top = part_top if row_top is None else jnp.maximum(row_top, part_top)
        top_scaled = row_top * exp_scale
        probs, row_total, row_dot = [], 0.0, 0.0
        for part, off in zip(both, bias):
            vals = jnp.exp2(part[:, :BLOCK_LEN] * exp_scale - (top_scaled + off))
            row_total += jnp.sum(vals, axis=0, keepdims=True)
            row_dot += jnp.sum(vals * part[:, BLOCK_LEN:], axis=0, keepdims=True)
            probs.append(vals)
        inverse = 1.0 / row_total
        row_delta = row_dot * inverse
        dq_acc = jnp.zeros((HEAD_DIM, BLOCK_LEN), jnp.float32)
        for nth, (part, vals, key_id) in enumerate(zip(both, probs, ids)):
            vals = vals * inverse
            ds_bf = (vals * (part[:, BLOCK_LEN:] - row_delta)).astype(bf16)
            left = jnp.concatenate([ds_bf, vals.astype(bf16)], axis=1)
            if nth < fixed:
                acc_ref[key_id] += dot_nn(left, pair)
            else:
                edge_ref[block_id * randoms + nth - fixed] = dot_nn(left, pair)
            dq_acc += dot_nn(kt_ref[key_id], ds_bf)
        grads_ref[0, block_id] = (dq_acc.T * score_scale).astype(bf16)

    def send_queries_grad(*peer):
        @pl.when(peer[0] * heads_axis + peer[1] >= GLOBALS)
        def _():
            remote(4, *peer).start()

    def handle(send, remote_block, *peer):
        block_id = peer[0] * heads_axis + peer[1]

        @pl.when(remote_block)
        def _():
            remote(2, *peer).wait_recv()
            remote(3, *peer).wait_recv()

        @pl.when(block_id >= GLOBALS)
        def _():
            attend(block_id)

            @pl.when(send & remote_block)
            def _():
                remote(4, *peer).start()

    def block_step(step, carry):
        group_id, head_off = step // heads_axis, step % heads_axis
        far_off = jnp.where(group_id == 2, far[0], far[1])
        ctx_off = jnp.where(group_id < 2, group_id, far_off)
        handle((group_id < 2) | jnp.logical_not(inner), step > 0, *peer_at(ctx_off, head_off))
        return carry

    lax.fori_loop(0, devices, block_step, 0)

    @pl.when(inner)
    def _():
        over_peers(far, send_queries_grad)

    q_glob = qg_ref[:GLOBALS, :, :HEAD_DIM].reshape(glob_rows, HEAD_DIM)
    g_glob = qg_ref[:GLOBALS, :, HEAD_DIM:].reshape(glob_rows, HEAD_DIM)

    def keys_of(step, half):
        part = kv_ref[pl.ds(step * group, group), :, half * HEAD_DIM : (half + 1) * HEAD_DIM]
        return part.reshape(chunk, HEAD_DIM)

    def scores_step(step, row_top):
        rows = pl.ds(pl.multiple_of(step * chunk, chunk), chunk)
        scores = dot_nt(keys_of(step, 0), q_glob)
        s_ref[rows, :] = scores
        return jnp.maximum(row_top, jnp.max(scores, axis=0, keepdims=True))

    row_top = lax.fori_loop(
        0, chunks, scores_step, jnp.full((1, glob_rows), NEG_BIG, jnp.float32)
    )
    top_scaled = row_top * exp_scale

    def probs_step(step, sums):
        rows = pl.ds(pl.multiple_of(step * chunk, chunk), chunk)
        probs = jnp.exp2(s_ref[rows, :] * exp_scale - top_scaled)
        dprobs = dot_nt(keys_of(step, 1), g_glob)
        s_ref[rows, :] = probs
        dp_ref[rows, :] = dprobs
        return (
            sums[0] + jnp.sum(probs, axis=0, keepdims=True),
            sums[1] + jnp.sum(probs * dprobs, axis=0, keepdims=True),
        )

    zero_row = jnp.zeros((1, glob_rows), jnp.float32)
    row_total, row_dot = lax.fori_loop(0, chunks, probs_step, (zero_row, zero_row))
    inverse = 1.0 / row_total
    row_delta = row_dot * inverse

    def grads_step(step, dq_acc):
        rows = pl.ds(pl.multiple_of(step * chunk, chunk), chunk)
        probs = s_ref[rows, :] * inverse
        ds_bf = (probs * (dp_ref[rows, :] - row_delta)).astype(bf16)
        probs_bf = probs.astype(bf16)
        at = pl.ds(step * group, group)
        shape = (group, BLOCK_LEN, HEAD_DIM)
        acc_ref[at, :, :HEAD_DIM] += dot_nn(ds_bf, q_glob).reshape(shape)
        acc_ref[at, :, HEAD_DIM:] += dot_nn(probs_bf, g_glob).reshape(shape)
        for nth in range(group):
            dq_acc += dot_nn(
                kt_ref[step * group + nth], ds_bf[nth * BLOCK_LEN : (nth + 1) * BLOCK_LEN]
            )
        return dq_acc

    dq_glob = lax.fori_loop(
        0, chunks, grads_step, jnp.zeros((HEAD_DIM, glob_rows), jnp.float32)
    )
    dq_rows = (dq_glob.T * score_scale).astype(bf16)
    for block_id in range(GLOBALS):
        grads_ref[0, block_id] = dq_rows[block_id * BLOCK_LEN : (block_id + 1) * BLOCK_LEN]

        @pl.when(me != block_id)
        def _():
            remote(4, 0, block_id, ctx_id * heads_axis + (head_id ^ block_id)).start()

    own(4).start()

    def linked(block_id, slot):
        edge = links_ref[block_id, slot]
        weight = jnp.where(edge >= 0, 1.0, 0.0).astype(jnp.float32)
        return weight * edge_ref[jnp.maximum(edge, 0)]

    def chain_step(block_id, carry):
        for nth in range(randoms):
            edge_ref[block_id * randoms + nth] += linked(block_id, nth)
        return carry

    lax.fori_loop(GLOBALS, blocks, chain_step, 0)

    def finish(*peer):
        block_id = peer[0] * heads_axis + peer[1]
        total = acc_ref[block_id] + linked(block_id, randoms)
        grads_ref[1, block_id] = (total[:, :HEAD_DIM] * score_scale).astype(bf16)
        grads_ref[2, block_id] = total[:, HEAD_DIM:].astype(bf16)

    def finish_step(step, carry):
        head_off, turn = step // ctx_size, step % ctx_size
        ctx_off = jnp.where(turn == 0, far[0], jnp.where(turn == 1, far[1], ctx_size - 1 - turn))
        peer = peer_at(ctx_off, head_off)
        finish(*peer)

        @pl.when(step != ctx_size - 1)
        def _():
            remote(5, *peer).start()
            remote(6, *peer).start()

        return carry

    lax.fori_loop(0, devices, finish_step, 0)
    own(5).start()
    own(6).start()
    for which in range(4, 7):
        own(which).wait()

    def all_done(*peer):
        for which in range(4):
            remote(which, *peer).wait_send()
        for which in range(4, 7):
            remote(which, *peer).wait()

    over_peers(far + near, all_done)


def copy_kernel(count, *refs):
    for nth in range(count):
        refs[count + nth][...] = refs[nth][...]


def one_head(queries, keys_in, values_in, out_grad, rand_owner, rand_local):
    ctx_size, heads_axis = lax.axis_size("ctx"), lax.axis_size("head")
    devices = ctx_size * heads_axis
    rows, feat_width = queries.shape
    tokens = rows * devices
    blocks, randoms = rand_owner.shape
    edges = blocks * randoms
    anywhere = pl.BlockSpec(memory_space=pl.ANY)
    smem = pl.BlockSpec(memory_space=pltpu.SMEM)
    vmem = pl.BlockSpec(memory_space=pltpu.VMEM)
    bf16 = jnp.bfloat16
    grads = pl.pallas_call(
        functools.partial(head_kernel, ctx_size, heads_axis),
        out_shape=[jax.ShapeDtypeStruct((rows, feat_width), bf16)] * 3,
        in_specs=[smem] * 2 + [vmem] * 2 + [anywhere] * 4,
        out_specs=[anywhere] * 3,
        scratch_shapes=[
            pltpu.SMEM((edges,), jnp.int32),
            pltpu.SMEM((edges,), jnp.float32),
            pltpu.SMEM((blocks, 128), jnp.int32),
            pltpu.VMEM((blocks, 128), jnp.int32),
            pltpu.VMEM((blocks, BLOCK_LEN, 2 * HEAD_DIM), bf16),
            pltpu.VMEM((blocks, BLOCK_LEN, 2 * HEAD_DIM), bf16),
            pltpu.VMEM((3, blocks, BLOCK_LEN, HEAD_DIM), bf16),
            pltpu.VMEM((blocks, BLOCK_LEN, 2 * HEAD_DIM), jnp.float32),
            pltpu.VMEM((edges, BLOCK_LEN, 2 * HEAD_DIM), jnp.float32),
            pltpu.VMEM((blocks, HEAD_DIM, BLOCK_LEN), bf16),
            pltpu.VMEM((2 * BLOCK_LEN, 2 * HEAD_DIM), bf16),
            pltpu.VMEM((tokens, GLOBALS * BLOCK_LEN), jnp.float32),
            pltpu.VMEM((tokens, GLOBALS * BLOCK_LEN), jnp.float32),
            pltpu.SemaphoreType.DMA((7, devices)),
            pltpu.SemaphoreType.DMA((7, devices)),
            pltpu.SemaphoreType.DMA((7,)),
            pltpu.SemaphoreType.DMA,
        ],
        compiler_params=pltpu.CompilerParams(
            collective_id=1, has_side_effects=True, vmem_limit_bytes=52 << 20
        ),
    )(rand_owner.T, rand_local.T, rand_owner.T, rand_local.T, keys_in, values_in, queries, out_grad)
    tile = pl.BlockSpec((rows // 4, feat_width), lambda step: (step, 0))
    return tuple(
        pl.pallas_call(
            functools.partial(copy_kernel, 3),
            out_shape=[jax.ShapeDtypeStruct((rows, feat_width), bf16)] * 3,
            grid=(4,),
            in_specs=[tile] * 3,
            out_specs=[tile] * 3,
        )(*grads)
    )


def per_device(*args):
    devices = lax.axis_size(("ctx", "head"))
    rows, feat_width = args[0].shape
    fits = feat_width == devices * HEAD_DIM and rows == BLOCK_LEN and lax.axis_size("ctx") == 4
    return one_head(*args) if fits else split_heads(*args)


def solution(mesh):
    return jax.shard_map(
        per_device,
        mesh=mesh,
        in_specs=(
            P(("ctx", "head"), None),
            P(("ctx", "head"), None),
            P(("ctx", "head"), None),
            P(("ctx", "head"), None),
            P(),
            P(),
        ),
        out_specs=(P(("ctx", "head"), None), P(("ctx", "head"), None), P(("ctx", "head"), None)),
        check_vma=False,
    )
```

```python
import functools
import math

import jax
import jax.numpy as jnp
from jax import lax
from jax.experimental import pallas as pl
from jax.experimental.pallas import tpu as pltpu
from jax.sharding import PartitionSpec as P

MESH = pl.DeviceIdType.MESH

HEAD_DIM = 128
BLOCK_LEN = 128
GLOBALS = 2


NEG_BIG = -1e30


def broadcast(block, axis, holder):
    block = jnp.where(lax.axis_index(axis) == holder, block, jnp.zeros_like(block))
    return lax.psum(block, axis)


def entry_blocks(rand_owner, rand_local, range_blocks, glob_count, total_blocks):
    block_ids = jnp.arange(total_blocks, dtype=jnp.int32)
    fixed_cols = [block_ids - 1, block_ids, block_ids + 1]
    fixed_cols = fixed_cols + [
        jnp.full((total_blocks,), glob_id, jnp.int32) for glob_id in range(glob_count)
    ]
    listed = jnp.concatenate(
        [jnp.stack(fixed_cols, axis=1), rand_owner * range_blocks + rand_local], axis=1
    )
    inside = (listed >= 0) & (listed < total_blocks)
    entry_count = listed.shape[1]
    equal_pair = (listed[:, :, None] == listed[:, None, :]) & inside[:, None, :]
    earlier = jnp.tril(jnp.ones((entry_count, entry_count), jnp.int32), -1) > 0
    repeated = jnp.any(equal_pair & earlier[None, :, :], axis=2)
    usable = inside & jnp.logical_not(repeated) & (block_ids >= glob_count)[:, None]
    return (jnp.clip(listed, 0, total_blocks - 1), usable)


def head_major(rows_arr, block_len, head_dim):
    row_count, feat_width = rows_arr.shape
    shaped = rows_arr.reshape(row_count // block_len, block_len, feat_width // head_dim, head_dim)
    return jnp.transpose(shaped, (0, 2, 1, 3))


def token_major(blocks_arr):
    block_count, heads, block_len, head_dim = blocks_arr.shape
    return jnp.transpose(blocks_arr, (0, 2, 1, 3)).reshape(
        block_count * block_len, heads * head_dim
    )


def regular_part(q_blocks, g_blocks, key_pool, pool_index, usable, score_scale):
    range_blocks, local_heads, block_len, head_dim = q_blocks.shape
    entry_count = pool_index.shape[1]
    group_size = math.gcd(range_blocks, max(1, 512 // block_len))
    group_count = range_blocks // group_size

    def split_groups(tensor):
        return tensor.reshape((group_count, group_size) + tensor.shape[1:])

    def group_step(grad_acc, inputs):
        q_tile, g_tile, index_group, usable_group = inputs
        kv_tile = jnp.stack(
            [
                lax.dynamic_index_in_dim(key_pool, index_group[row, col], 0, keepdims=False)
                for row in range(group_size)
                for col in range(entry_count)
            ]
        ).reshape(index_group.shape + key_pool.shape[1:])
        k_tile = kv_tile[:, :, 0]
        v_tile = kv_tile[:, :, 1]
        key_mask = usable_group[:, None, None, :, None]
        scores = (
            jnp.einsum("ghqd,gehkd->ghqek", q_tile, k_tile, preferred_element_type=jnp.float32)
            * score_scale
        )
        scores = jnp.where(key_mask, scores, NEG_BIG)
        row_top = jnp.max(scores, axis=(3, 4), keepdims=True)
        row_total = jnp.sum(
            jnp.where(key_mask, jnp.exp(scores - row_top), 0.0), axis=(3, 4), keepdims=True
        )
        log_norm = row_top + jnp.log(jnp.where(row_total > 0, row_total, 1.0))
        prob_vals = jnp.where(key_mask, jnp.exp(scores - log_norm), 0.0)
        probs_bf = prob_vals.astype(jnp.bfloat16)
        attended = jnp.einsum(
            "ghqek,gehkd->ghqd", probs_bf, v_tile, preferred_element_type=jnp.float32
        )
        row_delta = jnp.sum(g_tile.astype(jnp.float32) * attended, axis=3)
        dprobs = jnp.einsum("ghqd,gehkd->ghqek", g_tile, v_tile, preferred_element_type=jnp.float32)
        dscores = prob_vals * (dprobs - row_delta[:, :, :, None, None])
        ds_bf = dscores.astype(jnp.bfloat16)
        dq_tile = (
            jnp.einsum("ghqek,gehkd->ghqd", ds_bf, k_tile, preferred_element_type=jnp.float32)
            * score_scale
        ).astype(jnp.bfloat16)
        dk_tile = (
            jnp.einsum("ghqek,ghqd->gehkd", ds_bf, q_tile, preferred_element_type=jnp.float32)
            * score_scale
        )
        dv_tile = jnp.einsum(
            "ghqek,ghqd->gehkd", probs_bf, g_tile, preferred_element_type=jnp.float32
        )
        grads = jnp.stack([dk_tile, dv_tile], axis=2)
        grads = grads.reshape((group_size * entry_count,) + grads.shape[2:])
        grad_acc = grad_acc.at[index_group.reshape(-1)].add(grads)
        return (grad_acc, dq_tile)

    zero_acc = jnp.zeros(key_pool.shape, jnp.float32)
    inputs = (
        split_groups(q_blocks),
        split_groups(g_blocks),
        split_groups(pool_index),
        split_groups(usable),
    )
    grad_acc, dq_groups = lax.scan(group_step, zero_acc, inputs)
    return (grad_acc, dq_groups.reshape(q_blocks.shape))


def global_scores(q_glob, k_slice, score_scale):
    return (
        jnp.einsum("hqd,nhbd->hqnb", q_glob, k_slice, preferred_element_type=jnp.float32)
        * score_scale
    )


def global_grads(scores, log_norm, row_delta, g_glob, v_slice):
    prob_vals = jnp.exp(scores - log_norm[:, :, None, None])
    probs_bf = prob_vals.astype(jnp.bfloat16)
    dprobs = jnp.einsum("hqd,nhbd->hqnb", g_glob, v_slice, preferred_element_type=jnp.float32)
    ds_bf = (prob_vals * (dprobs - row_delta[:, :, None, None])).astype(jnp.bfloat16)
    return (probs_bf, ds_bf)


def split_heads(queries, keys_in, values_in, out_grad, rand_owner, rand_local):
    q_local, k_local, v_local, g_local = (
        lax.all_to_all(queries, "head", split_axis=1, concat_axis=0, tiled=True),
        lax.all_to_all(keys_in, "head", split_axis=1, concat_axis=0, tiled=True),
        lax.all_to_all(values_in, "head", split_axis=1, concat_axis=0, tiled=True),
        lax.all_to_all(out_grad, "head", split_axis=1, concat_axis=0, tiled=True),
    )
    n_ctx = lax.axis_size("ctx")
    ctx_id = lax.axis_index("ctx")
    local_rows, feat_width = q_local.shape
    range_blocks = local_rows // BLOCK_LEN
    local_heads = feat_width // HEAD_DIM
    total_blocks = range_blocks * n_ctx
    glob_rows = GLOBALS * BLOCK_LEN
    score_scale = 1.0 / math.sqrt(HEAD_DIM)
    q_blocks = head_major(q_local, BLOCK_LEN, HEAD_DIM)
    g_blocks = head_major(g_local, BLOCK_LEN, HEAD_DIM)
    kv_local = jnp.stack(
        [head_major(k_local, BLOCK_LEN, HEAD_DIM), head_major(v_local, BLOCK_LEN, HEAD_DIM)], axis=1
    )
    pool_tail = (2, local_heads, BLOCK_LEN, HEAD_DIM)
    listed, usable = entry_blocks(rand_owner, rand_local, range_blocks, GLOBALS, total_blocks)
    my_listed = lax.dynamic_slice_in_dim(listed, ctx_id * range_blocks, range_blocks, 0)
    my_usable = lax.dynamic_slice_in_dim(usable, ctx_id * range_blocks, range_blocks, 0)
    key_pool = lax.all_gather(kv_local, "ctx", axis=0, tiled=True)
    grad_acc, dq_regular = regular_part(
        q_blocks, g_blocks, key_pool, my_listed, my_usable, score_scale
    )
    summed = lax.psum_scatter(
        grad_acc.astype(jnp.bfloat16), "ctx", scatter_dimension=0, tiled=True
    ).astype(jnp.float32)
    q_shared, g_shared = (
        broadcast(q_blocks[:GLOBALS], "ctx", 0),
        broadcast(g_blocks[:GLOBALS], "ctx", 0),
    )
    q_glob = jnp.transpose(q_shared, (1, 0, 2, 3)).reshape(local_heads, glob_rows, HEAD_DIM)
    g_glob = jnp.transpose(g_shared, (1, 0, 2, 3)).reshape(local_heads, glob_rows, HEAD_DIM)
    k_own = kv_local[:, 0]
    v_own = kv_local[:, 1]
    slice_parts = key_pool.reshape((n_ctx, range_blocks) + pool_tail)

    def stats_step(stats_carry, slice_part):
        row_top, row_total = stats_carry
        scores = global_scores(q_glob, slice_part[:, 0], score_scale)
        new_top = jnp.maximum(row_top, jnp.max(scores, axis=(2, 3)))
        row_total = row_total * jnp.exp(row_top - new_top) + jnp.sum(
            jnp.exp(scores - new_top[:, :, None, None]), axis=(2, 3)
        )
        return ((new_top, row_total), None)

    start_stats = (
        jnp.full((local_heads, glob_rows), NEG_BIG, jnp.float32),
        jnp.zeros((local_heads, glob_rows), jnp.float32),
    )
    (row_top, row_total), _ = lax.scan(stats_step, start_stats, slice_parts)
    log_norm = row_top + jnp.log(row_total)

    def out_step(attended, slice_part):
        scores = global_scores(q_glob, slice_part[:, 0], score_scale)
        probs_bf = jnp.exp(scores - log_norm[:, :, None, None]).astype(jnp.bfloat16)
        return (
            attended
            + jnp.einsum(
                "hqnb,nhbd->hqd", probs_bf, slice_part[:, 1], preferred_element_type=jnp.float32
            ),
            None,
        )

    attended, _ = lax.scan(
        out_step, jnp.zeros((local_heads, glob_rows, HEAD_DIM), jnp.float32), slice_parts
    )
    row_delta = jnp.sum(g_glob.astype(jnp.float32) * attended, axis=2)

    def dq_step(dq_acc, slice_part):
        k_slice = slice_part[:, 0]
        scores = global_scores(q_glob, k_slice, score_scale)
        probs_bf, ds_bf = global_grads(scores, log_norm, row_delta, g_glob, slice_part[:, 1])
        return (
            dq_acc
            + jnp.einsum("hqnb,nhbd->hqd", ds_bf, k_slice, preferred_element_type=jnp.float32)
            * score_scale,
            None,
        )

    dq_glob, _ = lax.scan(
        dq_step, jnp.zeros((local_heads, glob_rows, HEAD_DIM), jnp.float32), slice_parts
    )
    own_scores = global_scores(q_glob, k_own, score_scale)
    probs_bf, ds_bf = global_grads(own_scores, log_norm, row_delta, g_glob, v_own)
    dk_glob = (
        jnp.einsum("hqnb,hqd->nhbd", ds_bf, q_glob, preferred_element_type=jnp.float32)
        * score_scale
    )
    dv_glob = jnp.einsum("hqnb,hqd->nhbd", probs_bf, g_glob, preferred_element_type=jnp.float32)
    glob_extra = jnp.stack([dk_glob, dv_glob], axis=1)
    final_kv = (summed + glob_extra).astype(jnp.bfloat16)
    dq_rows = token_major(dq_regular)
    glob_dq_rows = (
        jnp.transpose(dq_glob, (1, 0, 2)).reshape(glob_rows, feat_width).astype(jnp.bfloat16)
    )
    head_rows = jnp.where(ctx_id == 0, glob_dq_rows, dq_rows[:glob_rows])
    dq_final = jnp.concatenate([head_rows, dq_rows[glob_rows:]], axis=0)
    dk_final = token_major(final_kv[:, 0])
    dv_final = token_major(final_kv[:, 1])
    return (
        lax.all_to_all(dq_final, "head", split_axis=0, concat_axis=1, tiled=True),
        lax.all_to_all(dk_final, "head", split_axis=0, concat_axis=1, tiled=True),
        lax.all_to_all(dv_final, "head", split_axis=0, concat_axis=1, tiled=True),
    )


def dot_nn(left, right):
    return lax.dot_general(left, right, (((1,), (0,)), ((), ())), preferred_element_type=jnp.float32)


def dot_nt(left, right):
    return lax.dot_general(left, right, (((1,), (1,)), ((), ())), preferred_element_type=jnp.float32)


def name_edges(range_blocks, owner_ref, local_ref, named_ref, bias_ref):
    randoms, blocks = owner_ref.shape

    def name_step(block_id, carry):
        earlier = []
        for nth in range(randoms):
            named = owner_ref[nth, block_id] * range_blocks + local_ref[nth, block_id]
            fresh = (named >= GLOBALS) & ((named < block_id - 1) | (named > block_id + 1))
            for before in earlier:
                fresh = fresh & (named != before)
            earlier.append(named)
            edge = block_id * randoms + nth
            named_ref[edge] = named
            bias_ref[edge] = jnp.where(fresh, 0.0, -NEG_BIG).astype(jnp.float32)
        return carry

    lax.fori_loop(0, blocks, name_step, 0)


def link_edges(range_blocks, owner, local, width):
    randoms, blocks = owner.shape
    named = owner * range_blocks + local
    row_id = lax.broadcasted_iota(jnp.int32, (blocks, blocks), 0)
    column_id = lax.broadcasted_iota(jnp.int32, (blocks, blocks), 1)
    across = [jnp.broadcast_to(named[nth : nth + 1], (blocks, blocks)) for nth in range(randoms)]

    def latest(wanted, before):
        found = jnp.full((blocks, blocks), -1, jnp.int32)
        for nth in range(randoms):
            hit = (across[nth] == wanted) & (column_id >= GLOBALS) & (column_id < before)
            found = jnp.maximum(found, jnp.where(hit, column_id * randoms + nth, -1))
        return jnp.max(found, axis=1, keepdims=True)

    columns = []
    for nth in range(randoms):
        down = jnp.sum(jnp.where(row_id == column_id, across[nth], 0), axis=1, keepdims=True)
        columns.append(latest(down, row_id))
    columns.append(latest(row_id, blocks))
    slot = lax.broadcasted_iota(jnp.int32, (blocks, width), 1)
    table = jnp.full((blocks, width), -1, jnp.int32)
    for nth, column in enumerate(columns):
        table = jnp.where(slot == nth, column, table)
    return table


def head_kernel(ctx_size, heads_axis, owner_in, local_in, k_in, v_in, q_in, g_in,
                dq_out, dk_out, dv_out, owner_ref, local_ref, owner_rows, local_rows,
                named_ref, bias_ref, links_ref, table_ref, kv_ref, qg_ref, grads_ref, acc_ref, edge_ref, kt_ref, pair_ref, s_ref, dp_ref,
                send_sem, recv_sem, own_sem, table_sem, index_sem):
    blocks, randoms = kv_ref.shape[0], edge_ref.shape[0] // kv_ref.shape[0]
    devices = ctx_size * heads_axis
    score_scale = 1.0 / math.sqrt(HEAD_DIM)
    exp_scale = score_scale * math.log2(math.e)
    glob_rows = GLOBALS * BLOCK_LEN
    group = 4
    chunk = group * BLOCK_LEN
    chunks = blocks // group
    bf16 = jnp.bfloat16
    ctx_id, head_id = lax.axis_index("ctx"), lax.axis_index("head")
    me = ctx_id * heads_axis + head_id
    ins = (k_in, v_in, q_in, g_in)
    landing = (kv_ref, kv_ref, qg_ref, qg_ref)
    outs = (dq_out, dk_out, dv_out)

    def head_columns(block_id):
        return pl.ds(pl.multiple_of(block_id * HEAD_DIM, HEAD_DIM), HEAD_DIM)

    inner = (ctx_id > 0) & (ctx_id < ctx_size - 1)
    near = (1, 0)
    far = (jnp.where(inner, 3, 2), jnp.where(inner, 2, 3))

    def peer_at(ctx_off, head_off):
        return ctx_id ^ ctx_off, head_id ^ head_off, ctx_off * heads_axis + head_off

    def ends(which, peer):
        if which < 4:
            half = (which % 2) * HEAD_DIM
            return (
                ins[which].at[:, head_columns(peer)],
                landing[which].at[me, :, half : half + HEAD_DIM],
            )
        return (
            grads_ref.at[which - 4, peer],
            outs[which - 4].at[:, head_columns(me)],
        )

    def remote(which, peer_ctx, peer_head, offset):
        src, dst = ends(which, peer_ctx * heads_axis + peer_head)
        return pltpu.make_async_remote_copy(
            src_ref=src,
            dst_ref=dst,
            send_sem=send_sem.at[which, offset],
            recv_sem=recv_sem.at[which, offset],
            device_id=(peer_ctx, peer_head),
            device_id_type=MESH,
        )

    def own(which):
        src, dst = ends(which, me)
        return pltpu.make_async_copy(src, dst, own_sem.at[which])

    def over_peers(ctx_offs, action, first=0, until=heads_axis):
        def one(head_off, carry):
            for ctx_off in ctx_offs:
                if isinstance(ctx_off, int) and ctx_off == 0:

                    @pl.when(head_off > 0)
                    def _():
                        action(*peer_at(ctx_off, head_off))

                else:
                    action(*peer_at(ctx_off, head_off))
            return carry

        lax.fori_loop(first, until, one, 0)

    def start_all(ctx_offs, *names):
        def action(*peer):
            for which in names:
                remote(which, *peer).start()

        over_peers(ctx_offs, action)

    barrier = pltpu.get_barrier_semaphore()

    def greet(peer_ctx, peer_head, offset):
        pl.semaphore_signal(barrier, inc=1, device_id=(peer_ctx, peer_head), device_id_type=MESH)

    over_peers(far + near, greet)
    pl.semaphore_wait(barrier, devices - 1)
    start_all(far + near, 0)
    start_all(far + near, 1)

    for which in range(4):
        own(which).start()
    index_copies = [
        pltpu.make_async_copy(src, dst, index_sem.at[nth])
        for nth, (src, dst) in enumerate(
            zip((owner_in, local_in) * 2, (owner_ref, local_ref, owner_rows, local_rows))
        )
    ]
    for copy in index_copies:
        copy.start()
    for copy in index_copies:
        copy.wait()
    table_ref[...] = link_edges(
        blocks // ctx_size, owner_rows[...], local_rows[...], table_ref.shape[1]
    )
    table_copy = pltpu.make_async_copy(table_ref, links_ref, table_sem)
    table_copy.start()
    name_edges(blocks // ctx_size, owner_ref, local_ref, named_ref, bias_ref)
    pair_ref[...] = jnp.zeros_like(pair_ref)
    acc_ref[...] = jnp.zeros_like(acc_ref)
    edge_ref[: GLOBALS * randoms] = jnp.zeros(
        (GLOBALS * randoms, BLOCK_LEN, 2 * HEAD_DIM), jnp.float32
    )
    for which in range(4):
        own(which).wait()
    table_copy.wait()

    early = 4

    def keys_arrived(*peer):
        remote(0, *peer).wait_recv()
        remote(1, *peer).wait_recv()

    over_peers(far, keys_arrived, 0, early)

    start_all(far + near, 2, 3)
    over_peers(far, keys_arrived, early, heads_axis)
    over_peers(near, keys_arrived)

    def turn_step(block_id, carry):
        kt_ref[block_id] = kv_ref[block_id, :, :HEAD_DIM].T
        return carry

    lax.fori_loop(0, blocks, turn_step, 0, unroll=4)

    def attend(block_id):
        pair_ref[:BLOCK_LEN, :HEAD_DIM] = qg_ref[block_id, :, :HEAD_DIM]
        pair_ref[BLOCK_LEN:, HEAD_DIM:] = qg_ref[block_id, :, HEAD_DIM:]
        pair = pair_ref[...]
        ids = [block_id - 1, block_id, jnp.minimum(block_id + 1, blocks - 1)]
        bias = [
            jnp.where(block_id - 1 >= GLOBALS, 0.0, -NEG_BIG).astype(jnp.float32),
            0.0,
            jnp.where(block_id + 1 < blocks, 0.0, -NEG_BIG).astype(jnp.float32),
        ]
        ids += list(range(GLOBALS))
        bias += [0.0] * GLOBALS
        fixed = len(ids)
        for nth in range(randoms):
            ids.append(named_ref[block_id * randoms + nth])
            bias.append(bias_ref[block_id * randoms + nth])
        both = [dot_nt(kv_ref[key_id], pair) for key_id in ids]
        row_top = None
        for part, off in zip(both, bias):
            part_top = jnp.max(part[:, :BLOCK_LEN], axis=0, keepdims=True) - off
            row_top = part_top if row_top is None else jnp.maximum(row_top, part_top)
        top_scaled = row_top * exp_scale
        probs, row_total, row_dot = [], 0.0, 0.0
        for part, off in zip(both, bias):
            vals = jnp.exp2(part[:, :BLOCK_LEN] * exp_scale - (top_scaled + off))
            row_total += jnp.sum(vals, axis=0, keepdims=True)
            row_dot += jnp.sum(vals * part[:, BLOCK_LEN:], axis=0, keepdims=True)
            probs.append(vals)
        inverse = 1.0 / row_total
        row_delta = row_dot * inverse
        dq_acc = jnp.zeros((HEAD_DIM, BLOCK_LEN), jnp.float32)
        for nth, (part, vals, key_id) in enumerate(zip(both, probs, ids)):
            vals = vals * inverse
            ds_bf = (vals * (part[:, BLOCK_LEN:] - row_delta)).astype(bf16)
            left = jnp.concatenate([ds_bf, vals.astype(bf16)], axis=1)
            if nth < fixed:
                acc_ref[key_id] += dot_nn(left, pair)
            else:
                edge_ref[block_id * randoms + nth - fixed] = dot_nn(left, pair)
            if nth % 2 == 0:
                waiting, waiting_id = ds_bf, key_id
            else:
                dq_acc += dot_nn(
                    jnp.concatenate([kt_ref[waiting_id], kt_ref[key_id]], axis=1),
                    jnp.concatenate([waiting, ds_bf], axis=0),
                )
        if len(ids) % 2:
            dq_acc += dot_nn(kt_ref[waiting_id], waiting)
        grads_ref[0, block_id] = (dq_acc.T * score_scale).astype(bf16)

    def send_queries_grad(*peer):
        @pl.when(peer[0] * heads_axis + peer[1] >= GLOBALS)
        def _():
            remote(4, *peer).start()

    def handle(send, remote_block, *peer):
        block_id = peer[0] * heads_axis + peer[1]

        @pl.when(remote_block)
        def _():
            remote(2, *peer).wait_recv()
            remote(3, *peer).wait_recv()

        @pl.when(block_id >= GLOBALS)
        def _():
            attend(block_id)

            @pl.when(send & remote_block)
            def _():
                remote(4, *peer).start()

    def block_step(step, carry):
        group_id, head_off = step // heads_axis, step % heads_axis
        far_off = jnp.where(group_id == 2, far[0], far[1])
        ctx_off = jnp.where(group_id < 2, group_id, far_off)
        handle(group_id >= 0, step > 0, *peer_at(ctx_off, head_off))
        return carry

    lax.fori_loop(0, devices, block_step, 0)


    q_glob = qg_ref[:GLOBALS, :, :HEAD_DIM].reshape(glob_rows, HEAD_DIM)
    g_glob = qg_ref[:GLOBALS, :, HEAD_DIM:].reshape(glob_rows, HEAD_DIM)

    def keys_of(step, half):
        part = kv_ref[pl.ds(step * group, group), :, half * HEAD_DIM : (half + 1) * HEAD_DIM]
        return part.reshape(chunk, HEAD_DIM)

    def scores_step(step, row_top):
        rows = pl.ds(pl.multiple_of(step * chunk, chunk), chunk)
        scores = dot_nt(keys_of(step, 0), q_glob)
        s_ref[rows, :] = scores
        return jnp.maximum(row_top, jnp.max(scores, axis=0, keepdims=True))

    row_top = lax.fori_loop(
        0, chunks, scores_step, jnp.full((1, glob_rows), NEG_BIG, jnp.float32)
    )
    top_scaled = row_top * exp_scale

    def probs_step(step, sums):
        rows = pl.ds(pl.multiple_of(step * chunk, chunk), chunk)
        probs = jnp.exp2(s_ref[rows, :] * exp_scale - top_scaled)
        dprobs = dot_nt(keys_of(step, 1), g_glob)
        s_ref[rows, :] = probs
        dp_ref[rows, :] = dprobs
        return (
            sums[0] + jnp.sum(probs, axis=0, keepdims=True),
            sums[1] + jnp.sum(probs * dprobs, axis=0, keepdims=True),
        )

    zero_row = jnp.zeros((1, glob_rows), jnp.float32)
    row_total, row_dot = lax.fori_loop(0, chunks, probs_step, (zero_row, zero_row))
    inverse = 1.0 / row_total
    row_delta = row_dot * inverse

    def grads_step(step, dq_acc):
        rows = pl.ds(pl.multiple_of(step * chunk, chunk), chunk)
        probs = s_ref[rows, :] * inverse
        ds_bf = (probs * (dp_ref[rows, :] - row_delta)).astype(bf16)
        probs_bf = probs.astype(bf16)
        at = pl.ds(step * group, group)
        shape = (group, BLOCK_LEN, HEAD_DIM)
        acc_ref[at, :, :HEAD_DIM] += dot_nn(ds_bf, q_glob).reshape(shape)
        acc_ref[at, :, HEAD_DIM:] += dot_nn(probs_bf, g_glob).reshape(shape)
        for nth in range(group):
            dq_acc += dot_nn(
                kt_ref[step * group + nth], ds_bf[nth * BLOCK_LEN : (nth + 1) * BLOCK_LEN]
            )
        return dq_acc

    dq_glob = lax.fori_loop(
        0, chunks, grads_step, jnp.zeros((HEAD_DIM, glob_rows), jnp.float32)
    )
    dq_rows = (dq_glob.T * score_scale).astype(bf16)
    for block_id in range(GLOBALS):
        grads_ref[0, block_id] = dq_rows[block_id * BLOCK_LEN : (block_id + 1) * BLOCK_LEN]

        @pl.when(me != block_id)
        def _():
            remote(4, 0, block_id, ctx_id * heads_axis + (head_id ^ block_id)).start()

    own(4).start()

    def linked(block_id, slot):
        edge = links_ref[block_id, slot]
        weight = jnp.where(edge >= 0, 1.0, 0.0).astype(jnp.float32)
        return weight * edge_ref[jnp.maximum(edge, 0)]

    def chain_step(block_id, carry):
        for nth in range(randoms):
            edge_ref[block_id * randoms + nth] += linked(block_id, nth)
        return carry

    lax.fori_loop(GLOBALS, blocks, chain_step, 0)

    def finish(*peer):
        block_id = peer[0] * heads_axis + peer[1]
        total = acc_ref[block_id] + linked(block_id, randoms)
        grads_ref[1, block_id] = (total[:, :HEAD_DIM] * score_scale).astype(bf16)
        grads_ref[2, block_id] = total[:, HEAD_DIM:].astype(bf16)

    def finish_step(step, carry):
        head_off, turn = step // ctx_size, step % ctx_size
        ctx_off = jnp.where(turn == 0, far[0], jnp.where(turn == 1, far[1], ctx_size - 1 - turn))
        peer = peer_at(ctx_off, head_off)
        finish(*peer)

        @pl.when(step != ctx_size - 1)
        def _():
            remote(5, *peer).start()
            remote(6, *peer).start()

        return carry

    lax.fori_loop(0, devices, finish_step, 0)
    own(5).start()
    own(6).start()
    for which in range(4, 7):
        own(which).wait()

    def all_done(*peer):
        for which in range(4):
            remote(which, *peer).wait_send()
        for which in range(4, 7):
            remote(which, *peer).wait()

    over_peers(far + near, all_done)


def copy_kernel(count, *refs):
    ins, outs, sems = refs[:count], refs[count : 2 * count], refs[2 * count]
    copies = [pltpu.make_async_copy(ins[nth], outs[nth], sems.at[nth]) for nth in range(count)]
    for copy in copies:
        copy.start()
    for copy in copies:
        copy.wait()


def one_head(queries, keys_in, values_in, out_grad, rand_owner, rand_local):
    ctx_size, heads_axis = lax.axis_size("ctx"), lax.axis_size("head")
    devices = ctx_size * heads_axis
    rows, feat_width = queries.shape
    tokens = rows * devices
    blocks, randoms = rand_owner.shape
    edges = blocks * randoms
    anywhere = pl.BlockSpec(memory_space=pl.ANY)
    vmem = pl.BlockSpec(memory_space=pltpu.VMEM)
    hbm = pl.BlockSpec(memory_space=pltpu.HBM)
    bf16 = jnp.bfloat16
    grads = pl.pallas_call(
        functools.partial(head_kernel, ctx_size, heads_axis),
        out_shape=[jax.ShapeDtypeStruct((rows, feat_width), bf16)] * 3,
        in_specs=[hbm] * 6,
        out_specs=[vmem] * 3,
        scratch_shapes=[
            pltpu.SMEM((randoms, blocks), jnp.int32),
            pltpu.SMEM((randoms, blocks), jnp.int32),
            pltpu.VMEM((randoms, blocks), jnp.int32),
            pltpu.VMEM((randoms, blocks), jnp.int32),
            pltpu.SMEM((edges,), jnp.int32),
            pltpu.SMEM((edges,), jnp.float32),
            pltpu.SMEM((blocks, 128), jnp.int32),
            pltpu.VMEM((blocks, 128), jnp.int32),
            pltpu.VMEM((blocks, BLOCK_LEN, 2 * HEAD_DIM), bf16),
            pltpu.VMEM((blocks, BLOCK_LEN, 2 * HEAD_DIM), bf16),
            pltpu.VMEM((3, blocks, BLOCK_LEN, HEAD_DIM), bf16),
            pltpu.VMEM((blocks, BLOCK_LEN, 2 * HEAD_DIM), jnp.float32),
            pltpu.VMEM((edges, BLOCK_LEN, 2 * HEAD_DIM), jnp.float32),
            pltpu.VMEM((blocks, HEAD_DIM, BLOCK_LEN), bf16),
            pltpu.VMEM((2 * BLOCK_LEN, 2 * HEAD_DIM), bf16),
            pltpu.VMEM((tokens, GLOBALS * BLOCK_LEN), jnp.float32),
            pltpu.VMEM((tokens, GLOBALS * BLOCK_LEN), jnp.float32),
            pltpu.SemaphoreType.DMA((7, devices)),
            pltpu.SemaphoreType.DMA((7, devices)),
            pltpu.SemaphoreType.DMA((7,)),
            pltpu.SemaphoreType.DMA,
            pltpu.SemaphoreType.DMA((4,)),
        ],
        compiler_params=pltpu.CompilerParams(
            collective_id=1, has_side_effects=True, vmem_limit_bytes=50 << 20
        ),
    )(rand_owner.T, rand_local.T, keys_in, values_in, queries, out_grad)
    return tuple(
        pl.pallas_call(
            functools.partial(copy_kernel, 3),
            out_shape=[jax.ShapeDtypeStruct((rows, feat_width), bf16)] * 3,
            in_specs=[vmem] * 3,
            out_specs=[anywhere] * 3,
            scratch_shapes=[pltpu.SemaphoreType.DMA((3,))],
            compiler_params=pltpu.CompilerParams(vmem_limit_bytes=4 << 20),
        )(*grads)
    )


def per_device(*args):
    devices = lax.axis_size(("ctx", "head"))
    rows, feat_width = args[0].shape
    fits = feat_width == devices * HEAD_DIM and rows == BLOCK_LEN and lax.axis_size("ctx") == 4
    return one_head(*args) if fits else split_heads(*args)


def solution(mesh):
    return jax.shard_map(
        per_device,
        mesh=mesh,
        in_specs=(
            P(("ctx", "head"), None),
            P(("ctx", "head"), None),
            P(("ctx", "head"), None),
            P(("ctx", "head"), None),
            P(),
            P(),
        ),
        out_specs=(P(("ctx", "head"), None), P(("ctx", "head"), None), P(("ctx", "head"), None)),
        check_vma=False,
    )
```

```python
import functools
import math

import jax
import jax.numpy as jnp
from jax import lax
from jax.experimental import pallas as pl
from jax.experimental.pallas import tpu as pltpu
from jax.sharding import PartitionSpec as P

MESH = pl.DeviceIdType.MESH

HEAD_DIM = 128
BLOCK_LEN = 128
GLOBALS = 2


NEG_BIG = -1e30


def broadcast(block, axis, holder):
    block = jnp.where(lax.axis_index(axis) == holder, block, jnp.zeros_like(block))
    return lax.psum(block, axis)


def entry_blocks(rand_owner, rand_local, range_blocks, glob_count, total_blocks):
    block_ids = jnp.arange(total_blocks, dtype=jnp.int32)
    fixed_cols = [block_ids - 1, block_ids, block_ids + 1]
    fixed_cols = fixed_cols + [
        jnp.full((total_blocks,), glob_id, jnp.int32) for glob_id in range(glob_count)
    ]
    listed = jnp.concatenate(
        [jnp.stack(fixed_cols, axis=1), rand_owner * range_blocks + rand_local], axis=1
    )
    inside = (listed >= 0) & (listed < total_blocks)
    entry_count = listed.shape[1]
    equal_pair = (listed[:, :, None] == listed[:, None, :]) & inside[:, None, :]
    earlier = jnp.tril(jnp.ones((entry_count, entry_count), jnp.int32), -1) > 0
    repeated = jnp.any(equal_pair & earlier[None, :, :], axis=2)
    usable = inside & jnp.logical_not(repeated) & (block_ids >= glob_count)[:, None]
    return (jnp.clip(listed, 0, total_blocks - 1), usable)


def head_major(rows_arr, block_len, head_dim):
    row_count, feat_width = rows_arr.shape
    shaped = rows_arr.reshape(row_count // block_len, block_len, feat_width // head_dim, head_dim)
    return jnp.transpose(shaped, (0, 2, 1, 3))


def token_major(blocks_arr):
    block_count, heads, block_len, head_dim = blocks_arr.shape
    return jnp.transpose(blocks_arr, (0, 2, 1, 3)).reshape(
        block_count * block_len, heads * head_dim
    )


def regular_part(q_blocks, g_blocks, key_pool, pool_index, usable, score_scale):
    range_blocks, local_heads, block_len, head_dim = q_blocks.shape
    entry_count = pool_index.shape[1]
    group_size = math.gcd(range_blocks, max(1, 512 // block_len))
    group_count = range_blocks // group_size

    def split_groups(tensor):
        return tensor.reshape((group_count, group_size) + tensor.shape[1:])

    def group_step(grad_acc, inputs):
        q_tile, g_tile, index_group, usable_group = inputs
        kv_tile = jnp.stack(
            [
                lax.dynamic_index_in_dim(key_pool, index_group[row, col], 0, keepdims=False)
                for row in range(group_size)
                for col in range(entry_count)
            ]
        ).reshape(index_group.shape + key_pool.shape[1:])
        k_tile = kv_tile[:, :, 0]
        v_tile = kv_tile[:, :, 1]
        key_mask = usable_group[:, None, None, :, None]
        scores = (
            jnp.einsum("ghqd,gehkd->ghqek", q_tile, k_tile, preferred_element_type=jnp.float32)
            * score_scale
        )
        scores = jnp.where(key_mask, scores, NEG_BIG)
        row_top = jnp.max(scores, axis=(3, 4), keepdims=True)
        row_total = jnp.sum(
            jnp.where(key_mask, jnp.exp(scores - row_top), 0.0), axis=(3, 4), keepdims=True
        )
        log_norm = row_top + jnp.log(jnp.where(row_total > 0, row_total, 1.0))
        prob_vals = jnp.where(key_mask, jnp.exp(scores - log_norm), 0.0)
        probs_bf = prob_vals.astype(jnp.bfloat16)
        attended = jnp.einsum(
            "ghqek,gehkd->ghqd", probs_bf, v_tile, preferred_element_type=jnp.float32
        )
        row_delta = jnp.sum(g_tile.astype(jnp.float32) * attended, axis=3)
        dprobs = jnp.einsum("ghqd,gehkd->ghqek", g_tile, v_tile, preferred_element_type=jnp.float32)
        dscores = prob_vals * (dprobs - row_delta[:, :, :, None, None])
        ds_bf = dscores.astype(jnp.bfloat16)
        dq_tile = (
            jnp.einsum("ghqek,gehkd->ghqd", ds_bf, k_tile, preferred_element_type=jnp.float32)
            * score_scale
        ).astype(jnp.bfloat16)
        dk_tile = (
            jnp.einsum("ghqek,ghqd->gehkd", ds_bf, q_tile, preferred_element_type=jnp.float32)
            * score_scale
        )
        dv_tile = jnp.einsum(
            "ghqek,ghqd->gehkd", probs_bf, g_tile, preferred_element_type=jnp.float32
        )
        grads = jnp.stack([dk_tile, dv_tile], axis=2)
        grads = grads.reshape((group_size * entry_count,) + grads.shape[2:])
        grad_acc = grad_acc.at[index_group.reshape(-1)].add(grads)
        return (grad_acc, dq_tile)

    zero_acc = jnp.zeros(key_pool.shape, jnp.float32)
    inputs = (
        split_groups(q_blocks),
        split_groups(g_blocks),
        split_groups(pool_index),
        split_groups(usable),
    )
    grad_acc, dq_groups = lax.scan(group_step, zero_acc, inputs)
    return (grad_acc, dq_groups.reshape(q_blocks.shape))


def global_scores(q_glob, k_slice, score_scale):
    return (
        jnp.einsum("hqd,nhbd->hqnb", q_glob, k_slice, preferred_element_type=jnp.float32)
        * score_scale
    )


def global_grads(scores, log_norm, row_delta, g_glob, v_slice):
    prob_vals = jnp.exp(scores - log_norm[:, :, None, None])
    probs_bf = prob_vals.astype(jnp.bfloat16)
    dprobs = jnp.einsum("hqd,nhbd->hqnb", g_glob, v_slice, preferred_element_type=jnp.float32)
    ds_bf = (prob_vals * (dprobs - row_delta[:, :, None, None])).astype(jnp.bfloat16)
    return (probs_bf, ds_bf)


def split_heads(queries, keys_in, values_in, out_grad, rand_owner, rand_local):
    q_local, k_local, v_local, g_local = (
        lax.all_to_all(queries, "head", split_axis=1, concat_axis=0, tiled=True),
        lax.all_to_all(keys_in, "head", split_axis=1, concat_axis=0, tiled=True),
        lax.all_to_all(values_in, "head", split_axis=1, concat_axis=0, tiled=True),
        lax.all_to_all(out_grad, "head", split_axis=1, concat_axis=0, tiled=True),
    )
    n_ctx = lax.axis_size("ctx")
    ctx_id = lax.axis_index("ctx")
    local_rows, feat_width = q_local.shape
    range_blocks = local_rows // BLOCK_LEN
    local_heads = feat_width // HEAD_DIM
    total_blocks = range_blocks * n_ctx
    glob_rows = GLOBALS * BLOCK_LEN
    score_scale = 1.0 / math.sqrt(HEAD_DIM)
    q_blocks = head_major(q_local, BLOCK_LEN, HEAD_DIM)
    g_blocks = head_major(g_local, BLOCK_LEN, HEAD_DIM)
    kv_local = jnp.stack(
        [head_major(k_local, BLOCK_LEN, HEAD_DIM), head_major(v_local, BLOCK_LEN, HEAD_DIM)], axis=1
    )
    pool_tail = (2, local_heads, BLOCK_LEN, HEAD_DIM)
    listed, usable = entry_blocks(rand_owner, rand_local, range_blocks, GLOBALS, total_blocks)
    my_listed = lax.dynamic_slice_in_dim(listed, ctx_id * range_blocks, range_blocks, 0)
    my_usable = lax.dynamic_slice_in_dim(usable, ctx_id * range_blocks, range_blocks, 0)
    key_pool = lax.all_gather(kv_local, "ctx", axis=0, tiled=True)
    grad_acc, dq_regular = regular_part(
        q_blocks, g_blocks, key_pool, my_listed, my_usable, score_scale
    )
    summed = lax.psum_scatter(
        grad_acc.astype(jnp.bfloat16), "ctx", scatter_dimension=0, tiled=True
    ).astype(jnp.float32)
    q_shared, g_shared = (
        broadcast(q_blocks[:GLOBALS], "ctx", 0),
        broadcast(g_blocks[:GLOBALS], "ctx", 0),
    )
    q_glob = jnp.transpose(q_shared, (1, 0, 2, 3)).reshape(local_heads, glob_rows, HEAD_DIM)
    g_glob = jnp.transpose(g_shared, (1, 0, 2, 3)).reshape(local_heads, glob_rows, HEAD_DIM)
    k_own = kv_local[:, 0]
    v_own = kv_local[:, 1]
    slice_parts = key_pool.reshape((n_ctx, range_blocks) + pool_tail)

    def stats_step(stats_carry, slice_part):
        row_top, row_total = stats_carry
        scores = global_scores(q_glob, slice_part[:, 0], score_scale)
        new_top = jnp.maximum(row_top, jnp.max(scores, axis=(2, 3)))
        row_total = row_total * jnp.exp(row_top - new_top) + jnp.sum(
            jnp.exp(scores - new_top[:, :, None, None]), axis=(2, 3)
        )
        return ((new_top, row_total), None)

    start_stats = (
        jnp.full((local_heads, glob_rows), NEG_BIG, jnp.float32),
        jnp.zeros((local_heads, glob_rows), jnp.float32),
    )
    (row_top, row_total), _ = lax.scan(stats_step, start_stats, slice_parts)
    log_norm = row_top + jnp.log(row_total)

    def out_step(attended, slice_part):
        scores = global_scores(q_glob, slice_part[:, 0], score_scale)
        probs_bf = jnp.exp(scores - log_norm[:, :, None, None]).astype(jnp.bfloat16)
        return (
            attended
            + jnp.einsum(
                "hqnb,nhbd->hqd", probs_bf, slice_part[:, 1], preferred_element_type=jnp.float32
            ),
            None,
        )

    attended, _ = lax.scan(
        out_step, jnp.zeros((local_heads, glob_rows, HEAD_DIM), jnp.float32), slice_parts
    )
    row_delta = jnp.sum(g_glob.astype(jnp.float32) * attended, axis=2)

    def dq_step(dq_acc, slice_part):
        k_slice = slice_part[:, 0]
        scores = global_scores(q_glob, k_slice, score_scale)
        probs_bf, ds_bf = global_grads(scores, log_norm, row_delta, g_glob, slice_part[:, 1])
        return (
            dq_acc
            + jnp.einsum("hqnb,nhbd->hqd", ds_bf, k_slice, preferred_element_type=jnp.float32)
            * score_scale,
            None,
        )

    dq_glob, _ = lax.scan(
        dq_step, jnp.zeros((local_heads, glob_rows, HEAD_DIM), jnp.float32), slice_parts
    )
    own_scores = global_scores(q_glob, k_own, score_scale)
    probs_bf, ds_bf = global_grads(own_scores, log_norm, row_delta, g_glob, v_own)
    dk_glob = (
        jnp.einsum("hqnb,hqd->nhbd", ds_bf, q_glob, preferred_element_type=jnp.float32)
        * score_scale
    )
    dv_glob = jnp.einsum("hqnb,hqd->nhbd", probs_bf, g_glob, preferred_element_type=jnp.float32)
    glob_extra = jnp.stack([dk_glob, dv_glob], axis=1)
    final_kv = (summed + glob_extra).astype(jnp.bfloat16)
    dq_rows = token_major(dq_regular)
    glob_dq_rows = (
        jnp.transpose(dq_glob, (1, 0, 2)).reshape(glob_rows, feat_width).astype(jnp.bfloat16)
    )
    head_rows = jnp.where(ctx_id == 0, glob_dq_rows, dq_rows[:glob_rows])
    dq_final = jnp.concatenate([head_rows, dq_rows[glob_rows:]], axis=0)
    dk_final = token_major(final_kv[:, 0])
    dv_final = token_major(final_kv[:, 1])
    return (
        lax.all_to_all(dq_final, "head", split_axis=0, concat_axis=1, tiled=True),
        lax.all_to_all(dk_final, "head", split_axis=0, concat_axis=1, tiled=True),
        lax.all_to_all(dv_final, "head", split_axis=0, concat_axis=1, tiled=True),
    )


def dot_nn(left, right):
    return lax.dot_general(left, right, (((1,), (0,)), ((), ())), preferred_element_type=jnp.float32)


def dot_nt(left, right):
    return lax.dot_general(left, right, (((1,), (1,)), ((), ())), preferred_element_type=jnp.float32)


def name_edges(range_blocks, owner_ref, local_ref, named_ref, bias_ref):
    randoms, blocks = owner_ref.shape

    def name_step(block_id, carry):
        earlier = []
        for nth in range(randoms):
            named = owner_ref[nth, block_id] * range_blocks + local_ref[nth, block_id]
            fresh = (named >= GLOBALS) & ((named < block_id - 1) | (named > block_id + 1))
            for before in earlier:
                fresh = fresh & (named != before)
            earlier.append(named)
            edge = block_id * randoms + nth
            named_ref[edge] = named
            bias_ref[edge] = jnp.where(fresh, 0.0, -NEG_BIG).astype(jnp.float32)
        return carry

    lax.fori_loop(0, blocks, name_step, 0)


def link_edges(range_blocks, owner, local, width):
    randoms, blocks = owner.shape
    named = owner * range_blocks + local
    row_id = lax.broadcasted_iota(jnp.int32, (blocks, blocks), 0)
    column_id = lax.broadcasted_iota(jnp.int32, (blocks, blocks), 1)
    across = [jnp.broadcast_to(named[nth : nth + 1], (blocks, blocks)) for nth in range(randoms)]

    def latest(wanted, before):
        found = jnp.full((blocks, blocks), -1, jnp.int32)
        for nth in range(randoms):
            hit = (across[nth] == wanted) & (column_id >= GLOBALS) & (column_id < before)
            found = jnp.maximum(found, jnp.where(hit, column_id * randoms + nth, -1))
        return jnp.max(found, axis=1, keepdims=True)

    columns = []
    for nth in range(randoms):
        down = jnp.sum(jnp.where(row_id == column_id, across[nth], 0), axis=1, keepdims=True)
        columns.append(latest(down, row_id))
    columns.append(latest(row_id, blocks))
    slot = lax.broadcasted_iota(jnp.int32, (blocks, width), 1)
    table = jnp.full((blocks, width), -1, jnp.int32)
    for nth, column in enumerate(columns):
        table = jnp.where(slot == nth, column, table)
    return table


def head_kernel(ctx_size, heads_axis, owner_in, local_in, k_in, v_in, q_in, g_in,
                dq_out, dk_out, dv_out, owner_ref, local_ref, owner_rows, local_rows,
                named_ref, bias_ref, links_ref, table_ref, kv_ref, qg_ref, grads_ref, acc_ref, edge_ref, kt_ref, pair_ref, s_ref, dp_ref,
                send_sem, recv_sem, own_sem, table_sem, index_sem):
    blocks, randoms = kv_ref.shape[0], edge_ref.shape[0] // kv_ref.shape[0]
    devices = ctx_size * heads_axis
    score_scale = 1.0 / math.sqrt(HEAD_DIM)
    exp_scale = score_scale * math.log2(math.e)
    glob_rows = GLOBALS * BLOCK_LEN
    group = 4
    chunk = group * BLOCK_LEN
    chunks = blocks // group
    bf16 = jnp.bfloat16
    ctx_id, head_id = lax.axis_index("ctx"), lax.axis_index("head")
    me = ctx_id * heads_axis + head_id
    ins = (k_in, v_in, q_in, g_in)
    landing = (kv_ref, kv_ref, qg_ref, qg_ref)
    outs = (dq_out, dk_out, dv_out)

    def head_columns(block_id):
        return pl.ds(pl.multiple_of(block_id * HEAD_DIM, HEAD_DIM), HEAD_DIM)

    inner = (ctx_id > 0) & (ctx_id < ctx_size - 1)
    near = (1, 0)
    far = (jnp.where(inner, 3, 2), jnp.where(inner, 2, 3))

    def peer_at(ctx_off, head_off):
        return ctx_id ^ ctx_off, head_id ^ head_off, ctx_off * heads_axis + head_off

    def ends(which, peer):
        if which < 4:
            half = (which % 2) * HEAD_DIM
            return (
                ins[which].at[:, head_columns(peer)],
                landing[which].at[me, :, half : half + HEAD_DIM],
            )
        return (
            grads_ref.at[which - 4, peer],
            outs[which - 4].at[:, head_columns(me)],
        )

    def remote(which, peer_ctx, peer_head, offset):
        src, dst = ends(which, peer_ctx * heads_axis + peer_head)
        return pltpu.make_async_remote_copy(
            src_ref=src,
            dst_ref=dst,
            send_sem=send_sem.at[which, offset],
            recv_sem=recv_sem.at[which, offset],
            device_id=(peer_ctx, peer_head),
            device_id_type=MESH,
        )

    def own(which):
        src, dst = ends(which, me)
        return pltpu.make_async_copy(src, dst, own_sem.at[which])

    def over_peers(ctx_offs, action, first=0, until=heads_axis):
        def one(head_off, carry):
            for ctx_off in ctx_offs:
                if isinstance(ctx_off, int) and ctx_off == 0:

                    @pl.when(head_off > 0)
                    def _():
                        action(*peer_at(ctx_off, head_off))

                else:
                    action(*peer_at(ctx_off, head_off))
            return carry

        lax.fori_loop(first, until, one, 0)

    def start_all(ctx_offs, *names):
        def action(*peer):
            for which in names:
                remote(which, *peer).start()

        over_peers(ctx_offs, action)

    barrier = pltpu.get_barrier_semaphore()

    def greet(peer_ctx, peer_head, offset):
        pl.semaphore_signal(barrier, inc=1, device_id=(peer_ctx, peer_head), device_id_type=MESH)

    over_peers(far + near, greet)
    pl.semaphore_wait(barrier, devices - 1)
    start_all(far + near, 0)
    start_all(far + near, 1)
    start_all(far + near, 2, 3)

    for which in range(4):
        own(which).start()
    index_copies = [
        pltpu.make_async_copy(src, dst, index_sem.at[nth])
        for nth, (src, dst) in enumerate(
            zip((owner_in, local_in) * 2, (owner_ref, local_ref, owner_rows, local_rows))
        )
    ]
    for copy in index_copies:
        copy.start()
    for copy in index_copies:
        copy.wait()
    table_ref[...] = link_edges(
        blocks // ctx_size, owner_rows[...], local_rows[...], table_ref.shape[1]
    )
    table_copy = pltpu.make_async_copy(table_ref, links_ref, table_sem)
    table_copy.start()
    name_edges(blocks // ctx_size, owner_ref, local_ref, named_ref, bias_ref)
    pair_ref[...] = jnp.zeros_like(pair_ref)
    acc_ref[...] = jnp.zeros_like(acc_ref)
    edge_ref[: GLOBALS * randoms] = jnp.zeros(
        (GLOBALS * randoms, BLOCK_LEN, 2 * HEAD_DIM), jnp.float32
    )
    for which in range(4):
        own(which).wait()
    table_copy.wait()

    def keys_arrived(*peer):
        remote(0, *peer).wait_recv()
        remote(1, *peer).wait_recv()

    over_peers(far + near, keys_arrived)

    def turn_step(block_id, carry):
        kt_ref[block_id] = kv_ref[block_id, :, :HEAD_DIM].T
        return carry

    lax.fori_loop(0, blocks, turn_step, 0, unroll=4)

    def attend(block_id):
        pair_ref[:BLOCK_LEN, :HEAD_DIM] = qg_ref[block_id, :, :HEAD_DIM]
        pair_ref[BLOCK_LEN:, HEAD_DIM:] = qg_ref[block_id, :, HEAD_DIM:]
        pair = pair_ref[...]
        ids = [block_id - 1, block_id, jnp.minimum(block_id + 1, blocks - 1)]
        bias = [
            jnp.where(block_id - 1 >= GLOBALS, 0.0, -NEG_BIG).astype(jnp.float32),
            0.0,
            jnp.where(block_id + 1 < blocks, 0.0, -NEG_BIG).astype(jnp.float32),
        ]
        ids += list(range(GLOBALS))
        bias += [0.0] * GLOBALS
        fixed = len(ids)
        for nth in range(randoms):
            ids.append(named_ref[block_id * randoms + nth])
            bias.append(bias_ref[block_id * randoms + nth])
        both = [dot_nt(kv_ref[key_id], pair) for key_id in ids]
        row_top = None
        for part, off in zip(both, bias):
            part_top = jnp.max(part[:, :BLOCK_LEN], axis=0, keepdims=True) - off
            row_top = part_top if row_top is None else jnp.maximum(row_top, part_top)
        top_scaled = row_top * exp_scale
        probs, row_total, row_dot = [], 0.0, 0.0
        for part, off in zip(both, bias):
            vals = jnp.exp2(part[:, :BLOCK_LEN] * exp_scale - (top_scaled + off))
            row_total += jnp.sum(vals, axis=0, keepdims=True)
            row_dot += jnp.sum(vals * part[:, BLOCK_LEN:], axis=0, keepdims=True)
            probs.append(vals)
        inverse = 1.0 / row_total
        row_delta = row_dot * inverse
        dq_acc = jnp.zeros((HEAD_DIM, BLOCK_LEN), jnp.float32)
        for nth, (part, vals, key_id) in enumerate(zip(both, probs, ids)):
            vals = vals * inverse
            ds_bf = (vals * (part[:, BLOCK_LEN:] - row_delta)).astype(bf16)
            left = jnp.concatenate([ds_bf, vals.astype(bf16)], axis=1)
            if nth < fixed:
                acc_ref[key_id] += dot_nn(left, pair)
            else:
                edge_ref[block_id * randoms + nth - fixed] = dot_nn(left, pair)
            if nth % 2 == 0:
                waiting, waiting_id = ds_bf, key_id
            else:
                dq_acc += dot_nn(
                    jnp.concatenate([kt_ref[waiting_id], kt_ref[key_id]], axis=1),
                    jnp.concatenate([waiting, ds_bf], axis=0),
                )
        if len(ids) % 2:
            dq_acc += dot_nn(kt_ref[waiting_id], waiting)
        grads_ref[0, block_id] = (dq_acc.T * score_scale).astype(bf16)

    def send_queries_grad(*peer):
        @pl.when(peer[0] * heads_axis + peer[1] >= GLOBALS)
        def _():
            remote(4, *peer).start()

    def handle(send, remote_block, *peer):
        block_id = peer[0] * heads_axis + peer[1]

        @pl.when(remote_block)
        def _():
            remote(2, *peer).wait_recv()
            remote(3, *peer).wait_recv()

        @pl.when(block_id >= GLOBALS)
        def _():
            attend(block_id)

            @pl.when(send & remote_block)
            def _():
                remote(4, *peer).start()

    def block_step(step, carry):
        group_id, head_off = step // heads_axis, step % heads_axis
        far_off = jnp.where(group_id == 2, far[0], far[1])
        ctx_off = jnp.where(group_id < 2, group_id, far_off)
        handle(group_id >= 0, step > 0, *peer_at(ctx_off, head_off))
        return carry

    lax.fori_loop(0, devices, block_step, 0)


    q_glob = qg_ref[:GLOBALS, :, :HEAD_DIM].reshape(glob_rows, HEAD_DIM)
    g_glob = qg_ref[:GLOBALS, :, HEAD_DIM:].reshape(glob_rows, HEAD_DIM)

    def keys_of(step, half):
        part = kv_ref[pl.ds(step * group, group), :, half * HEAD_DIM : (half + 1) * HEAD_DIM]
        return part.reshape(chunk, HEAD_DIM)

    def scores_step(step, row_top):
        rows = pl.ds(pl.multiple_of(step * chunk, chunk), chunk)
        scores = dot_nt(keys_of(step, 0), q_glob)
        s_ref[rows, :] = scores
        return jnp.maximum(row_top, jnp.max(scores, axis=0, keepdims=True))

    row_top = lax.fori_loop(
        0, chunks, scores_step, jnp.full((1, glob_rows), NEG_BIG, jnp.float32)
    )
    top_scaled = row_top * exp_scale

    def probs_step(step, sums):
        rows = pl.ds(pl.multiple_of(step * chunk, chunk), chunk)
        probs = jnp.exp2(s_ref[rows, :] * exp_scale - top_scaled)
        dprobs = dot_nt(keys_of(step, 1), g_glob)
        s_ref[rows, :] = probs
        dp_ref[rows, :] = dprobs
        return (
            sums[0] + jnp.sum(probs, axis=0, keepdims=True),
            sums[1] + jnp.sum(probs * dprobs, axis=0, keepdims=True),
        )

    zero_row = jnp.zeros((1, glob_rows), jnp.float32)
    row_total, row_dot = lax.fori_loop(0, chunks, probs_step, (zero_row, zero_row))
    inverse = 1.0 / row_total
    row_delta = row_dot * inverse

    def grads_step(step, dq_acc):
        rows = pl.ds(pl.multiple_of(step * chunk, chunk), chunk)
        probs = s_ref[rows, :] * inverse
        ds_bf = (probs * (dp_ref[rows, :] - row_delta)).astype(bf16)
        probs_bf = probs.astype(bf16)
        at = pl.ds(step * group, group)
        shape = (group, BLOCK_LEN, HEAD_DIM)
        acc_ref[at, :, :HEAD_DIM] += dot_nn(ds_bf, q_glob).reshape(shape)
        acc_ref[at, :, HEAD_DIM:] += dot_nn(probs_bf, g_glob).reshape(shape)
        for nth in range(group):
            dq_acc += dot_nn(
                kt_ref[step * group + nth], ds_bf[nth * BLOCK_LEN : (nth + 1) * BLOCK_LEN]
            )
        return dq_acc

    dq_glob = lax.fori_loop(
        0, chunks, grads_step, jnp.zeros((HEAD_DIM, glob_rows), jnp.float32)
    )
    dq_rows = (dq_glob.T * score_scale).astype(bf16)
    for block_id in range(GLOBALS):
        grads_ref[0, block_id] = dq_rows[block_id * BLOCK_LEN : (block_id + 1) * BLOCK_LEN]

        @pl.when(me != block_id)
        def _():
            remote(4, 0, block_id, ctx_id * heads_axis + (head_id ^ block_id)).start()

    own(4).start()

    def linked(block_id, slot):
        edge = links_ref[block_id, slot]
        weight = jnp.where(edge >= 0, 1.0, 0.0).astype(jnp.float32)
        return weight * edge_ref[jnp.maximum(edge, 0)]

    def chain_step(block_id, carry):
        for nth in range(randoms):
            edge_ref[block_id * randoms + nth] += linked(block_id, nth)
        return carry

    lax.fori_loop(GLOBALS, blocks, chain_step, 0)

    def finish(*peer):
        block_id = peer[0] * heads_axis + peer[1]
        total = acc_ref[block_id] + linked(block_id, randoms)
        grads_ref[1, block_id] = (total[:, :HEAD_DIM] * score_scale).astype(bf16)
        grads_ref[2, block_id] = total[:, HEAD_DIM:].astype(bf16)

    def finish_step(step, carry):
        head_off, turn = step // ctx_size, step % ctx_size
        ctx_off = jnp.where(turn == 0, far[0], jnp.where(turn == 1, far[1], ctx_size - 1 - turn))
        peer = peer_at(ctx_off, head_off)
        finish(*peer)

        @pl.when(step != ctx_size - 1)
        def _():
            remote(5, *peer).start()
            remote(6, *peer).start()

        return carry

    lax.fori_loop(0, devices, finish_step, 0)
    own(5).start()
    own(6).start()
    for which in range(4, 7):
        own(which).wait()

    def all_sent(*peer):
        for which in range(7):
            remote(which, *peer).wait_send()

    def all_here(*peer):
        for which in range(4, 7):
            remote(which, *peer).wait_recv()

    over_peers(far + near, all_sent)
    over_peers(near + far, all_here)


def copy_kernel(count, *refs):
    ins, outs, sems = refs[:count], refs[count : 2 * count], refs[2 * count]
    copies = [pltpu.make_async_copy(ins[nth], outs[nth], sems.at[nth]) for nth in range(count)]
    for copy in copies:
        copy.start()
    for copy in copies:
        copy.wait()


def one_head(queries, keys_in, values_in, out_grad, rand_owner, rand_local):
    ctx_size, heads_axis = lax.axis_size("ctx"), lax.axis_size("head")
    devices = ctx_size * heads_axis
    rows, feat_width = queries.shape
    tokens = rows * devices
    blocks, randoms = rand_owner.shape
    edges = blocks * randoms
    anywhere = pl.BlockSpec(memory_space=pl.ANY)
    vmem = pl.BlockSpec(memory_space=pltpu.VMEM)
    hbm = pl.BlockSpec(memory_space=pltpu.HBM)
    bf16 = jnp.bfloat16
    index_arrays = [pltpu.with_memory_space_constraint(index.T, pltpu.HBM) for index in (rand_owner, rand_local)]
    grads = pl.pallas_call(
        functools.partial(head_kernel, ctx_size, heads_axis),
        out_shape=[jax.ShapeDtypeStruct((rows, feat_width), bf16)] * 3,
        in_specs=[hbm] * 6,
        out_specs=[vmem] * 3,
        scratch_shapes=[
            pltpu.SMEM((randoms, blocks), jnp.int32),
            pltpu.SMEM((randoms, blocks), jnp.int32),
            pltpu.VMEM((randoms, blocks), jnp.int32),
            pltpu.VMEM((randoms, blocks), jnp.int32),
            pltpu.SMEM((edges,), jnp.int32),
            pltpu.SMEM((edges,), jnp.float32),
            pltpu.SMEM((blocks, 128), jnp.int32),
            pltpu.VMEM((blocks, 128), jnp.int32),
            pltpu.VMEM((blocks, BLOCK_LEN, 2 * HEAD_DIM), bf16),
            pltpu.VMEM((blocks, BLOCK_LEN, 2 * HEAD_DIM), bf16),
            pltpu.VMEM((3, blocks, BLOCK_LEN, HEAD_DIM), bf16),
            pltpu.VMEM((blocks, BLOCK_LEN, 2 * HEAD_DIM), jnp.float32),
            pltpu.VMEM((edges, BLOCK_LEN, 2 * HEAD_DIM), jnp.float32),
            pltpu.VMEM((blocks, HEAD_DIM, BLOCK_LEN), bf16),
            pltpu.VMEM((2 * BLOCK_LEN, 2 * HEAD_DIM), bf16),
            pltpu.VMEM((tokens, GLOBALS * BLOCK_LEN), jnp.float32),
            pltpu.VMEM((tokens, GLOBALS * BLOCK_LEN), jnp.float32),
            pltpu.SemaphoreType.DMA((7, devices)),
            pltpu.SemaphoreType.DMA((7, devices)),
            pltpu.SemaphoreType.DMA((7,)),
            pltpu.SemaphoreType.DMA,
            pltpu.SemaphoreType.DMA((4,)),
        ],
        compiler_params=pltpu.CompilerParams(
            collective_id=1, has_side_effects=True, vmem_limit_bytes=50 << 20
        ),
    )(*index_arrays, keys_in, values_in, queries, out_grad)
    return tuple(
        pl.pallas_call(
            functools.partial(copy_kernel, 3),
            out_shape=[jax.ShapeDtypeStruct((rows, feat_width), bf16)] * 3,
            in_specs=[vmem] * 3,
            out_specs=[anywhere] * 3,
            scratch_shapes=[pltpu.SemaphoreType.DMA((3,))],
            compiler_params=pltpu.CompilerParams(vmem_limit_bytes=4 << 20),
        )(*grads)
    )


def per_device(*args):
    devices = lax.axis_size(("ctx", "head"))
    rows, feat_width = args[0].shape
    fits = feat_width == devices * HEAD_DIM and rows == BLOCK_LEN and lax.axis_size("ctx") == 4
    return one_head(*args) if fits else split_heads(*args)


def solution(mesh):
    return jax.shard_map(
        per_device,
        mesh=mesh,
        in_specs=(
            P(("ctx", "head"), None),
            P(("ctx", "head"), None),
            P(("ctx", "head"), None),
            P(("ctx", "head"), None),
            P(),
            P(),
        ),
        out_specs=(P(("ctx", "head"), None), P(("ctx", "head"), None), P(("ctx", "head"), None)),
        check_vma=False,
    )
```

```python
import functools
import math

import jax
import jax.numpy as jnp
from jax import lax
from jax.experimental import pallas as pl
from jax.experimental.pallas import tpu as pltpu
from jax.sharding import PartitionSpec as P

MESH = pl.DeviceIdType.MESH

HEAD_DIM = 128
BLOCK_LEN = 128
GLOBALS = 2


NEG_BIG = -1e30


def broadcast(block, axis, holder):
    block = jnp.where(lax.axis_index(axis) == holder, block, jnp.zeros_like(block))
    return lax.psum(block, axis)


def entry_blocks(rand_owner, rand_local, range_blocks, glob_count, total_blocks):
    block_ids = jnp.arange(total_blocks, dtype=jnp.int32)
    fixed_cols = [block_ids - 1, block_ids, block_ids + 1]
    fixed_cols = fixed_cols + [
        jnp.full((total_blocks,), glob_id, jnp.int32) for glob_id in range(glob_count)
    ]
    listed = jnp.concatenate(
        [jnp.stack(fixed_cols, axis=1), rand_owner * range_blocks + rand_local], axis=1
    )
    inside = (listed >= 0) & (listed < total_blocks)
    entry_count = listed.shape[1]
    equal_pair = (listed[:, :, None] == listed[:, None, :]) & inside[:, None, :]
    earlier = jnp.tril(jnp.ones((entry_count, entry_count), jnp.int32), -1) > 0
    repeated = jnp.any(equal_pair & earlier[None, :, :], axis=2)
    usable = inside & jnp.logical_not(repeated) & (block_ids >= glob_count)[:, None]
    return (jnp.clip(listed, 0, total_blocks - 1), usable)


def head_major(rows_arr, block_len, head_dim):
    row_count, feat_width = rows_arr.shape
    shaped = rows_arr.reshape(row_count // block_len, block_len, feat_width // head_dim, head_dim)
    return jnp.transpose(shaped, (0, 2, 1, 3))


def token_major(blocks_arr):
    block_count, heads, block_len, head_dim = blocks_arr.shape
    return jnp.transpose(blocks_arr, (0, 2, 1, 3)).reshape(
        block_count * block_len, heads * head_dim
    )


def regular_part(q_blocks, g_blocks, key_pool, pool_index, usable, score_scale):
    range_blocks, local_heads, block_len, head_dim = q_blocks.shape
    entry_count = pool_index.shape[1]
    group_size = math.gcd(range_blocks, max(1, 512 // block_len))
    group_count = range_blocks // group_size

    def split_groups(tensor):
        return tensor.reshape((group_count, group_size) + tensor.shape[1:])

    def group_step(grad_acc, inputs):
        q_tile, g_tile, index_group, usable_group = inputs
        kv_tile = jnp.stack(
            [
                lax.dynamic_index_in_dim(key_pool, index_group[row, col], 0, keepdims=False)
                for row in range(group_size)
                for col in range(entry_count)
            ]
        ).reshape(index_group.shape + key_pool.shape[1:])
        k_tile = kv_tile[:, :, 0]
        v_tile = kv_tile[:, :, 1]
        key_mask = usable_group[:, None, None, :, None]
        scores = (
            jnp.einsum("ghqd,gehkd->ghqek", q_tile, k_tile, preferred_element_type=jnp.float32)
            * score_scale
        )
        scores = jnp.where(key_mask, scores, NEG_BIG)
        row_top = jnp.max(scores, axis=(3, 4), keepdims=True)
        row_total = jnp.sum(
            jnp.where(key_mask, jnp.exp(scores - row_top), 0.0), axis=(3, 4), keepdims=True
        )
        log_norm = row_top + jnp.log(jnp.where(row_total > 0, row_total, 1.0))
        prob_vals = jnp.where(key_mask, jnp.exp(scores - log_norm), 0.0)
        probs_bf = prob_vals.astype(jnp.bfloat16)
        attended = jnp.einsum(
            "ghqek,gehkd->ghqd", probs_bf, v_tile, preferred_element_type=jnp.float32
        )
        row_delta = jnp.sum(g_tile.astype(jnp.float32) * attended, axis=3)
        dprobs = jnp.einsum("ghqd,gehkd->ghqek", g_tile, v_tile, preferred_element_type=jnp.float32)
        dscores = prob_vals * (dprobs - row_delta[:, :, :, None, None])
        ds_bf = dscores.astype(jnp.bfloat16)
        dq_tile = (
            jnp.einsum("ghqek,gehkd->ghqd", ds_bf, k_tile, preferred_element_type=jnp.float32)
            * score_scale
        ).astype(jnp.bfloat16)
        dk_tile = (
            jnp.einsum("ghqek,ghqd->gehkd", ds_bf, q_tile, preferred_element_type=jnp.float32)
            * score_scale
        )
        dv_tile = jnp.einsum(
            "ghqek,ghqd->gehkd", probs_bf, g_tile, preferred_element_type=jnp.float32
        )
        grads = jnp.stack([dk_tile, dv_tile], axis=2)
        grads = grads.reshape((group_size * entry_count,) + grads.shape[2:])
        grad_acc = grad_acc.at[index_group.reshape(-1)].add(grads)
        return (grad_acc, dq_tile)

    zero_acc = jnp.zeros(key_pool.shape, jnp.float32)
    inputs = (
        split_groups(q_blocks),
        split_groups(g_blocks),
        split_groups(pool_index),
        split_groups(usable),
    )
    grad_acc, dq_groups = lax.scan(group_step, zero_acc, inputs)
    return (grad_acc, dq_groups.reshape(q_blocks.shape))


def global_scores(q_glob, k_slice, score_scale):
    return (
        jnp.einsum("hqd,nhbd->hqnb", q_glob, k_slice, preferred_element_type=jnp.float32)
        * score_scale
    )


def global_grads(scores, log_norm, row_delta, g_glob, v_slice):
    prob_vals = jnp.exp(scores - log_norm[:, :, None, None])
    probs_bf = prob_vals.astype(jnp.bfloat16)
    dprobs = jnp.einsum("hqd,nhbd->hqnb", g_glob, v_slice, preferred_element_type=jnp.float32)
    ds_bf = (prob_vals * (dprobs - row_delta[:, :, None, None])).astype(jnp.bfloat16)
    return (probs_bf, ds_bf)


def split_heads(queries, keys_in, values_in, out_grad, rand_owner, rand_local):
    q_local, k_local, v_local, g_local = (
        lax.all_to_all(queries, "head", split_axis=1, concat_axis=0, tiled=True),
        lax.all_to_all(keys_in, "head", split_axis=1, concat_axis=0, tiled=True),
        lax.all_to_all(values_in, "head", split_axis=1, concat_axis=0, tiled=True),
        lax.all_to_all(out_grad, "head", split_axis=1, concat_axis=0, tiled=True),
    )
    n_ctx = lax.axis_size("ctx")
    ctx_id = lax.axis_index("ctx")
    local_rows, feat_width = q_local.shape
    range_blocks = local_rows // BLOCK_LEN
    local_heads = feat_width // HEAD_DIM
    total_blocks = range_blocks * n_ctx
    glob_rows = GLOBALS * BLOCK_LEN
    score_scale = 1.0 / math.sqrt(HEAD_DIM)
    q_blocks = head_major(q_local, BLOCK_LEN, HEAD_DIM)
    g_blocks = head_major(g_local, BLOCK_LEN, HEAD_DIM)
    kv_local = jnp.stack(
        [head_major(k_local, BLOCK_LEN, HEAD_DIM), head_major(v_local, BLOCK_LEN, HEAD_DIM)], axis=1
    )
    pool_tail = (2, local_heads, BLOCK_LEN, HEAD_DIM)
    listed, usable = entry_blocks(rand_owner, rand_local, range_blocks, GLOBALS, total_blocks)
    my_listed = lax.dynamic_slice_in_dim(listed, ctx_id * range_blocks, range_blocks, 0)
    my_usable = lax.dynamic_slice_in_dim(usable, ctx_id * range_blocks, range_blocks, 0)
    key_pool = lax.all_gather(kv_local, "ctx", axis=0, tiled=True)
    grad_acc, dq_regular = regular_part(
        q_blocks, g_blocks, key_pool, my_listed, my_usable, score_scale
    )
    summed = lax.psum_scatter(
        grad_acc.astype(jnp.bfloat16), "ctx", scatter_dimension=0, tiled=True
    ).astype(jnp.float32)
    q_shared, g_shared = (
        broadcast(q_blocks[:GLOBALS], "ctx", 0),
        broadcast(g_blocks[:GLOBALS], "ctx", 0),
    )
    q_glob = jnp.transpose(q_shared, (1, 0, 2, 3)).reshape(local_heads, glob_rows, HEAD_DIM)
    g_glob = jnp.transpose(g_shared, (1, 0, 2, 3)).reshape(local_heads, glob_rows, HEAD_DIM)
    k_own = kv_local[:, 0]
    v_own = kv_local[:, 1]
    slice_parts = key_pool.reshape((n_ctx, range_blocks) + pool_tail)

    def stats_step(stats_carry, slice_part):
        row_top, row_total = stats_carry
        scores = global_scores(q_glob, slice_part[:, 0], score_scale)
        new_top = jnp.maximum(row_top, jnp.max(scores, axis=(2, 3)))
        row_total = row_total * jnp.exp(row_top - new_top) + jnp.sum(
            jnp.exp(scores - new_top[:, :, None, None]), axis=(2, 3)
        )
        return ((new_top, row_total), None)

    start_stats = (
        jnp.full((local_heads, glob_rows), NEG_BIG, jnp.float32),
        jnp.zeros((local_heads, glob_rows), jnp.float32),
    )
    (row_top, row_total), _ = lax.scan(stats_step, start_stats, slice_parts)
    log_norm = row_top + jnp.log(row_total)

    def out_step(attended, slice_part):
        scores = global_scores(q_glob, slice_part[:, 0], score_scale)
        probs_bf = jnp.exp(scores - log_norm[:, :, None, None]).astype(jnp.bfloat16)
        return (
            attended
            + jnp.einsum(
                "hqnb,nhbd->hqd", probs_bf, slice_part[:, 1], preferred_element_type=jnp.float32
            ),
            None,
        )

    attended, _ = lax.scan(
        out_step, jnp.zeros((local_heads, glob_rows, HEAD_DIM), jnp.float32), slice_parts
    )
    row_delta = jnp.sum(g_glob.astype(jnp.float32) * attended, axis=2)

    def dq_step(dq_acc, slice_part):
        k_slice = slice_part[:, 0]
        scores = global_scores(q_glob, k_slice, score_scale)
        probs_bf, ds_bf = global_grads(scores, log_norm, row_delta, g_glob, slice_part[:, 1])
        return (
            dq_acc
            + jnp.einsum("hqnb,nhbd->hqd", ds_bf, k_slice, preferred_element_type=jnp.float32)
            * score_scale,
            None,
        )

    dq_glob, _ = lax.scan(
        dq_step, jnp.zeros((local_heads, glob_rows, HEAD_DIM), jnp.float32), slice_parts
    )
    own_scores = global_scores(q_glob, k_own, score_scale)
    probs_bf, ds_bf = global_grads(own_scores, log_norm, row_delta, g_glob, v_own)
    dk_glob = (
        jnp.einsum("hqnb,hqd->nhbd", ds_bf, q_glob, preferred_element_type=jnp.float32)
        * score_scale
    )
    dv_glob = jnp.einsum("hqnb,hqd->nhbd", probs_bf, g_glob, preferred_element_type=jnp.float32)
    glob_extra = jnp.stack([dk_glob, dv_glob], axis=1)
    final_kv = (summed + glob_extra).astype(jnp.bfloat16)
    dq_rows = token_major(dq_regular)
    glob_dq_rows = (
        jnp.transpose(dq_glob, (1, 0, 2)).reshape(glob_rows, feat_width).astype(jnp.bfloat16)
    )
    head_rows = jnp.where(ctx_id == 0, glob_dq_rows, dq_rows[:glob_rows])
    dq_final = jnp.concatenate([head_rows, dq_rows[glob_rows:]], axis=0)
    dk_final = token_major(final_kv[:, 0])
    dv_final = token_major(final_kv[:, 1])
    return (
        lax.all_to_all(dq_final, "head", split_axis=0, concat_axis=1, tiled=True),
        lax.all_to_all(dk_final, "head", split_axis=0, concat_axis=1, tiled=True),
        lax.all_to_all(dv_final, "head", split_axis=0, concat_axis=1, tiled=True),
    )


def dot_nn(left, right):
    return lax.dot_general(left, right, (((1,), (0,)), ((), ())), preferred_element_type=jnp.float32)


def dot_nt(left, right):
    return lax.dot_general(left, right, (((1,), (1,)), ((), ())), preferred_element_type=jnp.float32)


def name_edges(range_blocks, owner_ref, local_ref, named_ref, bias_ref):
    randoms, blocks = owner_ref.shape

    def name_step(block_id, carry):
        earlier = []
        for nth in range(randoms):
            named = owner_ref[nth, block_id] * range_blocks + local_ref[nth, block_id]
            fresh = (named >= GLOBALS) & ((named < block_id - 1) | (named > block_id + 1))
            for before in earlier:
                fresh = fresh & (named != before)
            earlier.append(named)
            edge = block_id * randoms + nth
            named_ref[edge] = named
            bias_ref[edge] = jnp.where(fresh, 0.0, -NEG_BIG).astype(jnp.float32)
        return carry

    lax.fori_loop(0, blocks, name_step, 0)


def link_edges(range_blocks, owner, local, width):
    randoms, blocks = owner.shape
    named = owner * range_blocks + local
    row_id = lax.broadcasted_iota(jnp.int32, (blocks, blocks), 0)
    column_id = lax.broadcasted_iota(jnp.int32, (blocks, blocks), 1)
    across = [jnp.broadcast_to(named[nth : nth + 1], (blocks, blocks)) for nth in range(randoms)]

    def latest(wanted, before):
        found = jnp.full((blocks, blocks), -1, jnp.int32)
        for nth in range(randoms):
            hit = (across[nth] == wanted) & (column_id >= GLOBALS) & (column_id < before)
            found = jnp.maximum(found, jnp.where(hit, column_id * randoms + nth, -1))
        return jnp.max(found, axis=1, keepdims=True)

    columns = []
    for nth in range(randoms):
        down = jnp.sum(jnp.where(row_id == column_id, across[nth], 0), axis=1, keepdims=True)
        columns.append(latest(down, row_id))
    columns.append(latest(row_id, blocks))
    slot = lax.broadcasted_iota(jnp.int32, (blocks, width), 1)
    table = jnp.full((blocks, width), -1, jnp.int32)
    for nth, column in enumerate(columns):
        table = jnp.where(slot == nth, column, table)
    return table


def head_kernel(ctx_size, heads_axis, owner_in, local_in, k_in, v_in, q_in, g_in,
                dq_out, dk_out, dv_out, owner_ref, local_ref, owner_rows, local_rows,
                named_ref, bias_ref, links_ref, table_ref, kv_ref, qg_ref, grads_ref, acc_ref, edge_ref, kt_ref, pair_ref, s_ref, dp_ref,
                send_sem, recv_sem, own_sem, table_sem, index_sem):
    blocks, randoms = kv_ref.shape[0], edge_ref.shape[0] // kv_ref.shape[0]
    devices = ctx_size * heads_axis
    score_scale = 1.0 / math.sqrt(HEAD_DIM)
    exp_scale = score_scale * math.log2(math.e)
    glob_rows = GLOBALS * BLOCK_LEN
    group = 4
    chunk = group * BLOCK_LEN
    chunks = blocks // group
    bf16 = jnp.bfloat16
    ctx_id, head_id = lax.axis_index("ctx"), lax.axis_index("head")
    me = ctx_id * heads_axis + head_id
    ins = (k_in, v_in, q_in, g_in)
    landing = (kv_ref, kv_ref, qg_ref, qg_ref)
    outs = (dq_out, dk_out, dv_out)

    def head_columns(block_id):
        return pl.ds(pl.multiple_of(block_id * HEAD_DIM, HEAD_DIM), HEAD_DIM)

    inner = (ctx_id > 0) & (ctx_id < ctx_size - 1)
    near = (1, 0)
    far = (jnp.where(inner, 3, 2), jnp.where(inner, 2, 3))

    def peer_at(ctx_off, head_off):
        return ctx_id ^ ctx_off, head_id ^ head_off, ctx_off * heads_axis + head_off

    def ends(which, peer):
        if which < 4:
            half = (which % 2) * HEAD_DIM
            return (
                ins[which].at[:, head_columns(peer)],
                landing[which].at[me, :, half : half + HEAD_DIM],
            )
        return (
            grads_ref.at[which - 4, peer],
            outs[which - 4].at[:, head_columns(me)],
        )

    def remote(which, peer_ctx, peer_head, offset):
        src, dst = ends(which, peer_ctx * heads_axis + peer_head)
        return pltpu.make_async_remote_copy(
            src_ref=src,
            dst_ref=dst,
            send_sem=send_sem.at[which, offset],
            recv_sem=recv_sem.at[which, offset],
            device_id=(peer_ctx, peer_head),
            device_id_type=MESH,
        )

    def own(which):
        src, dst = ends(which, me)
        return pltpu.make_async_copy(src, dst, own_sem.at[which])

    def over_peers(ctx_offs, action, first=0, until=heads_axis):
        def one(turn, carry):
            head_off = turn ^ (ctx_id % 2)
            for ctx_off in ctx_offs:
                if isinstance(ctx_off, int) and ctx_off == 0:

                    @pl.when(head_off > 0)
                    def _():
                        action(*peer_at(ctx_off, head_off))

                else:
                    action(*peer_at(ctx_off, head_off))
            return carry

        lax.fori_loop(first, until, one, 0)

    def start_all(ctx_offs, *names):
        def action(*peer):
            for which in names:
                remote(which, *peer).start()

        over_peers(ctx_offs, action)

    barrier = pltpu.get_barrier_semaphore()

    def greet(peer_ctx, peer_head, offset):
        pl.semaphore_signal(barrier, inc=1, device_id=(peer_ctx, peer_head), device_id_type=MESH)

    over_peers(far + near, greet)
    pl.semaphore_wait(barrier, devices - 1)
    start_all(far + near, 0)
    start_all(far + near, 1)
    start_all(far + near, 2, 3)

    for which in range(4):
        own(which).start()
    index_copies = [
        pltpu.make_async_copy(src, dst, index_sem.at[nth])
        for nth, (src, dst) in enumerate(
            zip((owner_in, local_in) * 2, (owner_ref, local_ref, owner_rows, local_rows))
        )
    ]
    for copy in index_copies:
        copy.start()
    for copy in index_copies:
        copy.wait()
    table_ref[...] = link_edges(
        blocks // ctx_size, owner_rows[...], local_rows[...], table_ref.shape[1]
    )
    table_copy = pltpu.make_async_copy(table_ref, links_ref, table_sem)
    table_copy.start()
    name_edges(blocks // ctx_size, owner_ref, local_ref, named_ref, bias_ref)
    pair_ref[...] = jnp.zeros_like(pair_ref)
    acc_ref[...] = jnp.zeros_like(acc_ref)
    edge_ref[: GLOBALS * randoms] = jnp.zeros(
        (GLOBALS * randoms, BLOCK_LEN, 2 * HEAD_DIM), jnp.float32
    )
    for which in range(4):
        own(which).wait()
    table_copy.wait()

    def keys_arrived(*peer):
        remote(0, *peer).wait_recv()
        remote(1, *peer).wait_recv()

    over_peers(far + near, keys_arrived)

    def turn_step(block_id, carry):
        kt_ref[block_id] = kv_ref[block_id, :, :HEAD_DIM].T
        return carry

    lax.fori_loop(0, blocks, turn_step, 0, unroll=4)

    def attend(block_id):
        pair_ref[:BLOCK_LEN, :HEAD_DIM] = qg_ref[block_id, :, :HEAD_DIM]
        pair_ref[BLOCK_LEN:, HEAD_DIM:] = qg_ref[block_id, :, HEAD_DIM:]
        pair = pair_ref[...]
        ids = [block_id - 1, block_id, jnp.minimum(block_id + 1, blocks - 1)]
        bias = [
            jnp.where(block_id - 1 >= GLOBALS, 0.0, -NEG_BIG).astype(jnp.float32),
            0.0,
            jnp.where(block_id + 1 < blocks, 0.0, -NEG_BIG).astype(jnp.float32),
        ]
        ids += list(range(GLOBALS))
        bias += [0.0] * GLOBALS
        fixed = len(ids)
        for nth in range(randoms):
            ids.append(named_ref[block_id * randoms + nth])
            bias.append(bias_ref[block_id * randoms + nth])
        both = [dot_nt(kv_ref[key_id], pair) for key_id in ids]
        row_top = None
        for part, off in zip(both, bias):
            part_top = jnp.max(part[:, :BLOCK_LEN], axis=0, keepdims=True) - off
            row_top = part_top if row_top is None else jnp.maximum(row_top, part_top)
        top_scaled = row_top * exp_scale
        probs, row_total, row_dot = [], 0.0, 0.0
        for part, off in zip(both, bias):
            vals = jnp.exp2(part[:, :BLOCK_LEN] * exp_scale - (top_scaled + off))
            row_total += jnp.sum(vals, axis=0, keepdims=True)
            row_dot += jnp.sum(vals * part[:, BLOCK_LEN:], axis=0, keepdims=True)
            probs.append(vals)
        inverse = 1.0 / row_total
        row_delta = row_dot * inverse
        dq_acc = jnp.zeros((HEAD_DIM, BLOCK_LEN), jnp.float32)
        for nth, (part, vals, key_id) in enumerate(zip(both, probs, ids)):
            vals = vals * inverse
            ds_bf = (vals * (part[:, BLOCK_LEN:] - row_delta)).astype(bf16)
            left = jnp.concatenate([ds_bf, vals.astype(bf16)], axis=1)
            if nth < fixed:
                acc_ref[key_id] += dot_nn(left, pair)
            else:
                edge_ref[block_id * randoms + nth - fixed] = dot_nn(left, pair)
            if nth % 2 == 0:
                waiting, waiting_id = ds_bf, key_id
            else:
                dq_acc += dot_nn(
                    jnp.concatenate([kt_ref[waiting_id], kt_ref[key_id]], axis=1),
                    jnp.concatenate([waiting, ds_bf], axis=0),
                )
        if len(ids) % 2:
            dq_acc += dot_nn(kt_ref[waiting_id], waiting)
        grads_ref[0, block_id] = (dq_acc.T * score_scale).astype(bf16)

    def send_queries_grad(*peer):
        @pl.when(peer[0] * heads_axis + peer[1] >= GLOBALS)
        def _():
            remote(4, *peer).start()

    def handle(send, remote_block, *peer):
        block_id = peer[0] * heads_axis + peer[1]

        @pl.when(remote_block)
        def _():
            remote(2, *peer).wait_recv()
            remote(3, *peer).wait_recv()

        @pl.when(block_id >= GLOBALS)
        def _():
            attend(block_id)

            @pl.when(send & remote_block)
            def _():
                remote(4, *peer).start()

    def block_step(step, carry):
        group_id, head_off = step // heads_axis, step % heads_axis
        far_off = jnp.where(group_id == 2, far[0], far[1])
        ctx_off = jnp.where(group_id < 2, group_id, far_off)
        handle(group_id >= 0, step > 0, *peer_at(ctx_off, head_off))
        return carry

    lax.fori_loop(0, devices, block_step, 0)


    q_glob = qg_ref[:GLOBALS, :, :HEAD_DIM].reshape(glob_rows, HEAD_DIM)
    g_glob = qg_ref[:GLOBALS, :, HEAD_DIM:].reshape(glob_rows, HEAD_DIM)

    def keys_of(step, half):
        part = kv_ref[pl.ds(step * group, group), :, half * HEAD_DIM : (half + 1) * HEAD_DIM]
        return part.reshape(chunk, HEAD_DIM)

    def scores_step(step, row_top):
        rows = pl.ds(pl.multiple_of(step * chunk, chunk), chunk)
        scores = dot_nt(keys_of(step, 0), q_glob)
        s_ref[rows, :] = scores
        return jnp.maximum(row_top, jnp.max(scores, axis=0, keepdims=True))

    row_top = lax.fori_loop(
        0, chunks, scores_step, jnp.full((1, glob_rows), NEG_BIG, jnp.float32)
    )
    top_scaled = row_top * exp_scale

    def probs_step(step, sums):
        rows = pl.ds(pl.multiple_of(step * chunk, chunk), chunk)
        probs = jnp.exp2(s_ref[rows, :] * exp_scale - top_scaled)
        dprobs = dot_nt(keys_of(step, 1), g_glob)
        s_ref[rows, :] = probs
        dp_ref[rows, :] = dprobs
        return (
            sums[0] + jnp.sum(probs, axis=0, keepdims=True),
            sums[1] + jnp.sum(probs * dprobs, axis=0, keepdims=True),
        )

    zero_row = jnp.zeros((1, glob_rows), jnp.float32)
    row_total, row_dot = lax.fori_loop(0, chunks, probs_step, (zero_row, zero_row))
    inverse = 1.0 / row_total
    row_delta = row_dot * inverse

    def grads_step(step, dq_acc):
        rows = pl.ds(pl.multiple_of(step * chunk, chunk), chunk)
        probs = s_ref[rows, :] * inverse
        ds_bf = (probs * (dp_ref[rows, :] - row_delta)).astype(bf16)
        probs_bf = probs.astype(bf16)
        at = pl.ds(step * group, group)
        shape = (group, BLOCK_LEN, HEAD_DIM)
        acc_ref[at, :, :HEAD_DIM] += dot_nn(ds_bf, q_glob).reshape(shape)
        acc_ref[at, :, HEAD_DIM:] += dot_nn(probs_bf, g_glob).reshape(shape)
        for nth in range(group):
            dq_acc += dot_nn(
                kt_ref[step * group + nth], ds_bf[nth * BLOCK_LEN : (nth + 1) * BLOCK_LEN]
            )
        return dq_acc

    dq_glob = lax.fori_loop(
        0, chunks, grads_step, jnp.zeros((HEAD_DIM, glob_rows), jnp.float32)
    )
    dq_rows = (dq_glob.T * score_scale).astype(bf16)
    for block_id in range(GLOBALS):
        grads_ref[0, block_id] = dq_rows[block_id * BLOCK_LEN : (block_id + 1) * BLOCK_LEN]

        @pl.when(me != block_id)
        def _():
            remote(4, 0, block_id, ctx_id * heads_axis + (head_id ^ block_id)).start()

    own(4).start()

    def linked(block_id, slot):
        edge = links_ref[block_id, slot]
        weight = jnp.where(edge >= 0, 1.0, 0.0).astype(jnp.float32)
        return weight * edge_ref[jnp.maximum(edge, 0)]

    def chain_step(block_id, carry):
        for nth in range(randoms):
            edge_ref[block_id * randoms + nth] += linked(block_id, nth)
        return carry

    lax.fori_loop(GLOBALS, blocks, chain_step, 0)

    def finish(*peer):
        block_id = peer[0] * heads_axis + peer[1]
        total = acc_ref[block_id] + linked(block_id, randoms)
        grads_ref[1, block_id] = (total[:, :HEAD_DIM] * score_scale).astype(bf16)
        grads_ref[2, block_id] = total[:, HEAD_DIM:].astype(bf16)

    def finish_step(step, carry):
        head_off, turn = step // ctx_size, step % ctx_size
        ctx_off = jnp.where(turn == 0, far[1], jnp.where(turn == 1, far[0], ctx_size - 1 - turn))
        peer = peer_at(ctx_off, head_off)
        finish(*peer)

        @pl.when(step != ctx_size - 1)
        def _():
            remote(5, *peer).start()
            remote(6, *peer).start()

        return carry

    lax.fori_loop(0, devices, finish_step, 0)
    own(5).start()
    own(6).start()
    for which in range(4, 7):
        own(which).wait()

    def all_sent(*peer):
        for which in range(7):
            remote(which, *peer).wait_send()

    def all_here(*peer):
        for which in range(4, 7):
            remote(which, *peer).wait_recv()

    over_peers(far + near, all_sent)
    over_peers(near + far, all_here)


def copy_kernel(count, *refs):
    ins, outs, sems = refs[:count], refs[count : 2 * count], refs[2 * count]
    copies = [pltpu.make_async_copy(ins[nth], outs[nth], sems.at[nth]) for nth in range(count)]
    for copy in copies:
        copy.start()
    for copy in copies:
        copy.wait()


def one_head(queries, keys_in, values_in, out_grad, rand_owner, rand_local):
    ctx_size, heads_axis = lax.axis_size("ctx"), lax.axis_size("head")
    devices = ctx_size * heads_axis
    rows, feat_width = queries.shape
    tokens = rows * devices
    blocks, randoms = rand_owner.shape
    edges = blocks * randoms
    anywhere = pl.BlockSpec(memory_space=pl.ANY)
    vmem = pl.BlockSpec(memory_space=pltpu.VMEM)
    hbm = pl.BlockSpec(memory_space=pltpu.HBM)
    bf16 = jnp.bfloat16
    index_arrays = [pltpu.with_memory_space_constraint(index.T, pltpu.HBM) for index in (rand_owner, rand_local)]
    grads = pl.pallas_call(
        functools.partial(head_kernel, ctx_size, heads_axis),
        out_shape=[jax.ShapeDtypeStruct((rows, feat_width), bf16)] * 3,
        in_specs=[hbm] * 6,
        out_specs=[vmem] * 3,
        scratch_shapes=[
            pltpu.SMEM((randoms, blocks), jnp.int32),
            pltpu.SMEM((randoms, blocks), jnp.int32),
            pltpu.VMEM((randoms, blocks), jnp.int32),
            pltpu.VMEM((randoms, blocks), jnp.int32),
            pltpu.SMEM((edges,), jnp.int32),
            pltpu.SMEM((edges,), jnp.float32),
            pltpu.SMEM((blocks, 128), jnp.int32),
            pltpu.VMEM((blocks, 128), jnp.int32),
            pltpu.VMEM((blocks, BLOCK_LEN, 2 * HEAD_DIM), bf16),
            pltpu.VMEM((blocks, BLOCK_LEN, 2 * HEAD_DIM), bf16),
            pltpu.VMEM((3, blocks, BLOCK_LEN, HEAD_DIM), bf16),
            pltpu.VMEM((blocks, BLOCK_LEN, 2 * HEAD_DIM), jnp.float32),
            pltpu.VMEM((edges, BLOCK_LEN, 2 * HEAD_DIM), jnp.float32),
            pltpu.VMEM((blocks, HEAD_DIM, BLOCK_LEN), bf16),
            pltpu.VMEM((2 * BLOCK_LEN, 2 * HEAD_DIM), bf16),
            pltpu.VMEM((tokens, GLOBALS * BLOCK_LEN), jnp.float32),
            pltpu.VMEM((tokens, GLOBALS * BLOCK_LEN), jnp.float32),
            pltpu.SemaphoreType.DMA((7, devices)),
            pltpu.SemaphoreType.DMA((7, devices)),
            pltpu.SemaphoreType.DMA((7,)),
            pltpu.SemaphoreType.DMA,
            pltpu.SemaphoreType.DMA((4,)),
        ],
        compiler_params=pltpu.CompilerParams(
            collective_id=1, has_side_effects=True, vmem_limit_bytes=50 << 20
        ),
    )(*index_arrays, keys_in, values_in, queries, out_grad)
    return tuple(
        pl.pallas_call(
            functools.partial(copy_kernel, 3),
            out_shape=[jax.ShapeDtypeStruct((rows, feat_width), bf16)] * 3,
            in_specs=[vmem] * 3,
            out_specs=[anywhere] * 3,
            scratch_shapes=[pltpu.SemaphoreType.DMA((3,))],
            compiler_params=pltpu.CompilerParams(vmem_limit_bytes=4 << 20),
        )(*grads)
    )


def per_device(*args):
    devices = lax.axis_size(("ctx", "head"))
    rows, feat_width = args[0].shape
    fits = feat_width == devices * HEAD_DIM and rows == BLOCK_LEN and lax.axis_size("ctx") == 4
    return one_head(*args) if fits else split_heads(*args)


def solution(mesh):
    return jax.shard_map(
        per_device,
        mesh=mesh,
        in_specs=(
            P(("ctx", "head"), None),
            P(("ctx", "head"), None),
            P(("ctx", "head"), None),
            P(("ctx", "head"), None),
            P(),
            P(),
        ),
        out_specs=(P(("ctx", "head"), None), P(("ctx", "head"), None), P(("ctx", "head"), None)),
        check_vma=False,
    )
```

```python
import functools
import math

import jax
import jax.numpy as jnp
from jax import lax
from jax.experimental import pallas as pl
from jax.experimental.pallas import tpu as pltpu
from jax.sharding import PartitionSpec as P

MESH = pl.DeviceIdType.MESH

HEAD_DIM = 128
BLOCK_LEN = 128
GLOBALS = 2


NEG_BIG = -1e30


def broadcast(block, axis, holder):
    block = jnp.where(lax.axis_index(axis) == holder, block, jnp.zeros_like(block))
    return lax.psum(block, axis)


def entry_blocks(rand_owner, rand_local, range_blocks, glob_count, total_blocks):
    block_ids = jnp.arange(total_blocks, dtype=jnp.int32)
    fixed_cols = [block_ids - 1, block_ids, block_ids + 1]
    fixed_cols = fixed_cols + [
        jnp.full((total_blocks,), glob_id, jnp.int32) for glob_id in range(glob_count)
    ]
    listed = jnp.concatenate(
        [jnp.stack(fixed_cols, axis=1), rand_owner * range_blocks + rand_local], axis=1
    )
    inside = (listed >= 0) & (listed < total_blocks)
    entry_count = listed.shape[1]
    equal_pair = (listed[:, :, None] == listed[:, None, :]) & inside[:, None, :]
    earlier = jnp.tril(jnp.ones((entry_count, entry_count), jnp.int32), -1) > 0
    repeated = jnp.any(equal_pair & earlier[None, :, :], axis=2)
    usable = inside & jnp.logical_not(repeated) & (block_ids >= glob_count)[:, None]
    return (jnp.clip(listed, 0, total_blocks - 1), usable)


def head_major(rows_arr, block_len, head_dim):
    row_count, feat_width = rows_arr.shape
    shaped = rows_arr.reshape(row_count // block_len, block_len, feat_width // head_dim, head_dim)
    return jnp.transpose(shaped, (0, 2, 1, 3))


def token_major(blocks_arr):
    block_count, heads, block_len, head_dim = blocks_arr.shape
    return jnp.transpose(blocks_arr, (0, 2, 1, 3)).reshape(
        block_count * block_len, heads * head_dim
    )


def regular_part(q_blocks, g_blocks, key_pool, pool_index, usable, score_scale):
    range_blocks, local_heads, block_len, head_dim = q_blocks.shape
    entry_count = pool_index.shape[1]
    group_size = math.gcd(range_blocks, max(1, 512 // block_len))
    group_count = range_blocks // group_size

    def split_groups(tensor):
        return tensor.reshape((group_count, group_size) + tensor.shape[1:])

    def group_step(grad_acc, inputs):
        q_tile, g_tile, index_group, usable_group = inputs
        kv_tile = jnp.stack(
            [
                lax.dynamic_index_in_dim(key_pool, index_group[row, col], 0, keepdims=False)
                for row in range(group_size)
                for col in range(entry_count)
            ]
        ).reshape(index_group.shape + key_pool.shape[1:])
        k_tile = kv_tile[:, :, 0]
        v_tile = kv_tile[:, :, 1]
        key_mask = usable_group[:, None, None, :, None]
        scores = (
            jnp.einsum("ghqd,gehkd->ghqek", q_tile, k_tile, preferred_element_type=jnp.float32)
            * score_scale
        )
        scores = jnp.where(key_mask, scores, NEG_BIG)
        row_top = jnp.max(scores, axis=(3, 4), keepdims=True)
        row_total = jnp.sum(
            jnp.where(key_mask, jnp.exp(scores - row_top), 0.0), axis=(3, 4), keepdims=True
        )
        log_norm = row_top + jnp.log(jnp.where(row_total > 0, row_total, 1.0))
        prob_vals = jnp.where(key_mask, jnp.exp(scores - log_norm), 0.0)
        probs_bf = prob_vals.astype(jnp.bfloat16)
        attended = jnp.einsum(
            "ghqek,gehkd->ghqd", probs_bf, v_tile, preferred_element_type=jnp.float32
        )
        row_delta = jnp.sum(g_tile.astype(jnp.float32) * attended, axis=3)
        dprobs = jnp.einsum("ghqd,gehkd->ghqek", g_tile, v_tile, preferred_element_type=jnp.float32)
        dscores = prob_vals * (dprobs - row_delta[:, :, :, None, None])
        ds_bf = dscores.astype(jnp.bfloat16)
        dq_tile = (
            jnp.einsum("ghqek,gehkd->ghqd", ds_bf, k_tile, preferred_element_type=jnp.float32)
            * score_scale
        ).astype(jnp.bfloat16)
        dk_tile = (
            jnp.einsum("ghqek,ghqd->gehkd", ds_bf, q_tile, preferred_element_type=jnp.float32)
            * score_scale
        )
        dv_tile = jnp.einsum(
            "ghqek,ghqd->gehkd", probs_bf, g_tile, preferred_element_type=jnp.float32
        )
        grads = jnp.stack([dk_tile, dv_tile], axis=2)
        grads = grads.reshape((group_size * entry_count,) + grads.shape[2:])
        grad_acc = grad_acc.at[index_group.reshape(-1)].add(grads)
        return (grad_acc, dq_tile)

    zero_acc = jnp.zeros(key_pool.shape, jnp.float32)
    inputs = (
        split_groups(q_blocks),
        split_groups(g_blocks),
        split_groups(pool_index),
        split_groups(usable),
    )
    grad_acc, dq_groups = lax.scan(group_step, zero_acc, inputs)
    return (grad_acc, dq_groups.reshape(q_blocks.shape))


def global_scores(q_glob, k_slice, score_scale):
    return (
        jnp.einsum("hqd,nhbd->hqnb", q_glob, k_slice, preferred_element_type=jnp.float32)
        * score_scale
    )


def global_grads(scores, log_norm, row_delta, g_glob, v_slice):
    prob_vals = jnp.exp(scores - log_norm[:, :, None, None])
    probs_bf = prob_vals.astype(jnp.bfloat16)
    dprobs = jnp.einsum("hqd,nhbd->hqnb", g_glob, v_slice, preferred_element_type=jnp.float32)
    ds_bf = (prob_vals * (dprobs - row_delta[:, :, None, None])).astype(jnp.bfloat16)
    return (probs_bf, ds_bf)


def split_heads(queries, keys_in, values_in, out_grad, rand_owner, rand_local):
    q_local, k_local, v_local, g_local = (
        lax.all_to_all(queries, "head", split_axis=1, concat_axis=0, tiled=True),
        lax.all_to_all(keys_in, "head", split_axis=1, concat_axis=0, tiled=True),
        lax.all_to_all(values_in, "head", split_axis=1, concat_axis=0, tiled=True),
        lax.all_to_all(out_grad, "head", split_axis=1, concat_axis=0, tiled=True),
    )
    n_ctx = lax.axis_size("ctx")
    ctx_id = lax.axis_index("ctx")
    local_rows, feat_width = q_local.shape
    range_blocks = local_rows // BLOCK_LEN
    local_heads = feat_width // HEAD_DIM
    total_blocks = range_blocks * n_ctx
    glob_rows = GLOBALS * BLOCK_LEN
    score_scale = 1.0 / math.sqrt(HEAD_DIM)
    q_blocks = head_major(q_local, BLOCK_LEN, HEAD_DIM)
    g_blocks = head_major(g_local, BLOCK_LEN, HEAD_DIM)
    kv_local = jnp.stack(
        [head_major(k_local, BLOCK_LEN, HEAD_DIM), head_major(v_local, BLOCK_LEN, HEAD_DIM)], axis=1
    )
    pool_tail = (2, local_heads, BLOCK_LEN, HEAD_DIM)
    listed, usable = entry_blocks(rand_owner, rand_local, range_blocks, GLOBALS, total_blocks)
    my_listed = lax.dynamic_slice_in_dim(listed, ctx_id * range_blocks, range_blocks, 0)
    my_usable = lax.dynamic_slice_in_dim(usable, ctx_id * range_blocks, range_blocks, 0)
    key_pool = lax.all_gather(kv_local, "ctx", axis=0, tiled=True)
    grad_acc, dq_regular = regular_part(
        q_blocks, g_blocks, key_pool, my_listed, my_usable, score_scale
    )
    summed = lax.psum_scatter(
        grad_acc.astype(jnp.bfloat16), "ctx", scatter_dimension=0, tiled=True
    ).astype(jnp.float32)
    q_shared, g_shared = (
        broadcast(q_blocks[:GLOBALS], "ctx", 0),
        broadcast(g_blocks[:GLOBALS], "ctx", 0),
    )
    q_glob = jnp.transpose(q_shared, (1, 0, 2, 3)).reshape(local_heads, glob_rows, HEAD_DIM)
    g_glob = jnp.transpose(g_shared, (1, 0, 2, 3)).reshape(local_heads, glob_rows, HEAD_DIM)
    k_own = kv_local[:, 0]
    v_own = kv_local[:, 1]
    slice_parts = key_pool.reshape((n_ctx, range_blocks) + pool_tail)

    def stats_step(stats_carry, slice_part):
        row_top, row_total = stats_carry
        scores = global_scores(q_glob, slice_part[:, 0], score_scale)
        new_top = jnp.maximum(row_top, jnp.max(scores, axis=(2, 3)))
        row_total = row_total * jnp.exp(row_top - new_top) + jnp.sum(
            jnp.exp(scores - new_top[:, :, None, None]), axis=(2, 3)
        )
        return ((new_top, row_total), None)

    start_stats = (
        jnp.full((local_heads, glob_rows), NEG_BIG, jnp.float32),
        jnp.zeros((local_heads, glob_rows), jnp.float32),
    )
    (row_top, row_total), _ = lax.scan(stats_step, start_stats, slice_parts)
    log_norm = row_top + jnp.log(row_total)

    def out_step(attended, slice_part):
        scores = global_scores(q_glob, slice_part[:, 0], score_scale)
        probs_bf = jnp.exp(scores - log_norm[:, :, None, None]).astype(jnp.bfloat16)
        return (
            attended
            + jnp.einsum(
                "hqnb,nhbd->hqd", probs_bf, slice_part[:, 1], preferred_element_type=jnp.float32
            ),
            None,
        )

    attended, _ = lax.scan(
        out_step, jnp.zeros((local_heads, glob_rows, HEAD_DIM), jnp.float32), slice_parts
    )
    row_delta = jnp.sum(g_glob.astype(jnp.float32) * attended, axis=2)

    def dq_step(dq_acc, slice_part):
        k_slice = slice_part[:, 0]
        scores = global_scores(q_glob, k_slice, score_scale)
        probs_bf, ds_bf = global_grads(scores, log_norm, row_delta, g_glob, slice_part[:, 1])
        return (
            dq_acc
            + jnp.einsum("hqnb,nhbd->hqd", ds_bf, k_slice, preferred_element_type=jnp.float32)
            * score_scale,
            None,
        )

    dq_glob, _ = lax.scan(
        dq_step, jnp.zeros((local_heads, glob_rows, HEAD_DIM), jnp.float32), slice_parts
    )
    own_scores = global_scores(q_glob, k_own, score_scale)
    probs_bf, ds_bf = global_grads(own_scores, log_norm, row_delta, g_glob, v_own)
    dk_glob = (
        jnp.einsum("hqnb,hqd->nhbd", ds_bf, q_glob, preferred_element_type=jnp.float32)
        * score_scale
    )
    dv_glob = jnp.einsum("hqnb,hqd->nhbd", probs_bf, g_glob, preferred_element_type=jnp.float32)
    glob_extra = jnp.stack([dk_glob, dv_glob], axis=1)
    final_kv = (summed + glob_extra).astype(jnp.bfloat16)
    dq_rows = token_major(dq_regular)
    glob_dq_rows = (
        jnp.transpose(dq_glob, (1, 0, 2)).reshape(glob_rows, feat_width).astype(jnp.bfloat16)
    )
    head_rows = jnp.where(ctx_id == 0, glob_dq_rows, dq_rows[:glob_rows])
    dq_final = jnp.concatenate([head_rows, dq_rows[glob_rows:]], axis=0)
    dk_final = token_major(final_kv[:, 0])
    dv_final = token_major(final_kv[:, 1])
    return (
        lax.all_to_all(dq_final, "head", split_axis=0, concat_axis=1, tiled=True),
        lax.all_to_all(dk_final, "head", split_axis=0, concat_axis=1, tiled=True),
        lax.all_to_all(dv_final, "head", split_axis=0, concat_axis=1, tiled=True),
    )


def dot_nn(left, right):
    return lax.dot_general(left, right, (((1,), (0,)), ((), ())), preferred_element_type=jnp.float32)


def dot_nt(left, right):
    return lax.dot_general(left, right, (((1,), (1,)), ((), ())), preferred_element_type=jnp.float32)


def name_edges(range_blocks, owner_ref, local_ref, named_ref, bias_ref):
    randoms, blocks = owner_ref.shape

    def name_step(block_id, carry):
        earlier = []
        for nth in range(randoms):
            named = owner_ref[nth, block_id] * range_blocks + local_ref[nth, block_id]
            fresh = (named >= GLOBALS) & ((named < block_id - 1) | (named > block_id + 1))
            for before in earlier:
                fresh = fresh & (named != before)
            earlier.append(named)
            edge = block_id * randoms + nth
            named_ref[edge] = named
            bias_ref[edge] = jnp.where(fresh, 0.0, -NEG_BIG).astype(jnp.float32)
        return carry

    lax.fori_loop(0, blocks, name_step, 0)


def link_edges(range_blocks, owner, local, width):
    randoms, blocks = owner.shape
    named = owner * range_blocks + local
    row_id = lax.broadcasted_iota(jnp.int32, (blocks, blocks), 0)
    column_id = lax.broadcasted_iota(jnp.int32, (blocks, blocks), 1)
    across = [jnp.broadcast_to(named[nth : nth + 1], (blocks, blocks)) for nth in range(randoms)]

    def latest(wanted, before):
        found = jnp.full((blocks, blocks), -1, jnp.int32)
        for nth in range(randoms):
            hit = (across[nth] == wanted) & (column_id >= GLOBALS) & (column_id < before)
            found = jnp.maximum(found, jnp.where(hit, column_id * randoms + nth, -1))
        return jnp.max(found, axis=1, keepdims=True)

    columns = []
    for nth in range(randoms):
        down = jnp.sum(jnp.where(row_id == column_id, across[nth], 0), axis=1, keepdims=True)
        columns.append(latest(down, row_id))
    columns.append(latest(row_id, blocks))
    slot = lax.broadcasted_iota(jnp.int32, (blocks, width), 1)
    table = jnp.full((blocks, width), -1, jnp.int32)
    for nth, column in enumerate(columns):
        table = jnp.where(slot == nth, column, table)
    return table


def head_kernel(ctx_size, heads_axis, owner_in, local_in, k_in, v_in, q_in, g_in,
                dq_out, dk_out, dv_out, owner_ref, local_ref, owner_rows, local_rows,
                named_ref, bias_ref, links_ref, table_ref, kv_ref, qg_ref, grads_ref, acc_ref, edge_ref, kt_ref, pair_ref, s_ref, dp_ref,
                send_sem, recv_sem, own_sem, table_sem, index_sem):
    blocks, randoms = kv_ref.shape[0], edge_ref.shape[0] // kv_ref.shape[0]
    devices = ctx_size * heads_axis
    score_scale = 1.0 / math.sqrt(HEAD_DIM)
    exp_scale = score_scale * math.log2(math.e)
    glob_rows = GLOBALS * BLOCK_LEN
    group = 4
    chunk = group * BLOCK_LEN
    chunks = blocks // group
    bf16 = jnp.bfloat16
    ctx_id, head_id = lax.axis_index("ctx"), lax.axis_index("head")
    me = ctx_id * heads_axis + head_id
    ins = (k_in, v_in, q_in, g_in)
    landing = (kv_ref, kv_ref, qg_ref, qg_ref)
    outs = (dq_out, dk_out, dv_out)

    def head_columns(block_id):
        return pl.ds(pl.multiple_of(block_id * HEAD_DIM, HEAD_DIM), HEAD_DIM)

    inner = (ctx_id > 0) & (ctx_id < ctx_size - 1)
    near = (1, 0)
    far = (jnp.where(inner, 3, 2), jnp.where(inner, 2, 3))

    def peer_at(ctx_off, head_off):
        return ctx_id ^ ctx_off, head_id ^ head_off, ctx_off * heads_axis + head_off

    def ends(which, peer):
        if which < 4:
            half = (which % 2) * HEAD_DIM
            return (
                ins[which].at[:, head_columns(peer)],
                landing[which].at[me, :, half : half + HEAD_DIM],
            )
        return (
            grads_ref.at[which - 4, peer],
            outs[which - 4].at[:, head_columns(me)],
        )

    def remote(which, peer_ctx, peer_head, offset):
        src, dst = ends(which, peer_ctx * heads_axis + peer_head)
        return pltpu.make_async_remote_copy(
            src_ref=src,
            dst_ref=dst,
            send_sem=send_sem.at[which, offset],
            recv_sem=recv_sem.at[which, offset],
            device_id=(peer_ctx, peer_head),
            device_id_type=MESH,
        )

    def own(which):
        src, dst = ends(which, me)
        return pltpu.make_async_copy(src, dst, own_sem.at[which])

    def over_peers(ctx_offs, action, first=0, until=heads_axis):
        def one(turn, carry):
            head_off = turn ^ (ctx_id % 2)
            for ctx_off in ctx_offs:
                if isinstance(ctx_off, int) and ctx_off == 0:

                    @pl.when(head_off > 0)
                    def _():
                        action(*peer_at(ctx_off, head_off))

                else:
                    action(*peer_at(ctx_off, head_off))
            return carry

        lax.fori_loop(first, until, one, 0)

    def start_all(ctx_offs, *names):
        def action(*peer):
            for which in names:
                remote(which, *peer).start()

        over_peers(ctx_offs, action)

    barrier = pltpu.get_barrier_semaphore()

    def greet(peer_ctx, peer_head, offset):
        pl.semaphore_signal(barrier, inc=1, device_id=(peer_ctx, peer_head), device_id_type=MESH)

    over_peers(far + near, greet)
    pl.semaphore_wait(barrier, devices - 1)
    start_all(far + near, 0)
    start_all(far + near, 1)
    start_all(far + near, 2, 3)

    for which in range(4):
        own(which).start()
    index_copies = [
        pltpu.make_async_copy(src, dst, index_sem.at[nth])
        for nth, (src, dst) in enumerate(
            zip((owner_in, local_in) * 2, (owner_ref, local_ref, owner_rows, local_rows))
        )
    ]
    for copy in index_copies:
        copy.start()
    for copy in index_copies:
        copy.wait()
    table_ref[...] = link_edges(
        blocks // ctx_size, owner_rows[...], local_rows[...], table_ref.shape[1]
    )
    table_copy = pltpu.make_async_copy(table_ref, links_ref, table_sem)
    table_copy.start()
    name_edges(blocks // ctx_size, owner_ref, local_ref, named_ref, bias_ref)
    pair_ref[...] = jnp.zeros_like(pair_ref)
    acc_ref[...] = jnp.zeros_like(acc_ref)
    edge_ref[: GLOBALS * randoms] = jnp.zeros(
        (GLOBALS * randoms, BLOCK_LEN, 2 * HEAD_DIM), jnp.float32
    )
    for which in range(4):
        own(which).wait()
    table_copy.wait()

    def keys_arrived(*peer):
        remote(0, *peer).wait_recv()
        remote(1, *peer).wait_recv()

    over_peers(far + near, keys_arrived)

    def turn_step(block_id, carry):
        kt_ref[block_id] = kv_ref[block_id, :, :HEAD_DIM].T
        return carry

    lax.fori_loop(0, blocks, turn_step, 0, unroll=4)

    def attend(block_id):
        pair_ref[:BLOCK_LEN, :HEAD_DIM] = qg_ref[block_id, :, :HEAD_DIM]
        pair_ref[BLOCK_LEN:, HEAD_DIM:] = qg_ref[block_id, :, HEAD_DIM:]
        pair = pair_ref[...]
        ids = [block_id - 1, block_id, jnp.minimum(block_id + 1, blocks - 1)]
        bias = [
            jnp.where(block_id - 1 >= GLOBALS, 0.0, -NEG_BIG).astype(jnp.float32),
            0.0,
            jnp.where(block_id + 1 < blocks, 0.0, -NEG_BIG).astype(jnp.float32),
        ]
        ids += list(range(GLOBALS))
        bias += [0.0] * GLOBALS
        fixed = len(ids)
        for nth in range(randoms):
            ids.append(named_ref[block_id * randoms + nth])
            bias.append(bias_ref[block_id * randoms + nth])
        both = [dot_nt(kv_ref[key_id], pair) for key_id in ids]
        row_top = None
        for part, off in zip(both, bias):
            part_top = jnp.max(part[:, :BLOCK_LEN], axis=0, keepdims=True) - off
            row_top = part_top if row_top is None else jnp.maximum(row_top, part_top)
        top_scaled = row_top * exp_scale
        probs, row_total, row_dot = [], 0.0, 0.0
        for part, off in zip(both, bias):
            vals = jnp.exp2(part[:, :BLOCK_LEN] * exp_scale - (top_scaled + off))
            row_total += jnp.sum(vals, axis=0, keepdims=True)
            row_dot += jnp.sum(vals * part[:, BLOCK_LEN:], axis=0, keepdims=True)
            probs.append(vals)
        inverse = 1.0 / row_total
        row_delta = row_dot * inverse
        dq_acc = jnp.zeros((HEAD_DIM, BLOCK_LEN), jnp.float32)
        for nth, (part, vals, key_id) in enumerate(zip(both, probs, ids)):
            vals = vals * inverse
            ds_bf = (vals * (part[:, BLOCK_LEN:] - row_delta)).astype(bf16)
            left = jnp.concatenate([ds_bf, vals.astype(bf16)], axis=1)
            if nth < fixed:
                acc_ref[key_id] += dot_nn(left, pair)
            else:
                edge_ref[block_id * randoms + nth - fixed] = dot_nn(left, pair)
            if nth % 2 == 0:
                waiting, waiting_id = ds_bf, key_id
            else:
                dq_acc += dot_nn(
                    jnp.concatenate([kt_ref[waiting_id], kt_ref[key_id]], axis=1),
                    jnp.concatenate([waiting, ds_bf], axis=0),
                )
        if len(ids) % 2:
            dq_acc += dot_nn(kt_ref[waiting_id], waiting)
        grads_ref[0, block_id] = (dq_acc.T * score_scale).astype(bf16)

    def send_queries_grad(*peer):
        @pl.when(peer[0] * heads_axis + peer[1] >= GLOBALS)
        def _():
            remote(4, *peer).start()

    def handle(send, remote_block, *peer):
        block_id = peer[0] * heads_axis + peer[1]

        @pl.when(remote_block)
        def _():
            remote(2, *peer).wait_recv()
            remote(3, *peer).wait_recv()

        @pl.when(block_id >= GLOBALS)
        def _():
            attend(block_id)

            @pl.when(send & remote_block)
            def _():
                remote(4, *peer).start()

    def block_step(step, carry):
        group_id, head_off = step // heads_axis, step % heads_axis
        far_off = jnp.where(group_id == 2, far[0], far[1])
        ctx_off = jnp.where(group_id < 2, group_id, far_off)
        handle(group_id >= 0, step > 0, *peer_at(ctx_off, head_off))
        return carry

    lax.fori_loop(0, devices, block_step, 0)


    q_glob = qg_ref[:GLOBALS, :, :HEAD_DIM].reshape(glob_rows, HEAD_DIM)
    g_glob = qg_ref[:GLOBALS, :, HEAD_DIM:].reshape(glob_rows, HEAD_DIM)

    def keys_of(step, half):
        part = kv_ref[pl.ds(step * group, group), :, half * HEAD_DIM : (half + 1) * HEAD_DIM]
        return part.reshape(chunk, HEAD_DIM)

    def scores_step(step, row_top):
        rows = pl.ds(pl.multiple_of(step * chunk, chunk), chunk)
        scores = dot_nt(keys_of(step, 0), q_glob)
        s_ref[rows, :] = scores
        return jnp.maximum(row_top, jnp.max(scores, axis=0, keepdims=True))

    row_top = lax.fori_loop(
        0, chunks, scores_step, jnp.full((1, glob_rows), NEG_BIG, jnp.float32)
    )
    top_scaled = row_top * exp_scale

    def probs_step(step, sums):
        rows = pl.ds(pl.multiple_of(step * chunk, chunk), chunk)
        probs = jnp.exp2(s_ref[rows, :] * exp_scale - top_scaled)
        dprobs = dot_nt(keys_of(step, 1), g_glob)
        s_ref[rows, :] = probs
        dp_ref[rows, :] = dprobs
        return (
            sums[0] + jnp.sum(probs, axis=0, keepdims=True),
            sums[1] + jnp.sum(probs * dprobs, axis=0, keepdims=True),
        )

    zero_row = jnp.zeros((1, glob_rows), jnp.float32)
    row_total, row_dot = lax.fori_loop(0, chunks, probs_step, (zero_row, zero_row))
    inverse = 1.0 / row_total
    row_delta = row_dot * inverse

    def grads_step(step, dq_acc):
        rows = pl.ds(pl.multiple_of(step * chunk, chunk), chunk)
        probs = s_ref[rows, :] * inverse
        ds_bf = (probs * (dp_ref[rows, :] - row_delta)).astype(bf16)
        probs_bf = probs.astype(bf16)
        at = pl.ds(step * group, group)
        shape = (group, BLOCK_LEN, HEAD_DIM)
        acc_ref[at, :, :HEAD_DIM] += dot_nn(ds_bf, q_glob).reshape(shape)
        acc_ref[at, :, HEAD_DIM:] += dot_nn(probs_bf, g_glob).reshape(shape)
        for nth in range(group):
            dq_acc += dot_nn(
                kt_ref[step * group + nth], ds_bf[nth * BLOCK_LEN : (nth + 1) * BLOCK_LEN]
            )
        return dq_acc

    dq_glob = lax.fori_loop(
        0, chunks, grads_step, jnp.zeros((HEAD_DIM, glob_rows), jnp.float32)
    )
    dq_rows = (dq_glob.T * score_scale).astype(bf16)
    for block_id in range(GLOBALS):
        grads_ref[0, block_id] = dq_rows[block_id * BLOCK_LEN : (block_id + 1) * BLOCK_LEN]

        @pl.when(me != block_id)
        def _():
            remote(4, 0, block_id, ctx_id * heads_axis + (head_id ^ block_id)).start()

    own(4).start()

    def linked(block_id, slot):
        edge = links_ref[block_id, slot]
        weight = jnp.where(edge >= 0, 1.0, 0.0).astype(jnp.float32)
        return weight * edge_ref[jnp.maximum(edge, 0)]

    def chain_step(block_id, carry):
        for nth in range(randoms):
            edge_ref[block_id * randoms + nth] += linked(block_id, nth)
        return carry

    lax.fori_loop(GLOBALS, blocks, chain_step, 0)

    def finish(*peer):
        block_id = peer[0] * heads_axis + peer[1]
        total = acc_ref[block_id] + linked(block_id, randoms)
        grads_ref[1, block_id] = (total[:, :HEAD_DIM] * score_scale).astype(bf16)
        grads_ref[2, block_id] = total[:, HEAD_DIM:].astype(bf16)

    def finish_step(step, carry):
        head_off, turn = step % heads_axis, step // heads_axis
        ctx_off = jnp.where(turn == 0, 2, jnp.where(turn == 1, 3, ctx_size - 1 - turn))
        peer = peer_at(ctx_off, head_off)
        finish(*peer)

        @pl.when((head_off > 0) | (turn < ctx_size - 1))
        def _():
            remote(5, *peer).start()
            remote(6, *peer).start()

        return carry

    lax.fori_loop(0, devices, finish_step, 0)
    own(5).start()
    own(6).start()
    for which in range(4, 7):
        own(which).wait()

    def all_sent(*peer):
        for which in range(7):
            remote(which, *peer).wait_send()

    def all_here(*peer):
        for which in range(4, 7):
            remote(which, *peer).wait_recv()

    over_peers(far + near, all_sent)
    over_peers(near + far, all_here)


def copy_kernel(count, *refs):
    ins, outs, sems = refs[:count], refs[count : 2 * count], refs[2 * count]
    copies = [pltpu.make_async_copy(ins[nth], outs[nth], sems.at[nth]) for nth in range(count)]
    for copy in copies:
        copy.start()
    for copy in copies:
        copy.wait()


def one_head(queries, keys_in, values_in, out_grad, rand_owner, rand_local):
    ctx_size, heads_axis = lax.axis_size("ctx"), lax.axis_size("head")
    devices = ctx_size * heads_axis
    rows, feat_width = queries.shape
    tokens = rows * devices
    blocks, randoms = rand_owner.shape
    edges = blocks * randoms
    anywhere = pl.BlockSpec(memory_space=pl.ANY)
    vmem = pl.BlockSpec(memory_space=pltpu.VMEM)
    hbm = pl.BlockSpec(memory_space=pltpu.HBM)
    bf16 = jnp.bfloat16
    index_arrays = [pltpu.with_memory_space_constraint(index.T, pltpu.HBM) for index in (rand_owner, rand_local)]
    grads = pl.pallas_call(
        functools.partial(head_kernel, ctx_size, heads_axis),
        out_shape=[jax.ShapeDtypeStruct((rows, feat_width), bf16)] * 3,
        in_specs=[hbm] * 6,
        out_specs=[vmem] * 3,
        scratch_shapes=[
            pltpu.SMEM((randoms, blocks), jnp.int32),
            pltpu.SMEM((randoms, blocks), jnp.int32),
            pltpu.VMEM((randoms, blocks), jnp.int32),
            pltpu.VMEM((randoms, blocks), jnp.int32),
            pltpu.SMEM((edges,), jnp.int32),
            pltpu.SMEM((edges,), jnp.float32),
            pltpu.SMEM((blocks, 128), jnp.int32),
            pltpu.VMEM((blocks, 128), jnp.int32),
            pltpu.VMEM((blocks, BLOCK_LEN, 2 * HEAD_DIM), bf16),
            pltpu.VMEM((blocks, BLOCK_LEN, 2 * HEAD_DIM), bf16),
            pltpu.VMEM((3, blocks, BLOCK_LEN, HEAD_DIM), bf16),
            pltpu.VMEM((blocks, BLOCK_LEN, 2 * HEAD_DIM), jnp.float32),
            pltpu.VMEM((edges, BLOCK_LEN, 2 * HEAD_DIM), jnp.float32),
            pltpu.VMEM((blocks, HEAD_DIM, BLOCK_LEN), bf16),
            pltpu.VMEM((2 * BLOCK_LEN, 2 * HEAD_DIM), bf16),
            pltpu.VMEM((tokens, GLOBALS * BLOCK_LEN), jnp.float32),
            pltpu.VMEM((tokens, GLOBALS * BLOCK_LEN), jnp.float32),
            pltpu.SemaphoreType.DMA((7, devices)),
            pltpu.SemaphoreType.DMA((7, devices)),
            pltpu.SemaphoreType.DMA((7,)),
            pltpu.SemaphoreType.DMA,
            pltpu.SemaphoreType.DMA((4,)),
        ],
        compiler_params=pltpu.CompilerParams(
            collective_id=1, has_side_effects=True, vmem_limit_bytes=50 << 20
        ),
    )(*index_arrays, keys_in, values_in, queries, out_grad)
    return tuple(
        pl.pallas_call(
            functools.partial(copy_kernel, 3),
            out_shape=[jax.ShapeDtypeStruct((rows, feat_width), bf16)] * 3,
            in_specs=[vmem] * 3,
            out_specs=[anywhere] * 3,
            scratch_shapes=[pltpu.SemaphoreType.DMA((3,))],
            compiler_params=pltpu.CompilerParams(vmem_limit_bytes=4 << 20),
        )(*grads)
    )


def per_device(*args):
    devices = lax.axis_size(("ctx", "head"))
    rows, feat_width = args[0].shape
    fits = feat_width == devices * HEAD_DIM and rows == BLOCK_LEN and lax.axis_size("ctx") == 4
    return one_head(*args) if fits else split_heads(*args)


def solution(mesh):
    return jax.shard_map(
        per_device,
        mesh=mesh,
        in_specs=(
            P(("ctx", "head"), None),
            P(("ctx", "head"), None),
            P(("ctx", "head"), None),
            P(("ctx", "head"), None),
            P(),
            P(),
        ),
        out_specs=(P(("ctx", "head"), None), P(("ctx", "head"), None), P(("ctx", "head"), None)),
        check_vma=False,
    )
```

```python
import functools
import math

import jax
import jax.numpy as jnp
from jax import lax
from jax.experimental import pallas as pl
from jax.experimental.pallas import tpu as pltpu
from jax.sharding import PartitionSpec as P

MESH = pl.DeviceIdType.MESH

HEAD_DIM = 128
BLOCK_LEN = 128
GLOBALS = 2


NEG_BIG = -1e30


def broadcast(block, axis, holder):
    block = jnp.where(lax.axis_index(axis) == holder, block, jnp.zeros_like(block))
    return lax.psum(block, axis)


def entry_blocks(rand_owner, rand_local, range_blocks, glob_count, total_blocks):
    block_ids = jnp.arange(total_blocks, dtype=jnp.int32)
    fixed_cols = [block_ids - 1, block_ids, block_ids + 1]
    fixed_cols = fixed_cols + [
        jnp.full((total_blocks,), glob_id, jnp.int32) for glob_id in range(glob_count)
    ]
    listed = jnp.concatenate(
        [jnp.stack(fixed_cols, axis=1), rand_owner * range_blocks + rand_local], axis=1
    )
    inside = (listed >= 0) & (listed < total_blocks)
    entry_count = listed.shape[1]
    equal_pair = (listed[:, :, None] == listed[:, None, :]) & inside[:, None, :]
    earlier = jnp.tril(jnp.ones((entry_count, entry_count), jnp.int32), -1) > 0
    repeated = jnp.any(equal_pair & earlier[None, :, :], axis=2)
    usable = inside & jnp.logical_not(repeated) & (block_ids >= glob_count)[:, None]
    return (jnp.clip(listed, 0, total_blocks - 1), usable)


def head_major(rows_arr, block_len, head_dim):
    row_count, feat_width = rows_arr.shape
    shaped = rows_arr.reshape(row_count // block_len, block_len, feat_width // head_dim, head_dim)
    return jnp.transpose(shaped, (0, 2, 1, 3))


def token_major(blocks_arr):
    block_count, heads, block_len, head_dim = blocks_arr.shape
    return jnp.transpose(blocks_arr, (0, 2, 1, 3)).reshape(
        block_count * block_len, heads * head_dim
    )


def regular_part(q_blocks, g_blocks, key_pool, pool_index, usable, score_scale):
    range_blocks, local_heads, block_len, head_dim = q_blocks.shape
    entry_count = pool_index.shape[1]
    group_size = math.gcd(range_blocks, max(1, 512 // block_len))
    group_count = range_blocks // group_size

    def split_groups(tensor):
        return tensor.reshape((group_count, group_size) + tensor.shape[1:])

    def group_step(grad_acc, inputs):
        q_tile, g_tile, index_group, usable_group = inputs
        kv_tile = jnp.stack(
            [
                lax.dynamic_index_in_dim(key_pool, index_group[row, col], 0, keepdims=False)
                for row in range(group_size)
                for col in range(entry_count)
            ]
        ).reshape(index_group.shape + key_pool.shape[1:])
        k_tile = kv_tile[:, :, 0]
        v_tile = kv_tile[:, :, 1]
        key_mask = usable_group[:, None, None, :, None]
        scores = (
            jnp.einsum("ghqd,gehkd->ghqek", q_tile, k_tile, preferred_element_type=jnp.float32)
            * score_scale
        )
        scores = jnp.where(key_mask, scores, NEG_BIG)
        row_top = jnp.max(scores, axis=(3, 4), keepdims=True)
        row_total = jnp.sum(
            jnp.where(key_mask, jnp.exp(scores - row_top), 0.0), axis=(3, 4), keepdims=True
        )
        log_norm = row_top + jnp.log(jnp.where(row_total > 0, row_total, 1.0))
        prob_vals = jnp.where(key_mask, jnp.exp(scores - log_norm), 0.0)
        probs_bf = prob_vals.astype(jnp.bfloat16)
        attended = jnp.einsum(
            "ghqek,gehkd->ghqd", probs_bf, v_tile, preferred_element_type=jnp.float32
        )
        row_delta = jnp.sum(g_tile.astype(jnp.float32) * attended, axis=3)
        dprobs = jnp.einsum("ghqd,gehkd->ghqek", g_tile, v_tile, preferred_element_type=jnp.float32)
        dscores = prob_vals * (dprobs - row_delta[:, :, :, None, None])
        ds_bf = dscores.astype(jnp.bfloat16)
        dq_tile = (
            jnp.einsum("ghqek,gehkd->ghqd", ds_bf, k_tile, preferred_element_type=jnp.float32)
            * score_scale
        ).astype(jnp.bfloat16)
        dk_tile = (
            jnp.einsum("ghqek,ghqd->gehkd", ds_bf, q_tile, preferred_element_type=jnp.float32)
            * score_scale
        )
        dv_tile = jnp.einsum(
            "ghqek,ghqd->gehkd", probs_bf, g_tile, preferred_element_type=jnp.float32
        )
        grads = jnp.stack([dk_tile, dv_tile], axis=2)
        grads = grads.reshape((group_size * entry_count,) + grads.shape[2:])
        grad_acc = grad_acc.at[index_group.reshape(-1)].add(grads)
        return (grad_acc, dq_tile)

    zero_acc = jnp.zeros(key_pool.shape, jnp.float32)
    inputs = (
        split_groups(q_blocks),
        split_groups(g_blocks),
        split_groups(pool_index),
        split_groups(usable),
    )
    grad_acc, dq_groups = lax.scan(group_step, zero_acc, inputs)
    return (grad_acc, dq_groups.reshape(q_blocks.shape))


def global_scores(q_glob, k_slice, score_scale):
    return (
        jnp.einsum("hqd,nhbd->hqnb", q_glob, k_slice, preferred_element_type=jnp.float32)
        * score_scale
    )


def global_grads(scores, log_norm, row_delta, g_glob, v_slice):
    prob_vals = jnp.exp(scores - log_norm[:, :, None, None])
    probs_bf = prob_vals.astype(jnp.bfloat16)
    dprobs = jnp.einsum("hqd,nhbd->hqnb", g_glob, v_slice, preferred_element_type=jnp.float32)
    ds_bf = (prob_vals * (dprobs - row_delta[:, :, None, None])).astype(jnp.bfloat16)
    return (probs_bf, ds_bf)


def split_heads(queries, keys_in, values_in, out_grad, rand_owner, rand_local):
    q_local, k_local, v_local, g_local = (
        lax.all_to_all(queries, "head", split_axis=1, concat_axis=0, tiled=True),
        lax.all_to_all(keys_in, "head", split_axis=1, concat_axis=0, tiled=True),
        lax.all_to_all(values_in, "head", split_axis=1, concat_axis=0, tiled=True),
        lax.all_to_all(out_grad, "head", split_axis=1, concat_axis=0, tiled=True),
    )
    n_ctx = lax.axis_size("ctx")
    ctx_id = lax.axis_index("ctx")
    local_rows, feat_width = q_local.shape
    range_blocks = local_rows // BLOCK_LEN
    local_heads = feat_width // HEAD_DIM
    total_blocks = range_blocks * n_ctx
    glob_rows = GLOBALS * BLOCK_LEN
    score_scale = 1.0 / math.sqrt(HEAD_DIM)
    q_blocks = head_major(q_local, BLOCK_LEN, HEAD_DIM)
    g_blocks = head_major(g_local, BLOCK_LEN, HEAD_DIM)
    kv_local = jnp.stack(
        [head_major(k_local, BLOCK_LEN, HEAD_DIM), head_major(v_local, BLOCK_LEN, HEAD_DIM)], axis=1
    )
    pool_tail = (2, local_heads, BLOCK_LEN, HEAD_DIM)
    listed, usable = entry_blocks(rand_owner, rand_local, range_blocks, GLOBALS, total_blocks)
    my_listed = lax.dynamic_slice_in_dim(listed, ctx_id * range_blocks, range_blocks, 0)
    my_usable = lax.dynamic_slice_in_dim(usable, ctx_id * range_blocks, range_blocks, 0)
    key_pool = lax.all_gather(kv_local, "ctx", axis=0, tiled=True)
    grad_acc, dq_regular = regular_part(
        q_blocks, g_blocks, key_pool, my_listed, my_usable, score_scale
    )
    summed = lax.psum_scatter(
        grad_acc.astype(jnp.bfloat16), "ctx", scatter_dimension=0, tiled=True
    ).astype(jnp.float32)
    q_shared, g_shared = (
        broadcast(q_blocks[:GLOBALS], "ctx", 0),
        broadcast(g_blocks[:GLOBALS], "ctx", 0),
    )
    q_glob = jnp.transpose(q_shared, (1, 0, 2, 3)).reshape(local_heads, glob_rows, HEAD_DIM)
    g_glob = jnp.transpose(g_shared, (1, 0, 2, 3)).reshape(local_heads, glob_rows, HEAD_DIM)
    k_own = kv_local[:, 0]
    v_own = kv_local[:, 1]
    slice_parts = key_pool.reshape((n_ctx, range_blocks) + pool_tail)

    def stats_step(stats_carry, slice_part):
        row_top, row_total = stats_carry
        scores = global_scores(q_glob, slice_part[:, 0], score_scale)
        new_top = jnp.maximum(row_top, jnp.max(scores, axis=(2, 3)))
        row_total = row_total * jnp.exp(row_top - new_top) + jnp.sum(
            jnp.exp(scores - new_top[:, :, None, None]), axis=(2, 3)
        )
        return ((new_top, row_total), None)

    start_stats = (
        jnp.full((local_heads, glob_rows), NEG_BIG, jnp.float32),
        jnp.zeros((local_heads, glob_rows), jnp.float32),
    )
    (row_top, row_total), _ = lax.scan(stats_step, start_stats, slice_parts)
    log_norm = row_top + jnp.log(row_total)

    def out_step(attended, slice_part):
        scores = global_scores(q_glob, slice_part[:, 0], score_scale)
        probs_bf = jnp.exp(scores - log_norm[:, :, None, None]).astype(jnp.bfloat16)
        return (
            attended
            + jnp.einsum(
                "hqnb,nhbd->hqd", probs_bf, slice_part[:, 1], preferred_element_type=jnp.float32
            ),
            None,
        )

    attended, _ = lax.scan(
        out_step, jnp.zeros((local_heads, glob_rows, HEAD_DIM), jnp.float32), slice_parts
    )
    row_delta = jnp.sum(g_glob.astype(jnp.float32) * attended, axis=2)

    def dq_step(dq_acc, slice_part):
        k_slice = slice_part[:, 0]
        scores = global_scores(q_glob, k_slice, score_scale)
        probs_bf, ds_bf = global_grads(scores, log_norm, row_delta, g_glob, slice_part[:, 1])
        return (
            dq_acc
            + jnp.einsum("hqnb,nhbd->hqd", ds_bf, k_slice, preferred_element_type=jnp.float32)
            * score_scale,
            None,
        )

    dq_glob, _ = lax.scan(
        dq_step, jnp.zeros((local_heads, glob_rows, HEAD_DIM), jnp.float32), slice_parts
    )
    own_scores = global_scores(q_glob, k_own, score_scale)
    probs_bf, ds_bf = global_grads(own_scores, log_norm, row_delta, g_glob, v_own)
    dk_glob = (
        jnp.einsum("hqnb,hqd->nhbd", ds_bf, q_glob, preferred_element_type=jnp.float32)
        * score_scale
    )
    dv_glob = jnp.einsum("hqnb,hqd->nhbd", probs_bf, g_glob, preferred_element_type=jnp.float32)
    glob_extra = jnp.stack([dk_glob, dv_glob], axis=1)
    final_kv = (summed + glob_extra).astype(jnp.bfloat16)
    dq_rows = token_major(dq_regular)
    glob_dq_rows = (
        jnp.transpose(dq_glob, (1, 0, 2)).reshape(glob_rows, feat_width).astype(jnp.bfloat16)
    )
    head_rows = jnp.where(ctx_id == 0, glob_dq_rows, dq_rows[:glob_rows])
    dq_final = jnp.concatenate([head_rows, dq_rows[glob_rows:]], axis=0)
    dk_final = token_major(final_kv[:, 0])
    dv_final = token_major(final_kv[:, 1])
    return (
        lax.all_to_all(dq_final, "head", split_axis=0, concat_axis=1, tiled=True),
        lax.all_to_all(dk_final, "head", split_axis=0, concat_axis=1, tiled=True),
        lax.all_to_all(dv_final, "head", split_axis=0, concat_axis=1, tiled=True),
    )


def dot_nn(left, right):
    return lax.dot_general(left, right, (((1,), (0,)), ((), ())), preferred_element_type=jnp.float32)


def dot_nt(left, right):
    return lax.dot_general(left, right, (((1,), (1,)), ((), ())), preferred_element_type=jnp.float32)


def name_edges(range_blocks, owner_ref, local_ref, named_ref, bias_ref):
    randoms, blocks = owner_ref.shape

    def name_step(block_id, carry):
        earlier = []
        for nth in range(randoms):
            named = owner_ref[nth, block_id] * range_blocks + local_ref[nth, block_id]
            fresh = (named >= GLOBALS) & ((named < block_id - 1) | (named > block_id + 1))
            for before in earlier:
                fresh = fresh & (named != before)
            earlier.append(named)
            edge = block_id * randoms + nth
            named_ref[edge] = named
            bias_ref[edge] = jnp.where(fresh, 0.0, -NEG_BIG).astype(jnp.float32)
        return carry

    lax.fori_loop(0, blocks, name_step, 0)


def link_edges(range_blocks, owner, local, width):
    randoms, blocks = owner.shape
    named = owner * range_blocks + local
    row_id = lax.broadcasted_iota(jnp.int32, (blocks, blocks), 0)
    column_id = lax.broadcasted_iota(jnp.int32, (blocks, blocks), 1)
    across = [jnp.broadcast_to(named[nth : nth + 1], (blocks, blocks)) for nth in range(randoms)]

    def latest(wanted, before):
        found = jnp.full((blocks, blocks), -1, jnp.int32)
        for nth in range(randoms):
            hit = (across[nth] == wanted) & (column_id >= GLOBALS) & (column_id < before)
            found = jnp.maximum(found, jnp.where(hit, column_id * randoms + nth, -1))
        return jnp.max(found, axis=1, keepdims=True)

    columns = []
    for nth in range(randoms):
        down = jnp.sum(jnp.where(row_id == column_id, across[nth], 0), axis=1, keepdims=True)
        columns.append(latest(down, row_id))
    columns.append(latest(row_id, blocks))
    slot = lax.broadcasted_iota(jnp.int32, (blocks, width), 1)
    table = jnp.full((blocks, width), -1, jnp.int32)
    for nth, column in enumerate(columns):
        table = jnp.where(slot == nth, column, table)
    return table


def head_kernel(ctx_size, heads_axis, owner_in, local_in, k_in, v_in, q_in, g_in,
                dq_out, dk_out, dv_out, owner_ref, local_ref, owner_rows, local_rows,
                named_ref, bias_ref, links_ref, table_ref, kv_ref, qg_ref, grads_ref, acc_ref, edge_ref, kt_ref, pair_ref, s_ref, dp_ref,
                send_sem, recv_sem, own_sem, table_sem, index_sem):
    blocks, randoms = kv_ref.shape[0], edge_ref.shape[0] // kv_ref.shape[0]
    devices = ctx_size * heads_axis
    score_scale = 1.0 / math.sqrt(HEAD_DIM)
    exp_scale = score_scale * math.log2(math.e)
    glob_rows = GLOBALS * BLOCK_LEN
    group = 4
    chunk = group * BLOCK_LEN
    chunks = blocks // group
    bf16 = jnp.bfloat16
    ctx_id, head_id = lax.axis_index("ctx"), lax.axis_index("head")
    me = ctx_id * heads_axis + head_id
    ins = (k_in, v_in, q_in, g_in)
    landing = (kv_ref, kv_ref, qg_ref, qg_ref)
    outs = (dq_out, dk_out, dv_out)

    def head_columns(block_id):
        return pl.ds(pl.multiple_of(block_id * HEAD_DIM, HEAD_DIM), HEAD_DIM)

    inner = (ctx_id > 0) & (ctx_id < ctx_size - 1)
    near = (1, 0)
    far = (jnp.where(inner, 3, 2), jnp.where(inner, 2, 3))

    def peer_at(ctx_off, head_off):
        return ctx_id ^ ctx_off, head_id ^ head_off, ctx_off * heads_axis + head_off

    def ends(which, peer):
        if which < 4:
            half = (which % 2) * HEAD_DIM
            return (
                ins[which].at[:, head_columns(peer)],
                landing[which].at[me, :, half : half + HEAD_DIM],
            )
        return (
            grads_ref.at[which - 4, peer],
            outs[which - 4].at[:, head_columns(me)],
        )

    def remote(which, peer_ctx, peer_head, offset):
        src, dst = ends(which, peer_ctx * heads_axis + peer_head)
        return pltpu.make_async_remote_copy(
            src_ref=src,
            dst_ref=dst,
            send_sem=send_sem.at[which, offset],
            recv_sem=recv_sem.at[which, offset],
            device_id=(peer_ctx, peer_head),
            device_id_type=MESH,
        )

    def own(which):
        src, dst = ends(which, me)
        return pltpu.make_async_copy(src, dst, own_sem.at[which])

    def over_peers(ctx_offs, action, first=0, until=heads_axis):
        def one(turn, carry):
            head_off = turn ^ (ctx_id % 2)
            for ctx_off in ctx_offs:
                if isinstance(ctx_off, int) and ctx_off == 0:

                    @pl.when(head_off > 0)
                    def _():
                        action(*peer_at(ctx_off, head_off))

                else:
                    action(*peer_at(ctx_off, head_off))
            return carry

        lax.fori_loop(first, until, one, 0)

    def start_all(ctx_offs, *names):
        def action(*peer):
            for which in names:
                remote(which, *peer).start()

        over_peers(ctx_offs, action)

    barrier = pltpu.get_barrier_semaphore()

    def greet(peer_ctx, peer_head, offset):
        pl.semaphore_signal(barrier, inc=1, device_id=(peer_ctx, peer_head), device_id_type=MESH)

    over_peers(far + near, greet)
    pl.semaphore_wait(barrier, devices - 1)
    start_all(far + near, 0)
    start_all(far + near, 1)
    start_all(far + near, 2, 3)

    for which in range(4):
        own(which).start()
    index_copies = [
        pltpu.make_async_copy(src, dst, index_sem.at[nth])
        for nth, (src, dst) in enumerate(
            zip((owner_in, local_in) * 2, (owner_ref, local_ref, owner_rows, local_rows))
        )
    ]
    for copy in index_copies:
        copy.start()
    for copy in index_copies:
        copy.wait()
    table_ref[...] = link_edges(
        blocks // ctx_size, owner_rows[...], local_rows[...], table_ref.shape[1]
    )
    table_copy = pltpu.make_async_copy(table_ref, links_ref, table_sem)
    table_copy.start()
    name_edges(blocks // ctx_size, owner_ref, local_ref, named_ref, bias_ref)
    pair_ref[...] = jnp.zeros_like(pair_ref)
    acc_ref[...] = jnp.zeros_like(acc_ref)
    edge_ref[: GLOBALS * randoms] = jnp.zeros(
        (GLOBALS * randoms, BLOCK_LEN, 2 * HEAD_DIM), jnp.float32
    )
    for which in range(4):
        own(which).wait()
    table_copy.wait()

    def keys_arrived(*peer):
        remote(0, *peer).wait_recv()
        remote(1, *peer).wait_recv()

    over_peers(far + near, keys_arrived)

    def turn_step(block_id, carry):
        kt_ref[block_id] = kv_ref[block_id, :, :HEAD_DIM].T
        return carry

    lax.fori_loop(0, blocks, turn_step, 0, unroll=4)

    def attend(block_id):
        pair_ref[:BLOCK_LEN, :HEAD_DIM] = qg_ref[block_id, :, :HEAD_DIM]
        pair_ref[BLOCK_LEN:, HEAD_DIM:] = qg_ref[block_id, :, HEAD_DIM:]
        pair = pair_ref[...]
        ids = [block_id - 1, block_id, jnp.minimum(block_id + 1, blocks - 1)]
        bias = [
            jnp.where(block_id - 1 >= GLOBALS, 0.0, -NEG_BIG).astype(jnp.float32),
            0.0,
            jnp.where(block_id + 1 < blocks, 0.0, -NEG_BIG).astype(jnp.float32),
        ]
        ids += list(range(GLOBALS))
        bias += [0.0] * GLOBALS
        fixed = len(ids)
        for nth in range(randoms):
            ids.append(named_ref[block_id * randoms + nth])
            bias.append(bias_ref[block_id * randoms + nth])
        both = [dot_nt(kv_ref[key_id], pair) for key_id in ids]
        row_top = None
        for part, off in zip(both, bias):
            part_top = jnp.max(part[:, :BLOCK_LEN], axis=0, keepdims=True) - off
            row_top = part_top if row_top is None else jnp.maximum(row_top, part_top)
        top_scaled = row_top * exp_scale
        probs, row_total, row_dot = [], 0.0, 0.0
        for part, off in zip(both, bias):
            vals = jnp.exp2(part[:, :BLOCK_LEN] * exp_scale - (top_scaled + off))
            row_total += jnp.sum(vals, axis=0, keepdims=True)
            row_dot += jnp.sum(vals * part[:, BLOCK_LEN:], axis=0, keepdims=True)
            probs.append(vals)
        inverse = 1.0 / row_total
        row_delta = row_dot * inverse
        dq_acc = jnp.zeros((HEAD_DIM, BLOCK_LEN), jnp.float32)
        for nth, (part, vals, key_id) in enumerate(zip(both, probs, ids)):
            vals = vals * inverse
            ds_bf = (vals * (part[:, BLOCK_LEN:] - row_delta)).astype(bf16)
            left = jnp.concatenate([ds_bf, vals.astype(bf16)], axis=1)
            if nth < fixed:
                acc_ref[key_id] += dot_nn(left, pair)
            else:
                edge_ref[block_id * randoms + nth - fixed] = dot_nn(left, pair)
            if nth % 2 == 0:
                waiting, waiting_id = ds_bf, key_id
            else:
                dq_acc += dot_nn(
                    jnp.concatenate([kt_ref[waiting_id], kt_ref[key_id]], axis=1),
                    jnp.concatenate([waiting, ds_bf], axis=0),
                )
        if len(ids) % 2:
            dq_acc += dot_nn(kt_ref[waiting_id], waiting)
        grads_ref[0, block_id] = (dq_acc.T * score_scale).astype(bf16)

    def send_queries_grad(*peer):
        @pl.when(peer[0] * heads_axis + peer[1] >= GLOBALS)
        def _():
            remote(4, *peer).start()

    def handle(send, remote_block, *peer):
        block_id = peer[0] * heads_axis + peer[1]

        @pl.when(remote_block)
        def _():
            remote(2, *peer).wait_recv()
            remote(3, *peer).wait_recv()

        @pl.when(block_id >= GLOBALS)
        def _():
            attend(block_id)

            @pl.when(send & remote_block)
            def _():
                remote(4, *peer).start()

    def block_step(step, carry):
        group_id, head_off = step // heads_axis, step % heads_axis
        far_off = jnp.where(group_id == 2, far[0], far[1])
        ctx_off = jnp.where(group_id < 2, group_id, far_off)
        handle(group_id >= 0, step > 0, *peer_at(ctx_off, head_off))
        return carry

    lax.fori_loop(0, devices, block_step, 0)


    q_glob = qg_ref[:GLOBALS, :, :HEAD_DIM].reshape(glob_rows, HEAD_DIM)
    g_glob = qg_ref[:GLOBALS, :, HEAD_DIM:].reshape(glob_rows, HEAD_DIM)

    def keys_of(step, half):
        part = kv_ref[pl.ds(step * group, group), :, half * HEAD_DIM : (half + 1) * HEAD_DIM]
        return part.reshape(chunk, HEAD_DIM)

    def scores_step(step, row_top):
        rows = pl.ds(pl.multiple_of(step * chunk, chunk), chunk)
        scores = dot_nt(keys_of(step, 0), q_glob)
        s_ref[rows, :] = scores
        return jnp.maximum(row_top, jnp.max(scores, axis=0, keepdims=True))

    row_top = lax.fori_loop(
        0, chunks, scores_step, jnp.full((1, glob_rows), NEG_BIG, jnp.float32)
    )
    top_scaled = row_top * exp_scale

    def probs_step(step, sums):
        rows = pl.ds(pl.multiple_of(step * chunk, chunk), chunk)
        probs = jnp.exp2(s_ref[rows, :] * exp_scale - top_scaled)
        dprobs = dot_nt(keys_of(step, 1), g_glob)
        s_ref[rows, :] = probs
        dp_ref[rows, :] = dprobs
        return (
            sums[0] + jnp.sum(probs, axis=0, keepdims=True),
            sums[1] + jnp.sum(probs * dprobs, axis=0, keepdims=True),
        )

    zero_row = jnp.zeros((1, glob_rows), jnp.float32)
    row_total, row_dot = lax.fori_loop(0, chunks, probs_step, (zero_row, zero_row))
    inverse = 1.0 / row_total
    row_delta = row_dot * inverse

    def grads_step(step, dq_acc):
        rows = pl.ds(pl.multiple_of(step * chunk, chunk), chunk)
        probs = s_ref[rows, :] * inverse
        ds_bf = (probs * (dp_ref[rows, :] - row_delta)).astype(bf16)
        probs_bf = probs.astype(bf16)
        at = pl.ds(step * group, group)
        shape = (group, BLOCK_LEN, HEAD_DIM)
        acc_ref[at, :, :HEAD_DIM] += dot_nn(ds_bf, q_glob).reshape(shape)
        acc_ref[at, :, HEAD_DIM:] += dot_nn(probs_bf, g_glob).reshape(shape)
        for nth in range(group):
            dq_acc += dot_nn(
                kt_ref[step * group + nth], ds_bf[nth * BLOCK_LEN : (nth + 1) * BLOCK_LEN]
            )
        return dq_acc

    dq_glob = lax.fori_loop(
        0, chunks, grads_step, jnp.zeros((HEAD_DIM, glob_rows), jnp.float32)
    )
    dq_rows = (dq_glob.T * score_scale).astype(bf16)
    for block_id in range(GLOBALS):
        grads_ref[0, block_id] = dq_rows[block_id * BLOCK_LEN : (block_id + 1) * BLOCK_LEN]

        @pl.when(me != block_id)
        def _():
            remote(4, 0, block_id, ctx_id * heads_axis + (head_id ^ block_id)).start()

    own(4).start()

    def linked(block_id, slot):
        edge = links_ref[block_id, slot]
        weight = jnp.where(edge >= 0, 1.0, 0.0).astype(jnp.float32)
        return weight * edge_ref[jnp.maximum(edge, 0)]

    def chain_step(block_id, carry):
        for nth in range(randoms):
            edge_ref[block_id * randoms + nth] += linked(block_id, nth)
        return carry

    lax.fori_loop(GLOBALS, blocks, chain_step, 0)

    def finish(*peer):
        block_id = peer[0] * heads_axis + peer[1]
        total = acc_ref[block_id] + linked(block_id, randoms)
        grads_ref[1, block_id] = (total[:, :HEAD_DIM] * score_scale).astype(bf16)
        grads_ref[2, block_id] = total[:, HEAD_DIM:].astype(bf16)

    def finish_step(step, carry):
        head_off, turn = step % heads_axis, step // heads_axis
        ctx_off = jnp.where(turn == 0, 2, jnp.where(turn == 1, 3, ctx_size - 1 - turn))
        peer = peer_at(ctx_off, head_off ^ (ctx_id % 2))
        finish(*peer)

        @pl.when(peer[2] > 0)
        def _():
            remote(5, *peer).start()
            remote(6, *peer).start()

        return carry

    lax.fori_loop(0, devices, finish_step, 0)
    own(5).start()
    own(6).start()
    for which in range(4, 7):
        own(which).wait()

    def all_sent(*peer):
        for which in range(7):
            remote(which, *peer).wait_send()

    def all_here(*peer):
        for which in range(4, 7):
            remote(which, *peer).wait_recv()

    over_peers(far + near, all_sent)
    over_peers(near + far, all_here)


def copy_kernel(count, *refs):
    ins, outs, sems = refs[:count], refs[count : 2 * count], refs[2 * count]
    copies = [pltpu.make_async_copy(ins[nth], outs[nth], sems.at[nth]) for nth in range(count)]
    for copy in copies:
        copy.start()
    for copy in copies:
        copy.wait()


def one_head(queries, keys_in, values_in, out_grad, rand_owner, rand_local):
    ctx_size, heads_axis = lax.axis_size("ctx"), lax.axis_size("head")
    devices = ctx_size * heads_axis
    rows, feat_width = queries.shape
    tokens = rows * devices
    blocks, randoms = rand_owner.shape
    edges = blocks * randoms
    anywhere = pl.BlockSpec(memory_space=pl.ANY)
    vmem = pl.BlockSpec(memory_space=pltpu.VMEM)
    hbm = pl.BlockSpec(memory_space=pltpu.HBM)
    bf16 = jnp.bfloat16
    index_arrays = [pltpu.with_memory_space_constraint(index.T, pltpu.HBM) for index in (rand_owner, rand_local)]
    grads = pl.pallas_call(
        functools.partial(head_kernel, ctx_size, heads_axis),
        out_shape=[jax.ShapeDtypeStruct((rows, feat_width), bf16)] * 3,
        in_specs=[hbm] * 6,
        out_specs=[vmem] * 3,
        scratch_shapes=[
            pltpu.SMEM((randoms, blocks), jnp.int32),
            pltpu.SMEM((randoms, blocks), jnp.int32),
            pltpu.VMEM((randoms, blocks), jnp.int32),
            pltpu.VMEM((randoms, blocks), jnp.int32),
            pltpu.SMEM((edges,), jnp.int32),
            pltpu.SMEM((edges,), jnp.float32),
            pltpu.SMEM((blocks, 128), jnp.int32),
            pltpu.VMEM((blocks, 128), jnp.int32),
            pltpu.VMEM((blocks, BLOCK_LEN, 2 * HEAD_DIM), bf16),
            pltpu.VMEM((blocks, BLOCK_LEN, 2 * HEAD_DIM), bf16),
            pltpu.VMEM((3, blocks, BLOCK_LEN, HEAD_DIM), bf16),
            pltpu.VMEM((blocks, BLOCK_LEN, 2 * HEAD_DIM), jnp.float32),
            pltpu.VMEM((edges, BLOCK_LEN, 2 * HEAD_DIM), jnp.float32),
            pltpu.VMEM((blocks, HEAD_DIM, BLOCK_LEN), bf16),
            pltpu.VMEM((2 * BLOCK_LEN, 2 * HEAD_DIM), bf16),
            pltpu.VMEM((tokens, GLOBALS * BLOCK_LEN), jnp.float32),
            pltpu.VMEM((tokens, GLOBALS * BLOCK_LEN), jnp.float32),
            pltpu.SemaphoreType.DMA((7, devices)),
            pltpu.SemaphoreType.DMA((7, devices)),
            pltpu.SemaphoreType.DMA((7,)),
            pltpu.SemaphoreType.DMA,
            pltpu.SemaphoreType.DMA((4,)),
        ],
        compiler_params=pltpu.CompilerParams(
            collective_id=1, has_side_effects=True, vmem_limit_bytes=50 << 20
        ),
    )(*index_arrays, keys_in, values_in, queries, out_grad)
    return tuple(
        pl.pallas_call(
            functools.partial(copy_kernel, 3),
            out_shape=[jax.ShapeDtypeStruct((rows, feat_width), bf16)] * 3,
            in_specs=[vmem] * 3,
            out_specs=[anywhere] * 3,
            scratch_shapes=[pltpu.SemaphoreType.DMA((3,))],
            compiler_params=pltpu.CompilerParams(vmem_limit_bytes=4 << 20),
        )(*grads)
    )


def per_device(*args):
    devices = lax.axis_size(("ctx", "head"))
    rows, feat_width = args[0].shape
    fits = feat_width == devices * HEAD_DIM and rows == BLOCK_LEN and lax.axis_size("ctx") == 4
    return one_head(*args) if fits else split_heads(*args)


def solution(mesh):
    return jax.shard_map(
        per_device,
        mesh=mesh,
        in_specs=(
            P(("ctx", "head"), None),
            P(("ctx", "head"), None),
            P(("ctx", "head"), None),
            P(("ctx", "head"), None),
            P(),
            P(),
        ),
        out_specs=(P(("ctx", "head"), None), P(("ctx", "head"), None), P(("ctx", "head"), None)),
        check_vma=False,
    )
```
